32 devices in a mesh: groups: 2 (over x), gx: 16 (over z, y, core).
Axes of the slice: x: 2, y: 2, z: 4, core: 2. Of those that a mesh axis runs over, the one named last changes fastest.
Arguments:
- right_side: float32 [3, 2048, 512], P(None, ('groups', 'gx')), parts along dimension 1, may hold values from -135 to 135
- masses: float32 [2048, 512], P(('groups', 'gx')), parts along dimension 0, may hold values from 0.5 to 2
- stiffness: float32 [2, 2048, 512], P(None, ('groups', 'gx')), parts along dimension 1, may hold values from 0.3 to 3
- hessian: bfloat16 [1152, 384, 384], P(('groups', 'gx')), parts along dimension 0, may hold values from -1 to 4, as said below
- send_list: int32 [32, 48], P(('groups', 'gx')), parts along dimension 0, may hold values from 0 to 255, as said below
- pair_refs: int32 [1152, 2], P(('groups', 'gx')), parts along dimension 0, may hold values from 0 to 47, as said below
- counts: int32 [32], P(('groups', 'gx')), parts along dimension 0, may hold values from 18 to 36, as said below
Outputs:
- solution: float32 [3, 2048, 512], P(None, ('groups', 'gx')), parts along dimension 1
- residual: float32 [3, 2048, 512], P(None, ('groups', 'gx')), parts along dimension 1
The draws below stay inside these ranges and needn't reach their ends.
There are 2 independent parts, one for each index of `groups`. The reference program is written for one: setup_inputs(seed, part) draws one part's arguments, and reference() takes and returns one part's arrays. A program takes and returns all parts, laid end to end along the dimension named above; each array names one. Nothing has to cross between parts.
Inputs may be any that keep to these rules, and one draw needn't show every extreme that they name: `hessian`: every block is symmetric. `send_list`: row d names 48 different blocks of device d. `pair_refs`: the two positions of a row differ. `counts`: some device holds 36 live slots.
All inputs are finite; a program needn't handle non-finite values.
Results may differ from the reference program's by a relative error of at most 0.018.
Values may be sent and summed in bfloat16 or wider, within the bound.
No kernel may reach another device: no remote copies, remote signals or barrier semaphores. Data moves between devices by JAX's collectives and lax.ppermute only.
A program may use at most 64 MiB of HBM per device.

```python
import math
import jax
import jax.numpy as jnp
from jax import lax

BLOCK = 128
HMAX = 36
CAP = 3
ITERS = 3
NY = 512
HDIM = 384
NX = 1024
BLK_DEV = 256
N_GX = 16


def draw_right_side(key, part):
    key = jax.random.fold_in(key, 11)
    key_base, key_rows, key_cols = jax.random.split(key, 3)
    row_ids = jnp.arange(NX, dtype=jnp.float32)
    row_scale = jnp.exp(math.log(3.0) * row_ids / NX + jax.random.uniform(key_rows, (NX,), jnp.float32, 0.0, math.log(3.0)))
    col_scale = jnp.exp(jax.random.uniform(key_cols, (NY,), jnp.float32, math.log(0.3), math.log(3.0)))
    base_vals = jnp.clip(jax.random.normal(key_base, (3, NX, NY), jnp.float32), -5.0, 5.0)
    return base_vals * row_scale[None, :, None] * col_scale[None, None, :]


def draw_hessian(key, part):
    key = jax.random.fold_in(key, 23)
    key_off, key_diag = jax.random.split(key)
    bound_off = 1.8 / math.sqrt(HDIM)
    raw_vals = jax.random.uniform(key_off, (N_GX * HMAX, HDIM, HDIM), jnp.float32, -bound_off, bound_off)
    symmetric = 0.5 * (raw_vals + jnp.swapaxes(raw_vals, 1, 2))
    eye_mask = jnp.eye(HDIM, dtype=jnp.float32)
    diag_vals = jax.random.uniform(key_diag, (N_GX * HMAX, HDIM), jnp.float32, 2.0, 4.0)
    return (symmetric * (1.0 - eye_mask) + diag_vals[:, :, None] * eye_mask).astype(jnp.bfloat16)


def draw_send_list(key, part):
    key = jax.random.fold_in(key, 37)
    row_keys = jax.random.split(key, N_GX)
    chosen = jax.vmap(lambda one_key: jax.random.permutation(one_key, BLK_DEV))(row_keys)
    return chosen[:, :N_GX * CAP].astype(jnp.int32)


def draw_pair_refs(key, part):
    key = jax.random.fold_in(key, 41)
    key_first, key_gap = jax.random.split(key)
    sends_all = N_GX * CAP
    first_ref = jax.random.randint(key_first, (N_GX * HMAX,), 0, sends_all, dtype=jnp.int32)
    gap_vals = jax.random.randint(key_gap, (N_GX * HMAX,), 1, sends_all, dtype=jnp.int32)
    return jnp.stack([first_ref, (first_ref + gap_vals) % sends_all], axis=1)


def draw_counts(key, part):
    key = jax.random.fold_in(key, 53)
    key_vals, key_top = jax.random.split(key)
    base_counts = jax.random.randint(key_vals, (N_GX,), HMAX // 2, HMAX, dtype=jnp.int32)
    busiest = jax.random.randint(key_top, (), 0, N_GX, dtype=jnp.int32)
    return jnp.where(jnp.arange(N_GX, dtype=jnp.int32) == busiest, HMAX, base_counts).astype(jnp.int32)


def block_scale(stream_key, shape, pieces, smallest, largest):
    factor_of, own = 1.0, jax.random.fold_in(stream_key, 6)
    for axis_at, shards_of in pieces:
        draws = jnp.exp(jax.random.uniform(jax.random.fold_in(own, axis_at), (shards_of,), jnp.float32, smallest / len(pieces), largest / len(pieces)))
        factor_of = factor_of * jnp.repeat(draws, shape[axis_at] // shards_of).reshape([-1 if axis == axis_at else 1 for axis in range(len(shape))])
    return factor_of


def setup_inputs(seed: int = 0, part: int = 0) -> dict:
    streams_of = jax.random.split(jax.random.key(seed), 8)
    part_splits = jax.random.split(jax.random.fold_in(streams_of[7], part), 8)
    return {
        "right_side": draw_right_side(jax.random.fold_in(jax.random.fold_in(streams_of[7], part), 71), part),
        "masses": jnp.clip(jnp.exp(math.log(2.0) - 1.3862944 * jax.random.uniform(part_splits[1], (NX, NY), jnp.float32) ** block_scale(part_splits[1], (NX, NY), ((0, 16),), -0.2, 0.2)), 0.5, 2.0),
        "stiffness": jnp.clip(jnp.exp(math.log(3.0) - 2.3025851 * jax.random.uniform(part_splits[2], (2, NX, NY), jnp.float32) ** block_scale(part_splits[2], (2, NX, NY), ((1, 16),), -0.2, 0.2)), 0.3, 3.0),
        "hessian": draw_hessian(jax.random.fold_in(jax.random.fold_in(streams_of[7], part), 71), part),
        "send_list": draw_send_list(jax.random.fold_in(jax.random.fold_in(streams_of[7], part), 71), part),
        "pair_refs": draw_pair_refs(jax.random.fold_in(jax.random.fold_in(streams_of[7], part), 71), part),
        "counts": draw_counts(jax.random.fold_in(jax.random.fold_in(streams_of[7], part), 71), part),
    }


HIGH = lax.Precision.HIGHEST


def to_blocks(grid_vals, block_len):
    comp_count, row_count, col_count = grid_vals.shape
    shaped = grid_vals.reshape(comp_count, row_count, col_count // block_len, block_len)
    return shaped.transpose(1, 2, 0, 3).reshape(row_count * (col_count // block_len), comp_count * block_len)


def from_blocks(blocks, row_count, col_count, block_len):
    shaped = blocks.reshape(row_count, col_count // block_len, 3, block_len)
    return shaped.transpose(2, 0, 1, 3).reshape(3, row_count, col_count)


def membrane(padded, kx_here, kx_prev, ky_here, ky_prev):
    centre = padded[:, 1:-1, :]
    next_row = padded[:, 2:, :]
    prev_row = padded[:, :-2, :]
    zero_col = jnp.zeros_like(centre[:, :, :1])
    next_col = jnp.concatenate([centre[:, :, 1:], zero_col], axis=2)
    prev_col = jnp.concatenate([zero_col, centre[:, :, :-1]], axis=2)
    return (kx_here * (centre - next_row) + kx_prev * (centre - prev_row)
            + ky_here * (centre - next_col) + ky_prev * (centre - prev_col))


def reference(right_side, masses, stiffness, hessian, send_list, pair_refs, counts):
    row_ids = jnp.arange(NX, dtype=jnp.int32)
    col_ids = jnp.arange(NY, dtype=jnp.int32)
    kx_here = jnp.where((row_ids < NX - 1)[:, None], stiffness[0], 0.0)
    ky_here = jnp.where((col_ids < NY - 1)[None, :], stiffness[1], 0.0)
    kx_prev = jnp.concatenate([jnp.zeros_like(kx_here[:1]), kx_here[:-1]], axis=0)
    ky_prev = jnp.concatenate([jnp.zeros_like(ky_here[:, :1]), ky_here[:, :-1]], axis=1)
    send_table = send_list.reshape(N_GX, N_GX, CAP) + (jnp.arange(N_GX, dtype=jnp.int32) * BLK_DEV)[:, None, None]
    glob_idx = jnp.transpose(send_table, (1, 0, 2)).reshape(N_GX, N_GX * CAP).astype(jnp.int32)
    ref_table = pair_refs.reshape(N_GX, HMAX, 2).astype(jnp.int32)
    glob_a = jnp.take_along_axis(glob_idx, ref_table[:, :, 0], axis=1)
    glob_b = jnp.take_along_axis(glob_idx, ref_table[:, :, 1], axis=1)
    live_mask = (jnp.arange(HMAX, dtype=jnp.int32)[None, :] < counts[:, None]).astype(jnp.float32)
    hess_owner = hessian.reshape(N_GX, HMAX, HDIM, HDIM)

    def contact(vector):
        blocks = to_blocks(vector, BLOCK).astype(jnp.bfloat16)

        def per_owner(owner_items):
            hess_one, idx_a, idx_b = owner_items
            stacked = jnp.stack([blocks[idx_a], blocks[idx_b]], axis=1).astype(jnp.float32)
            products = jnp.einsum("hij,hkj->hki", hess_one.astype(jnp.float32), stacked, precision=HIGH)
            return products[:, 0] - products[:, 1]

        pushes = lax.map(per_owner, (hess_owner, glob_a, glob_b)) * live_mask[:, :, None]
        flat_push = pushes.reshape(N_GX * HMAX, HDIM)
        summed = jnp.zeros((NX * NY // BLOCK, HDIM), jnp.float32)
        summed = summed.at[glob_a.reshape(-1)].add(flat_push).at[glob_b.reshape(-1)].add(-flat_push)
        return from_blocks(summed, NX, NY, BLOCK)

    def operate(vector):
        padded = jnp.pad(vector, ((0, 0), (1, 1), (0, 0)))
        return masses[None] * vector + membrane(padded, kx_here, kx_prev, ky_here, ky_prev) + contact(vector)

    solution = jnp.zeros_like(right_side)
    residual = right_side
    direction = right_side
    norm_now = jnp.sum(residual * residual)
    for step_index in range(ITERS):
        image_vec = operate(direction)
        step_len = norm_now / jnp.sum(direction * image_vec)
        solution = solution + step_len * direction
        residual = residual - step_len * image_vec
        norm_next = jnp.sum(residual * residual)
        direction = residual + (norm_next / norm_now) * direction
        norm_now = norm_next
    return solution, residual
```

```python
import jax
import jax.numpy as jnp
from jax import lax
from jax.sharding import PartitionSpec as P

HIGH = lax.Precision.HIGHEST


def to_blocks(grid_vals, block_len):
    comp_count, row_count, col_count = grid_vals.shape
    shaped = grid_vals.reshape(comp_count, row_count, col_count // block_len, block_len)
    return shaped.transpose(1, 2, 0, 3).reshape(
        row_count * (col_count // block_len), comp_count * block_len
    )


def from_blocks(blocks, row_count, col_count, block_len):
    shaped = blocks.reshape(row_count, col_count // block_len, 3, block_len)
    return shaped.transpose(2, 0, 1, 3).reshape(3, row_count, col_count)


def local_apply(padded, mass, kx_here, kx_prev, ky_here):
    centre = padded[:, 1:-1, :]
    next_row = padded[:, 2:, :]
    prev_row = padded[:, :-2, :]
    zero_col = jnp.zeros_like(centre[:, :, :1])
    next_col = jnp.concatenate([centre[:, :, 1:], zero_col], axis=2)
    prev_col = jnp.concatenate([zero_col, centre[:, :, :-1]], axis=2)
    ky_prev = jnp.concatenate([jnp.zeros_like(ky_here[:, :1]), ky_here[:, :-1]], axis=1)
    return (
        mass * centre
        + kx_here * (centre - next_row)
        + kx_prev * (centre - prev_row)
        + ky_here * (centre - next_col)
        + ky_prev * (centre - prev_col)
    )


def per_device(right_side, masses, stiffness, hessian, send_list, pair_refs, counts):
    comp_count, row_count, col_count = right_side.shape
    width = hessian.shape[1]
    block_len = width // 3
    slot_count = hessian.shape[0]
    peers = lax.axis_size("gx")
    me = lax.axis_index("gx")
    order = send_list[0]
    cap = order.shape[0] // peers
    f32 = jnp.float32

    up = [(i, i + 1) for i in range(peers - 1)]
    down = [(i + 1, i) for i in range(peers - 1)]

    global_row = me * row_count + jnp.arange(row_count, dtype=jnp.int32)
    kx = jnp.where((global_row < row_count * peers - 1)[:, None], stiffness[0], 0.0)
    col_ids = jnp.arange(col_count, dtype=jnp.int32)
    ky = jnp.where((col_ids < col_count - 1)[None, :], stiffness[1], 0.0)

    low = lax.ppermute(
        jnp.concatenate([right_side[:, -1], kx[-2:], ky[-1:], masses[-1:]], axis=0), "gx", up
    )
    high = lax.ppermute(
        jnp.concatenate([right_side[:, 0], kx[:1], ky[:1], masses[:1]], axis=0), "gx", down
    )
    b_ext = jnp.concatenate([low[:3, None], right_side, high[:3, None]], axis=1)
    kxh_ext = jnp.concatenate([low[4:5], kx, high[3:4]], axis=0)
    kxp_ext = jnp.concatenate([low[3:5], kx], axis=0)
    ky_ext = jnp.concatenate([low[5:6], ky, high[4:5]], axis=0)
    m_ext = jnp.concatenate([low[6:7], masses, high[5:6]], axis=0)

    def own_apply(ext):
        return local_apply(ext, masses, kx, kxp_ext[1:-1], ky)

    live = (jnp.arange(slot_count, dtype=jnp.int32) < counts[0]).astype(f32)
    slots_all = jnp.arange(peers * cap, dtype=jnp.int32)
    signs = (
        (pair_refs[:, 0:1] == slots_all[None, :]).astype(f32)
        - (pair_refs[:, 1:2] == slots_all[None, :]).astype(f32)
    ) * live[:, None]

    def contact(held):
        delta = held[pair_refs[:, 0]] - held[pair_refs[:, 1]]
        coarse = delta.astype(jnp.bfloat16)
        fine = (delta - coarse.astype(f32)).astype(jnp.bfloat16)
        both = jnp.stack([coarse, fine], axis=1)
        products = jnp.einsum("hij,hkj->hki", hessian, both, preferred_element_type=f32)
        return jnp.einsum(
            "hp,hi->pi", signs, products[:, 0] + products[:, 1], precision=HIGH
        )

    def exchange(fields, scalars):
        rows = jnp.stack(fields, axis=1).reshape(peers, cap * len(fields), width)
        line = jnp.zeros((width,), f32).at[: len(scalars)].set(jnp.stack(scalars))
        line = jnp.broadcast_to(line, (peers, 1, width))
        got = lax.all_to_all(
            jnp.concatenate([rows, line], axis=1), "gx", split_axis=0, concat_axis=0, tiled=True
        )
        blocks = got[:, :-1].reshape(peers * cap, len(fields), width)
        sums = jnp.sum(got[:, -1, : len(scalars)], axis=0)
        return [blocks[:, k] for k in range(len(fields))], [sums[k] for k in range(len(scalars))]

    def gathered(field):
        return to_blocks(field, block_len)[order]

    def spread(blocks):
        dense = jnp.zeros((row_count * col_count // block_len, width), f32).at[order].set(blocks)
        return from_blocks(dense, row_count, col_count, block_len)

    db = own_apply(b_ext)
    (b_o, db_o), (rr0, dad0) = exchange(
        [gathered(right_side), gathered(db)],
        [jnp.sum(right_side * right_side), jnp.sum(right_side * db)],
    )
    cb_o = contact(b_o)
    v1_o = db_o + cb_o
    cv1_o = contact(v1_o)
    (cb, cv1), (bcb,) = exchange([cb_o, cv1_o], [jnp.sum(b_o * cb_o)])
    alpha0 = rr0 / (dad0 + bcb)
    v1 = db + spread(cb)
    cv1 = spread(cv1)

    low1 = lax.ppermute(
        jnp.concatenate([v1[:, -2:], cv1[:, -1:]], axis=1), "gx", up
    )
    high1 = lax.ppermute(
        jnp.concatenate([v1[:, :2], cv1[:, :1]], axis=1), "gx", down
    )
    v1_wide = jnp.concatenate([low1[:, :2], v1, high1[:, :2]], axis=1)
    v1_ext = v1_wide[:, 1:-1]
    cv1_ext = jnp.concatenate([low1[:, 2:], cv1, high1[:, 2:]], axis=1)
    dv1_ext = local_apply(v1_wide, m_ext, kxh_ext, kxp_ext, ky_ext)
    v2_ext = dv1_ext + cv1_ext
    r1_ext = b_ext - alpha0 * v1_ext
    w_ext = v1_ext - alpha0 * v2_ext
    r1, w = (r1_ext[:, 1:-1], w_ext[:, 1:-1])

    (dv1_o,), sums = exchange(
        [gathered(dv1_ext[:, 1:-1])],
        [
            jnp.sum(r1 * r1),
            jnp.sum(r1 * w),
            jnp.sum(r1 * v1),
            jnp.sum(right_side * w),
            jnp.sum(right_side * v1),
            jnp.sum(w * w),
            jnp.sum(w * v1),
            jnp.sum(v1 * v1),
        ],
    )
    rr1, r1w, r1v1, bw, bv1, ww, wv1, v1v1 = sums
    beta0 = rr1 / rr0
    dad1 = r1w + beta0 * (r1v1 + bw) + beta0 * beta0 * bv1
    alpha1 = rr1 / dad1
    r1_image = r1w + beta0 * r1v1
    image_sq = ww + 2.0 * beta0 * wv1 + beta0 * beta0 * v1v1
    beta1 = (rr1 - 2.0 * alpha1 * r1_image + alpha1 * alpha1 * image_sq) / rr1

    def advance(b, v1, v2):
        r1 = b - alpha0 * v1
        d1 = r1 + beta0 * b
        r2 = r1 - alpha1 * (v1 - alpha0 * v2 + beta0 * v1)
        return d1, r2, r2 + beta1 * d1

    _, _, d2_o = advance(b_o, v1_o, dv1_o + cv1_o)
    cd2_o = contact(d2_o)
    d1_ext, r2_ext, d2_ext = advance(b_ext, v1_ext, v2_ext)
    d1, r2, d2 = (d1_ext[:, 1:-1], r2_ext[:, 1:-1], d2_ext[:, 1:-1])
    dd2 = own_apply(d2_ext)
    (cd2,), (rr2, dad2) = exchange(
        [cd2_o], [jnp.sum(r2 * r2), jnp.sum(d2 * dd2) + jnp.sum(d2_o * cd2_o)]
    )
    alpha2 = rr2 / dad2
    solution = alpha0 * right_side + alpha1 * d1 + alpha2 * d2
    residual = r2 - alpha2 * (dd2 + spread(cd2))
    return (solution, residual)


def solution(mesh):
    placed = (
        P(None, ("groups", "gx"), None),
        P(("groups", "gx"), None),
        P(None, ("groups", "gx"), None),
        P(("groups", "gx"), None, None),
        P(("groups", "gx"), None),
        P(("groups", "gx"), None),
        P(("groups", "gx")),
    )
    return jax.shard_map(
        per_device,
        mesh=mesh,
        in_specs=placed,
        out_specs=(P(None, ("groups", "gx"), None), P(None, ("groups", "gx"), None)),
        check_vma=False,
    )
```

```python
import functools

import jax
import jax.numpy as jnp
from jax import lax
from jax.experimental import pallas as pl
from jax.experimental.pallas import tpu as pltpu
from jax.sharding import PartitionSpec as P

F32 = jnp.float32
VMEM_LIMIT = 40 * 1024 * 1024
CAP = 3
SUMS_TWO, SUMS_ONE = 2 * CAP, CAP


def iota(shape, dim):
    return lax.broadcasted_iota(jnp.int32, shape, dim)


def total(value):
    return jnp.sum(jnp.sum(value, axis=0, keepdims=True), axis=1, keepdims=True)


def line_of(scalars, width):
    lanes = iota((1, width), 1)
    line = jnp.zeros((1, width), F32)
    for k, value in enumerate(scalars):
        line = jnp.where(lanes == k, value, line)
    return line


def line_sum(message, row):
    peers = message.shape[0]
    parts = [message[d, row : row + 1, 0:128] for d in range(peers)]
    while len(parts) > 1:
        parts = [a + b for a, b in zip(parts[::2], parts[1::2])] + (
            parts[-1:] if len(parts) % 2 else []
        )
    return parts[0]


def pick(line, k):
    return line[:, k : k + 1]


def place_of(send, position, col_blocks):
    block = send[0, position]
    return lax.div(block, jnp.int32(col_blocks)), lax.rem(block, jnp.int32(col_blocks))


def gather_blocks(send, panels, message):
    peers = message.shape[0]
    _, col_blocks, _, block_len = panels[0].shape

    def one(d, carry):
        for c in range(CAP):
            row, col = place_of(send, d * CAP + c, col_blocks)
            for f, field in enumerate(panels):
                for e in range(3):
                    message[d, f * CAP + c : f * CAP + c + 1, e * block_len : (e + 1) * block_len] = (
                        field[e, col, pl.ds(row, 1), :]
                    )
        return carry

    lax.fori_loop(0, peers, one, 0, unroll=4)


def scatter_blocks(send, message, panels):
    peers = message.shape[0]
    _, col_blocks, _, block_len = panels[0].shape
    for field in panels:
        field[...] = jnp.zeros_like(field)

    def one(d, carry):
        for c in range(CAP):
            row, col = place_of(send, d * CAP + c, col_blocks)
            for f, field in enumerate(panels):
                for e in range(3):
                    field[e, col, pl.ds(row, 1), :] = message[
                        d, f * CAP + c : f * CAP + c + 1, e * block_len : (e + 1) * block_len
                    ]
        return carry

    lax.fori_loop(0, peers, one, 0, unroll=4)


def to_panels(panels, e, value):
    _, col_blocks, _, block_len = panels.shape
    for q in range(col_blocks):
        panels[e, q] = value[:, q * block_len : (q + 1) * block_len]


def from_panels(panels, e):
    return jnp.concatenate([panels[e, q] for q in range(panels.shape[1])], axis=1)


def put_line(message, row, line):
    for d in range(message.shape[0]):
        message[d, row : row + 1, :] = line


def inner_apply(v, mass, kx, ky):
    rows, cols = v.shape
    row_ids = iota((rows, cols), 0)
    flux_x = jnp.where(row_ids == rows - 1, 0.0, kx * (v - pltpu.roll(v, rows - 1, 0)))
    flux_y = ky * (v - pltpu.roll(v, cols - 1, 1))
    return mass * v + (flux_x - pltpu.roll(flux_x, 1, 0)) + (flux_y - pltpu.roll(flux_y, 1, 1))


def masked_ky(stiff):
    ky = stiff[1]
    return jnp.where(iota(ky.shape, 1) == ky.shape[1] - 1, 0.0, ky)


def edge_coefs(stiff, low, high):
    rows = stiff.shape[1]
    last = jnp.where(high[3:4, :] > 0.5, stiff[0, rows - 1 : rows, :], 0.0)
    return low[3:4, :], last


def start_kernel(send, b, mass, stiff, low, high, message, db, b_panels, db_panels):
    rows = b.shape[1]
    kx_low, kx_high = edge_coefs(stiff, low, high)
    ky = masked_ky(stiff)
    sq, dot = [], []
    for e in range(3):
        v = b[e]
        db[e] = inner_apply(v, mass[...], stiff[0], ky)
        first, last = b[e, 0:1, :], b[e, rows - 1 : rows, :]
        db[e, 0:1, :] = db[e, 0:1, :] + kx_low * (first - low[e : e + 1, :])
        db[e, rows - 1 : rows, :] = db[e, rows - 1 : rows, :] + kx_high * (last - high[e : e + 1, :])
        to_panels(b_panels, e, v)
        to_panels(db_panels, e, db[e])
        sq.append(v * v)
        dot.append(v * db[e])
    line = line_of([total(sq[0] + sq[1] + sq[2]), total(dot[0] + dot[1] + dot[2])], message.shape[2])
    gather_blocks(send, [b_panels, db_panels], message)
    put_line(message, SUMS_TWO, line)
    put_line(message, SUMS_TWO + 1, jnp.zeros_like(line))


def fetch_hessian(hessian, held, sems):
    chunks = sems.shape[0]
    size = hessian.shape[0] // chunks
    copies = [
        pltpu.make_async_copy(
            hessian.at[pl.ds(k * size, size)], held.at[pl.ds(k * size, size)], sems.at[k]
        )
        for k in range(chunks)
    ]
    for copy in copies:
        copy.start()
    return copies, size


def contact_products(pairs, live_count, x8, y8, held, copies, size):
    y8[...] = jnp.zeros_like(y8)
    for h in range(held.shape[0]):
        if copies is not None and h % size == 0:
            copies[h // size].wait()
        a, b = pairs[h, 0], pairs[h, 1]
        delta = x8[a] - x8[b]
        delta = jnp.where(h < live_count, delta, 0.0)
        coarse = delta.astype(jnp.bfloat16).astype(F32)
        both = jnp.concatenate([coarse, delta - coarse], axis=0).astype(jnp.bfloat16)
        product = jnp.dot(both, held[h], preferred_element_type=F32)
        y = product[0:8] + product[8:16]
        y8[a] = y8[a] + y
        y8[b] = y8[b] - y


def wide(row):
    return jnp.broadcast_to(row, (8, row.shape[1]))


def contact_dot(x8, y8):
    value = x8[0] * y8[0]
    for p in range(1, x8.shape[0]):
        value = value + x8[p] * y8[p]
    return total(value[0:1])


def owner_kernel(pairs, live, got, hessian, message, x8, y8, z8, held, sems):
    copies, size = fetch_hessian(hessian, held, sems)
    peers, _, width = got.shape
    for d in range(peers):
        for c in range(CAP):
            x8[d * CAP + c] = wide(got[d, c : c + 1, :])
    contact_products(pairs, live[0], x8, y8, held, copies, size)
    line = line_of([contact_dot(x8, y8)], width)
    for d in range(peers):
        for c in range(CAP):
            p = d * CAP + c
            x8[p] = wide(got[d, CAP + c : CAP + c + 1, :]) + y8[p]
    contact_products(pairs, live[0], x8, z8, held, None, size)
    sub = iota((8, width), 0)
    for d in range(peers):
        tile = jnp.where(sub == SUMS_TWO, wide(line), 0.0)
        for c in range(CAP):
            tile = jnp.where(sub == c, y8[d * CAP + c], tile)
            tile = jnp.where(sub == CAP + c, z8[d * CAP + c], tile)
        message[d] = tile


def spread_kernel(send, got1, got2, db, mass, stiff, v1, dv1, v2, up, down, known, cb, cv1):
    rows = db.shape[1]
    scatter_blocks(send, got2, [cb, cv1])
    ky = masked_ky(stiff)
    for e in range(3):
        v = db[e] + from_panels(cb, e)
        v1[e] = v
        image = inner_apply(v, mass[...], stiff[0], ky)
        dv1[e] = image
        v2[e] = image + from_panels(cv1, e)
        up[e : e + 1, :] = v1[e, rows - 1 : rows, :]
        up[3 + e : 4 + e, :] = v2[e, rows - 1 : rows, :]
        down[e : e + 1, :] = v1[e, 0:1, :]
        down[3 + e : 4 + e, :] = v2[e, 0:1, :]
    sums1, sums2 = line_sum(got1, SUMS_TWO), line_sum(got2, SUMS_TWO)
    rr0 = pick(sums1, 0)
    alpha0 = rr0 / (pick(sums1, 1) + pick(sums2, 0))
    known[...] = line_of([rr0, alpha0], 128)


def edge_kernel(send, b, v1, dv1, v2, stiff, low, high, low1, high1, known, message, v2_out, full, panels):
    rows = b.shape[1]
    alpha0 = pick(known[...], 1)
    kx_low, kx_high = edge_coefs(stiff, low, high)
    sums = None
    for e in range(3):
        first = kx_low * (v1[e, 0:1, :] - low1[e : e + 1, :])
        last = kx_high * (v1[e, rows - 1 : rows, :] - high1[e : e + 1, :])
        full[e] = dv1[e]
        full[e, 0:1, :] = full[e, 0:1, :] + first
        full[e, rows - 1 : rows, :] = full[e, rows - 1 : rows, :] + last
        to_panels(panels, e, full[e])
        v2_out[e] = v2[e]
        v2_out[e, 0:1, :] = v2_out[e, 0:1, :] + first
        v2_out[e, rows - 1 : rows, :] = v2_out[e, rows - 1 : rows, :] + last
        right, image = b[e], v1[e]
        r1 = right - alpha0 * image
        w = image - alpha0 * v2_out[e]
        terms = [r1 * r1, r1 * w, r1 * image, right * w, right * image, w * w, w * image, image * image]
        sums = terms if sums is None else [s + t for s, t in zip(sums, terms)]
    line = line_of([total(s) for s in sums], message.shape[2])
    gather_blocks(send, [panels], message)
    put_line(message, SUMS_ONE, line)


def coefficients(known, sums):
    rr0, alpha0 = pick(known, 0), pick(known, 1)
    rr1, r1w, r1v1, bw, bv1, ww, wv1, v1v1 = [pick(sums, k) for k in range(8)]
    beta0 = rr1 / rr0
    alpha1 = rr1 / (r1w + beta0 * (r1v1 + bw) + beta0 * beta0 * bv1)
    image_sq = ww + 2.0 * beta0 * wv1 + beta0 * beta0 * v1v1
    rr2 = rr1 - 2.0 * alpha1 * (r1w + beta0 * r1v1) + alpha1 * alpha1 * image_sq
    return alpha0, beta0, alpha1, rr2 / rr1


def advance(b, v1, v2, coefs):
    alpha0, beta0, alpha1, beta1 = coefs
    r1 = b - alpha0 * v1
    d1 = r1 + beta0 * b
    r2 = r1 - alpha1 * (v1 - alpha0 * v2 + beta0 * v1)
    return d1, r2, r2 + beta1 * d1


def last_kernel(
    pairs, live, got1, sent2, got3, known, b, v1, v2, mass, stiff, low, high, low1, high1, hessian,
    message, part, r2_out, d2_out, dd2, x8, y8, held, sems,
):
    copies, size = fetch_hessian(hessian, held, sems)
    peers, _, width = got1.shape
    rows = b.shape[1]
    coefs = coefficients(known[...], line_sum(got3, SUMS_ONE))
    for d in range(peers):
        b_o = got1[d, 0:CAP, :]
        v1_o = got1[d, CAP : 2 * CAP, :] + sent2[d, 0:CAP, :]
        v2_o = got3[d, 0:CAP, :] + sent2[d, CAP : 2 * CAP, :]
        d2_o = advance(b_o, v1_o, v2_o, coefs)[2]
        for c in range(CAP):
            x8[d * CAP + c] = wide(d2_o[c : c + 1, :])

    kx_low, kx_high = edge_coefs(stiff, low, high)
    ky = masked_ky(stiff)
    sq = dot = None
    for e in range(3):
        d1, r2, d2 = advance(b[e], v1[e], v2[e], coefs)
        part[e] = coefs[0] * b[e] + coefs[2] * d1
        r2_out[e] = r2
        d2_out[e] = d2
        v1_low, v1_high = low1[e : e + 1, :], high1[e : e + 1, :]
        v2_low = low1[3 + e : 4 + e, :] + kx_low * (v1_low - v1[e, 0:1, :])
        v2_high = high1[3 + e : 4 + e, :] + kx_high * (v1_high - v1[e, rows - 1 : rows, :])
        d2_low = advance(low[e : e + 1, :], v1_low, v2_low, coefs)[2]
        d2_high = advance(high[e : e + 1, :], v1_high, v2_high, coefs)[2]
        dd2[e] = inner_apply(d2, mass[...], stiff[0], ky)
        dd2[e, 0:1, :] = dd2[e, 0:1, :] + kx_low * (d2_out[e, 0:1, :] - d2_low)
        dd2[e, rows - 1 : rows, :] = dd2[e, rows - 1 : rows, :] + kx_high * (
            d2_out[e, rows - 1 : rows, :] - d2_high
        )
        sq = r2 * r2 if sq is None else sq + r2 * r2
        dot = d2 * dd2[e] if dot is None else dot + d2 * dd2[e]
    rr2, dad2 = total(sq), total(dot)

    contact_products(pairs, live[0], x8, y8, held, copies, size)
    line = line_of([rr2, dad2 + contact_dot(x8, y8)], width)
    for d in range(peers):
        for c in range(CAP):
            message[d, c : c + 1, :] = y8[d * CAP + c, 0:1, :]
    put_line(message, SUMS_ONE, line)


def finish_kernel(send, got4, part, r2, d2, dd2, solution, residual, cd2):
    scatter_blocks(send, got4, [cd2])
    sums = line_sum(got4, SUMS_ONE)
    alpha2 = pick(sums, 0) / pick(sums, 1)
    for e in range(3):
        solution[e] = part[e] + alpha2 * d2[e]
        residual[e] = r2[e] - alpha2 * (dd2[e] + from_panels(cd2, e))


def call(kernel, spaces, outs, scratch=(), name=None):
    kinds = {"s": pltpu.SMEM, "v": pltpu.VMEM, "a": pl.ANY}
    return pl.pallas_call(
        kernel,
        out_shape=tuple(jax.ShapeDtypeStruct(shape, F32) for shape in outs),
        in_specs=[pl.BlockSpec(memory_space=kinds[k]) for k in spaces],
        out_specs=tuple(pl.BlockSpec(memory_space=pltpu.VMEM) for _ in outs),
        scratch_shapes=list(scratch),
        compiler_params=pltpu.CompilerParams(vmem_limit_bytes=VMEM_LIMIT),
        name=name,
    )


def per_device(right_side, masses, stiffness, hessian, send_list, pair_refs, counts):
    _, row_count, col_count = right_side.shape
    slot_count, width, _ = hessian.shape
    peers = lax.axis_size("gx")
    assert send_list.shape[1] == peers * CAP
    positions = peers * CAP
    field = right_side.shape
    two, one, edge = (peers, 8, width), (peers, 4, width), (6, col_count)
    chunks = next(k for k in (9, 6, 4, 3, 2, 1) if slot_count % k == 0)
    panels = pltpu.VMEM((3, col_count * 3 // width, row_count, width // 3), F32)
    tiles = pltpu.VMEM((positions, 8, width), F32)
    stored = [pltpu.VMEM(hessian.shape, hessian.dtype), pltpu.SemaphoreType.DMA((chunks,))]

    up = [(i, i + 1) for i in range(peers - 1)]
    down = [(i + 1, i) for i in range(peers - 1)]

    def swap(message):
        return lax.all_to_all(message, "gx", split_axis=0, concat_axis=0, tiled=True)

    low = lax.ppermute(jnp.concatenate([right_side[:, -1], stiffness[0, -1:]], axis=0), "gx", up)
    high = lax.ppermute(
        jnp.concatenate([right_side[:, 0], jnp.ones((1, col_count), F32)], axis=0), "gx", down
    )
    sent1, db = call(start_kernel, "svvvvv", [two, field], [panels, panels], name="start")(
        send_list, right_side, masses, stiffness, low, high
    )
    got1 = swap(sent1)
    (sent2,) = call(owner_kernel, "ssva", [two], [tiles, tiles, tiles, *stored], name="owner")(
        pair_refs, counts, got1, hessian
    )
    got2 = swap(sent2)
    v1, dv1, v2, up1, down1, known = call(
        spread_kernel,
        "svvvvv",
        [field, field, field, edge, edge, (1, 128)],
        [panels, panels],
        name="spread",
    )(send_list, got1, got2, db, masses, stiffness)
    low1 = lax.ppermute(up1, "gx", up)
    high1 = lax.ppermute(down1, "gx", down)
    sent3, v2 = call(
        edge_kernel, "svvvvvvvvvv", [one, field], [pltpu.VMEM(field, F32), panels], name="edge"
    )(send_list, right_side, v1, dv1, v2, stiffness, low, high, low1, high1, known)
    got3 = swap(sent3)
    sent4, part, r2, d2, dd2 = call(
        last_kernel, "ssvvvvvvvvvvvvva", [one] + [field] * 4, [tiles, tiles, *stored], name="last"
    )(
        pair_refs, counts, got1, sent2, got3, known, right_side, v1, v2, masses, stiffness,
        low, high, low1, high1, hessian,
    )
    got4 = swap(sent4)
    return call(
        finish_kernel, "svvvvv", [field, field], [panels], name="finish"
    )(send_list, got4, part, r2, d2, dd2)


def solution(mesh):
    placed = (
        P(None, ("groups", "gx"), None),
        P(("groups", "gx"), None),
        P(None, ("groups", "gx"), None),
        P(("groups", "gx"), None, None),
        P(("groups", "gx"), None),
        P(("groups", "gx"), None),
        P(("groups", "gx")),
    )
    return jax.shard_map(
        per_device,
        mesh=mesh,
        in_specs=placed,
        out_specs=(P(None, ("groups", "gx"), None), P(None, ("groups", "gx"), None)),
        check_vma=False,
    )
```

```python
import functools

import jax
import jax.numpy as jnp
from jax import lax
from jax.experimental import pallas as pl
from jax.experimental.pallas import tpu as pltpu
from jax.sharding import PartitionSpec as P

F32 = jnp.float32
CAP = 3
SUMS_TWO, SUMS_ONE = 2 * CAP, CAP


def iota(shape, dim):
    return lax.broadcasted_iota(jnp.int32, shape, dim)


def total(value):
    return jnp.sum(jnp.sum(value, axis=0, keepdims=True), axis=1, keepdims=True)


def line_of(scalars, width):
    lanes = iota((1, width), 1)
    line = jnp.zeros((1, width), F32)
    for k, value in enumerate(scalars):
        line = jnp.where(lanes == k, value, line)
    return line


def line_sum(message, row):
    peers = message.shape[0]
    parts = [message[d, row : row + 1, 0:128] for d in range(peers)]
    while len(parts) > 1:
        parts = [a + b for a, b in zip(parts[::2], parts[1::2])] + (
            parts[-1:] if len(parts) % 2 else []
        )
    return parts[0]


def pick(line, k):
    return line[:, k : k + 1]


def place_of(send, position, col_blocks):
    block = send[0, position]
    return lax.div(block, jnp.int32(col_blocks)), lax.rem(block, jnp.int32(col_blocks))


def gather_blocks(send, panels, message):
    peers = message.shape[0]
    _, col_blocks, _, block_len = panels[0].shape

    def one(d, carry):
        for c in range(CAP):
            row, col = place_of(send, d * CAP + c, col_blocks)
            for f, field in enumerate(panels):
                for e in range(3):
                    message[d, f * CAP + c : f * CAP + c + 1, e * block_len : (e + 1) * block_len] = (
                        field[e, col, pl.ds(row, 1), :]
                    )
        return carry

    lax.fori_loop(0, peers, one, 0, unroll=4)


def scatter_blocks(send, message, panels):
    peers = message.shape[0]
    _, col_blocks, _, block_len = panels[0].shape
    for field in panels:
        field[...] = jnp.zeros_like(field)

    def one(d, carry):
        for c in range(CAP):
            row, col = place_of(send, d * CAP + c, col_blocks)
            for f, field in enumerate(panels):
                for e in range(3):
                    field[e, col, pl.ds(row, 1), :] = message[
                        d, f * CAP + c : f * CAP + c + 1, e * block_len : (e + 1) * block_len
                    ]
        return carry

    lax.fori_loop(0, peers, one, 0, unroll=4)


def to_panels(panels, e, value):
    _, col_blocks, _, block_len = panels.shape
    for q in range(col_blocks):
        panels[e, q] = value[:, q * block_len : (q + 1) * block_len]


def from_panels(panels, e):
    return jnp.concatenate([panels[e, q] for q in range(panels.shape[1])], axis=1)


def put_line(message, row, line):
    for d in range(message.shape[0]):
        message[d, row : row + 1, :] = line


def inner_apply(v, mass, kx, ky):
    rows, cols = v.shape
    row_ids = iota((rows, cols), 0)
    flux_x = jnp.where(row_ids == rows - 1, 0.0, kx * (v - pltpu.roll(v, rows - 1, 0)))
    flux_y = ky * (v - pltpu.roll(v, cols - 1, 1))
    return mass * v + (flux_x - pltpu.roll(flux_x, 1, 0)) + (flux_y - pltpu.roll(flux_y, 1, 1))


def masked_ky(stiff):
    ky = stiff[1]
    return jnp.where(iota(ky.shape, 1) == ky.shape[1] - 1, 0.0, ky)


def edge_coefs(stiff, low, high):
    rows = stiff.shape[1]
    last = jnp.where(high[3:4, :] > 0.5, stiff[0, rows - 1 : rows, :], 0.0)
    return low[3:4, :], last


def start_kernel(send, b, mass, stiff, low, high, message, db, b_panels, db_panels):
    rows = b.shape[1]
    kx_low, kx_high = edge_coefs(stiff, low, high)
    ky = masked_ky(stiff)
    sq, dot = [], []
    for e in range(3):
        v = b[e]
        db[e] = inner_apply(v, mass[...], stiff[0], ky)
        first, last = b[e, 0:1, :], b[e, rows - 1 : rows, :]
        db[e, 0:1, :] = db[e, 0:1, :] + kx_low * (first - low[e : e + 1, :])
        db[e, rows - 1 : rows, :] = db[e, rows - 1 : rows, :] + kx_high * (last - high[e : e + 1, :])
        to_panels(b_panels, e, v)
        to_panels(db_panels, e, db[e])
        sq.append(v * v)
        dot.append(v * db[e])
    line = line_of([total(sq[0] + sq[1] + sq[2]), total(dot[0] + dot[1] + dot[2])], message.shape[2])
    gather_blocks(send, [b_panels, db_panels], message)
    put_line(message, SUMS_TWO, line)
    put_line(message, SUMS_TWO + 1, jnp.zeros_like(line))


def contact_products(pairs, live_count, x8, y8, held):
    y8[...] = jnp.zeros_like(y8)
    for h in range(held.shape[0]):
        a, b = pairs[h, 0], pairs[h, 1]
        delta = x8[a] - x8[b]
        delta = jnp.where(h < live_count, delta, 0.0)
        coarse = delta.astype(jnp.bfloat16).astype(F32)
        both = jnp.concatenate([coarse, delta - coarse], axis=0).astype(jnp.bfloat16)
        product = jnp.dot(both, held[h], preferred_element_type=F32)
        y = product[0:8] + product[8:16]
        y8[a] = y8[a] + y
        y8[b] = y8[b] - y


def wide(row):
    return jnp.broadcast_to(row, (8, row.shape[1]))


def contact_dot(x8, y8):
    value = x8[0] * y8[0]
    for p in range(1, x8.shape[0]):
        value = value + x8[p] * y8[p]
    return total(value[0:1])


def owner_kernel(pairs, live, got, hessian, message, x8, y8, z8):
    peers, _, width = got.shape
    for d in range(peers):
        for c in range(CAP):
            x8[d * CAP + c] = wide(got[d, c : c + 1, :])
    contact_products(pairs, live[0], x8, y8, hessian)
    line = line_of([contact_dot(x8, y8)], width)
    for d in range(peers):
        for c in range(CAP):
            p = d * CAP + c
            x8[p] = wide(got[d, CAP + c : CAP + c + 1, :]) + y8[p]
    contact_products(pairs, live[0], x8, z8, hessian)
    sub = iota((8, width), 0)
    for d in range(peers):
        tile = jnp.where(sub == SUMS_TWO, wide(line), 0.0)
        for c in range(CAP):
            tile = jnp.where(sub == c, y8[d * CAP + c], tile)
            tile = jnp.where(sub == CAP + c, z8[d * CAP + c], tile)
        message[d] = tile


def spread_kernel(send, got1, got2, db, mass, stiff, v1, dv1, v2, up, down, known, cb, cv1):
    rows = db.shape[1]
    scatter_blocks(send, got2, [cb, cv1])
    ky = masked_ky(stiff)
    for e in range(3):
        v = db[e] + from_panels(cb, e)
        v1[e] = v
        image = inner_apply(v, mass[...], stiff[0], ky)
        dv1[e] = image
        v2[e] = image + from_panels(cv1, e)
        up[e : e + 1, :] = v1[e, rows - 1 : rows, :]
        up[3 + e : 4 + e, :] = v2[e, rows - 1 : rows, :]
        down[e : e + 1, :] = v1[e, 0:1, :]
        down[3 + e : 4 + e, :] = v2[e, 0:1, :]
    sums1, sums2 = line_sum(got1, SUMS_TWO), line_sum(got2, SUMS_TWO)
    rr0 = pick(sums1, 0)
    alpha0 = rr0 / (pick(sums1, 1) + pick(sums2, 0))
    known[...] = line_of([rr0, alpha0], 128)


def edge_kernel(send, b, v1, dv1, v2, stiff, low, high, low1, high1, known, message, v2_out, full, panels):
    rows = b.shape[1]
    alpha0 = pick(known[...], 1)
    kx_low, kx_high = edge_coefs(stiff, low, high)
    sums = None
    for e in range(3):
        first = kx_low * (v1[e, 0:1, :] - low1[e : e + 1, :])
        last = kx_high * (v1[e, rows - 1 : rows, :] - high1[e : e + 1, :])
        full[e] = dv1[e]
        full[e, 0:1, :] = full[e, 0:1, :] + first
        full[e, rows - 1 : rows, :] = full[e, rows - 1 : rows, :] + last
        to_panels(panels, e, full[e])
        v2_out[e] = v2[e]
        v2_out[e, 0:1, :] = v2_out[e, 0:1, :] + first
        v2_out[e, rows - 1 : rows, :] = v2_out[e, rows - 1 : rows, :] + last
        right, image = b[e], v1[e]
        r1 = right - alpha0 * image
        w = image - alpha0 * v2_out[e]
        terms = [r1 * r1, r1 * w, r1 * image, right * w, right * image, w * w, w * image, image * image]
        sums = terms if sums is None else [s + t for s, t in zip(sums, terms)]
    line = line_of([total(s) for s in sums], message.shape[2])
    gather_blocks(send, [panels], message)
    put_line(message, SUMS_ONE, line)


def coefficients(known, sums):
    rr0, alpha0 = pick(known, 0), pick(known, 1)
    rr1, r1w, r1v1, bw, bv1, ww, wv1, v1v1 = [pick(sums, k) for k in range(8)]
    beta0 = rr1 / rr0
    alpha1 = rr1 / (r1w + beta0 * (r1v1 + bw) + beta0 * beta0 * bv1)
    image_sq = ww + 2.0 * beta0 * wv1 + beta0 * beta0 * v1v1
    rr2 = rr1 - 2.0 * alpha1 * (r1w + beta0 * r1v1) + alpha1 * alpha1 * image_sq
    return alpha0, beta0, alpha1, rr2 / rr1


def advance(b, v1, v2, coefs):
    alpha0, beta0, alpha1, beta1 = coefs
    r1 = b - alpha0 * v1
    d1 = r1 + beta0 * b
    r2 = r1 - alpha1 * (v1 - alpha0 * v2 + beta0 * v1)
    return d1, r2, r2 + beta1 * d1


def last_kernel(
    pairs, live, got1, sent2, got3, known, b, v1, v2, mass, stiff, low, high, low1, high1, hessian,
    message, part, r2_out, d2_out, dd2, x8, y8,
):
    peers, _, width = got1.shape
    rows = b.shape[1]
    coefs = coefficients(known[...], line_sum(got3, SUMS_ONE))
    for d in range(peers):
        b_o = got1[d, 0:CAP, :]
        v1_o = got1[d, CAP : 2 * CAP, :] + sent2[d, 0:CAP, :]
        v2_o = got3[d, 0:CAP, :] + sent2[d, CAP : 2 * CAP, :]
        d2_o = advance(b_o, v1_o, v2_o, coefs)[2]
        for c in range(CAP):
            x8[d * CAP + c] = wide(d2_o[c : c + 1, :])

    kx_low, kx_high = edge_coefs(stiff, low, high)
    ky = masked_ky(stiff)
    sq = dot = None
    for e in range(3):
        d1, r2, d2 = advance(b[e], v1[e], v2[e], coefs)
        part[e] = coefs[0] * b[e] + coefs[2] * d1
        r2_out[e] = r2
        d2_out[e] = d2
        v1_low, v1_high = low1[e : e + 1, :], high1[e : e + 1, :]
        v2_low = low1[3 + e : 4 + e, :] + kx_low * (v1_low - v1[e, 0:1, :])
        v2_high = high1[3 + e : 4 + e, :] + kx_high * (v1_high - v1[e, rows - 1 : rows, :])
        d2_low = advance(low[e : e + 1, :], v1_low, v2_low, coefs)[2]
        d2_high = advance(high[e : e + 1, :], v1_high, v2_high, coefs)[2]
        dd2[e] = inner_apply(d2, mass[...], stiff[0], ky)
        dd2[e, 0:1, :] = dd2[e, 0:1, :] + kx_low * (d2_out[e, 0:1, :] - d2_low)
        dd2[e, rows - 1 : rows, :] = dd2[e, rows - 1 : rows, :] + kx_high * (
            d2_out[e, rows - 1 : rows, :] - d2_high
        )
        sq = r2 * r2 if sq is None else sq + r2 * r2
        dot = d2 * dd2[e] if dot is None else dot + d2 * dd2[e]
    rr2, dad2 = total(sq), total(dot)

    contact_products(pairs, live[0], x8, y8, hessian)
    line = line_of([rr2, dad2 + contact_dot(x8, y8)], width)
    for d in range(peers):
        for c in range(CAP):
            message[d, c : c + 1, :] = y8[d * CAP + c, 0:1, :]
    put_line(message, SUMS_ONE, line)


def finish_kernel(send, got4, part, r2, d2, dd2, solution, residual, cd2):
    scatter_blocks(send, got4, [cd2])
    sums = line_sum(got4, SUMS_ONE)
    alpha2 = pick(sums, 0) / pick(sums, 1)
    for e in range(3):
        solution[e] = part[e] + alpha2 * d2[e]
        residual[e] = r2[e] - alpha2 * (dd2[e] + from_panels(cd2, e))


def call(kernel, spaces, outs, scratch=(), mebibytes=12, name=None):
    kinds = {"s": pltpu.SMEM, "v": pltpu.VMEM}
    return pl.pallas_call(
        kernel,
        out_shape=tuple(jax.ShapeDtypeStruct(shape, F32) for shape in outs),
        in_specs=[pl.BlockSpec(memory_space=kinds[k]) for k in spaces],
        out_specs=tuple(pl.BlockSpec(memory_space=pltpu.VMEM) for _ in outs),
        scratch_shapes=list(scratch),
        compiler_params=pltpu.CompilerParams(vmem_limit_bytes=mebibytes * 1024 * 1024),
        name=name,
    )


def per_device(right_side, masses, stiffness, hessian, send_list, pair_refs, counts):
    _, row_count, col_count = right_side.shape
    width = hessian.shape[1]
    peers = lax.axis_size("gx")
    assert send_list.shape[1] == peers * CAP
    positions = peers * CAP
    field = right_side.shape
    two, one, edge = (peers, 8, width), (peers, 4, width), (6, col_count)
    panels = pltpu.VMEM((3, col_count * 3 // width, row_count, width // 3), F32)
    tiles = pltpu.VMEM((positions, 8, width), F32)

    up = [(i, i + 1) for i in range(peers - 1)]
    down = [(i + 1, i) for i in range(peers - 1)]

    def swap(message):
        return lax.all_to_all(message, "gx", split_axis=0, concat_axis=0, tiled=True)

    low = lax.ppermute(jnp.concatenate([right_side[:, -1], stiffness[0, -1:]], axis=0), "gx", up)
    high = lax.ppermute(
        jnp.concatenate([right_side[:, 0], jnp.ones((1, col_count), F32)], axis=0), "gx", down
    )
    sent1, db = call(start_kernel, "svvvvv", [two, field], [panels, panels], name="start")(
        send_list, right_side, masses, stiffness, low, high
    )
    got1 = swap(sent1)
    (sent2,) = call(owner_kernel, "ssvv", [two], [tiles] * 3, 24, name="owner")(
        pair_refs, counts, got1, hessian
    )
    got2 = swap(sent2)
    v1, dv1, v2, up1, down1, known = call(
        spread_kernel,
        "svvvvv",
        [field, field, field, edge, edge, (1, 128)],
        [panels, panels],
        name="spread",
    )(send_list, got1, got2, db, masses, stiffness)
    low1 = lax.ppermute(up1, "gx", up)
    high1 = lax.ppermute(down1, "gx", down)
    sent3, v2 = call(
        edge_kernel, "svvvvvvvvvv", [one, field], [pltpu.VMEM(field, F32), panels], name="edge"
    )(send_list, right_side, v1, dv1, v2, stiffness, low, high, low1, high1, known)
    got3 = swap(sent3)
    sent4, part, r2, d2, dd2 = call(
        last_kernel, "ssvvvvvvvvvvvvvv", [one] + [field] * 4, [tiles] * 2, 24, name="last"
    )(
        pair_refs, counts, got1, sent2, got3, known, right_side, v1, v2, masses, stiffness,
        low, high, low1, high1, hessian,
    )
    got4 = swap(sent4)
    return call(
        finish_kernel, "svvvvv", [field, field], [panels], name="finish"
    )(send_list, got4, part, r2, d2, dd2)


def solution(mesh):
    placed = (
        P(None, ("groups", "gx"), None),
        P(("groups", "gx"), None),
        P(None, ("groups", "gx"), None),
        P(("groups", "gx"), None, None),
        P(("groups", "gx"), None),
        P(("groups", "gx"), None),
        P(("groups", "gx")),
    )
    return jax.shard_map(
        per_device,
        mesh=mesh,
        in_specs=placed,
        out_specs=(P(None, ("groups", "gx"), None), P(None, ("groups", "gx"), None)),
        check_vma=False,
    )
```

```python
import jax
import jax.numpy as jnp
from jax import lax
from jax.experimental import pallas as pl
from jax.experimental.pallas import tpu as pltpu
from jax.sharding import PartitionSpec as P

F32 = jnp.float32
BF16 = jnp.bfloat16
CAP = 3
SUMS_TWO, SUMS_ONE = 2 * CAP, CAP
CODE_LANE = 64


def iota(shape, dim):
    return lax.broadcasted_iota(jnp.int32, shape, dim)


def total(value):
    return jnp.sum(jnp.sum(value, axis=0, keepdims=True), axis=1, keepdims=True)


def line_of(scalars, width):
    lanes = iota((1, width), 1)
    line = jnp.zeros((1, width), F32)
    for k, value in enumerate(scalars):
        line = jnp.where(lanes == k, value, line)
    return line


def line_sum(message, row):
    peers = message.shape[0]
    parts = [message[d, row : row + 1, 0:128] for d in range(peers)]
    while len(parts) > 1:
        parts = [a + b for a, b in zip(parts[::2], parts[1::2])] + (
            parts[-1:] if len(parts) % 2 else []
        )
    return parts[0]


def pick(line, k):
    return line[:, k : k + 1]


def place_of(send, position, col_blocks):
    block = send[0, position]
    return lax.div(block, jnp.int32(col_blocks)), lax.rem(block, jnp.int32(col_blocks))


def scatter_blocks(send, message, panels):
    peers = message.shape[0]
    _, col_blocks, _, block_len = panels[0].shape
    for field in panels:
        field[...] = jnp.zeros_like(field)

    def one(d, carry):
        for c in range(CAP):
            row, col = place_of(send, d * CAP + c, col_blocks)
            for f, field in enumerate(panels):
                for e in range(3):
                    field[e, col, pl.ds(row, 1), :] = message[
                        d, f * CAP + c : f * CAP + c + 1, e * block_len : (e + 1) * block_len
                    ]
        return carry

    lax.fori_loop(0, peers, one, 0, unroll=4)


def to_panels(panels, e, value):
    _, col_blocks, _, block_len = panels.shape
    for q in range(col_blocks):
        panels[e, q] = value[:, q * block_len : (q + 1) * block_len]


def from_panels(panels, e):
    return jnp.concatenate([panels[e, q] for q in range(panels.shape[1])], axis=1)


def put_line(message, row, line):
    for d in range(message.shape[0]):
        message[d, row : row + 1, :] = line


def inner_apply(v, mass, kx, ky):
    rows, cols = v.shape
    row_ids = iota((rows, cols), 0)
    flux_x = jnp.where(row_ids == rows - 1, 0.0, kx * (v - pltpu.roll(v, rows - 1, 0)))
    flux_y = ky * (v - pltpu.roll(v, cols - 1, 1))
    return mass * v + (flux_x - pltpu.roll(flux_x, 1, 0)) + (flux_y - pltpu.roll(flux_y, 1, 1))


def masked_ky(stiff):
    ky = stiff[1]
    return jnp.where(iota(ky.shape, 1) == ky.shape[1] - 1, 0.0, ky)


def rounded(value):
    return value.astype(BF16).astype(F32)


def packed_line(scalars):
    parts = []
    for value in scalars:
        high = rounded(value)
        middle = rounded(value - high)
        parts += [high, middle, value - high - middle]
    return line_of(parts, 128)


def pick_packed(line, k):
    return pick(line, 3 * k) + pick(line, 3 * k + 1) + pick(line, 3 * k + 2)


def thrice(tile):
    return jnp.concatenate([tile] * 3, axis=1)


def write_rim(target, field):
    rows, block_len = field.shape[1], 128
    col_blocks = field.shape[2] // block_len
    for side, row in enumerate((0, rows - 1)):
        for q in range(col_blocks):
            for e in range(3):
                line = side * col_blocks + q
                target[line : line + 1, e * block_len : (e + 1) * block_len] = field[
                    e, row : row + 1, q * block_len : (q + 1) * block_len
                ]


def rim_row(tile, side, e):
    block_len = tile.shape[1] // 3
    half = tile.shape[0] // 2
    return jnp.concatenate(
        [
            tile[side * half + q : side * half + q + 1, e * block_len : (e + 1) * block_len]
            for q in range(half)
        ],
        axis=1,
    )


def across(before, after):
    half = before.shape[0] // 2
    return pltpu.roll(jnp.where(iota(before.shape, 0) >= half, before, after), half, 0)


def around(d, peers):
    return jnp.maximum(d - 1, 0), jnp.minimum(d + 1, peers - 1)


def rim_coefs(tiles, d):
    before, _ = around(d, tiles.shape[0])
    here, other = tiles[d, 0:8, 384:512], tiles[before, 0:8, 384:512]
    other = jnp.where(d > 0, other, 0.0)
    return thrice(jnp.where(iota(here.shape, 0) < 4, other, here))


def chosen(code, tile):
    return jnp.sum(
        jnp.where(iota(tile.shape, 0).astype(F32) == code, tile, 0.0), axis=0, keepdims=True
    )


def start_kernel(send, b, mass, stiff, message, loc, b_panels, loc_panels, rim, stage):
    rows, peers = b.shape[1], message.shape[0]
    col_blocks, block_len = b_panels.shape[1], b_panels.shape[3]
    ky = masked_ky(stiff)
    sq = dot = None
    for e in range(3):
        v = b[e]
        image = inner_apply(v, mass[...], stiff[0], ky)
        loc[e] = image
        to_panels(b_panels, e, v)
        to_panels(loc_panels, e, image)
        sq = v * v if sq is None else sq + v * v
        dot = v * image if dot is None else dot + v * image
    write_rim(rim, b)
    ends = lax.axis_index("gx") == peers - 1
    for q in range(col_blocks):
        kx = stiff[0, rows - 1 : rows, q * block_len : (q + 1) * block_len]
        kx = jnp.where(ends, 0.0, kx)
        rim[q : q + 1, 3 * block_len :] = kx
        rim[col_blocks + q : col_blocks + q + 1, 3 * block_len :] = kx
    line = packed_line([total(sq), total(dot)])
    lanes, sub = iota((1, 128), 1), iota((8, 3 * block_len), 0)
    sub_one = iota((8, block_len), 0)

    def one(d, carry):
        own_line = line
        for c in range(CAP):
            row, col = place_of(send, d * CAP + c, col_blocks)
            code = jnp.where(row == 0, col, jnp.where(row == rows - 1, col_blocks + col, 99))
            own_line = jnp.where(lanes == CODE_LANE + c, code.astype(F32), own_line)
            for e in range(3):
                span = slice(e * block_len, (e + 1) * block_len)
                stage[d, c : c + 1, span] = b_panels[e, col, pl.ds(row, 1), :]
                stage[d, CAP + c : CAP + c + 1, span] = loc_panels[e, col, pl.ds(row, 1), :]
        body = stage[d]
        rest = pltpu.roll(body - rounded(body), 3, 0)
        body = jnp.where(sub >= 2 * CAP, rest, body)
        extra = jnp.where(sub_one == 4, wide(own_line), 0.0)
        for j in range(3):
            piece = rest[0:1, j * block_len : (j + 1) * block_len]
            extra = jnp.where(sub_one == j, wide(piece), extra)
        lower = jnp.concatenate([body, extra], axis=1)
        message[d] = jnp.concatenate([rim[...], lower], axis=0).astype(BF16)
        return carry

    lax.fori_loop(0, peers, one, 0, unroll=4)


def contact_products(pairs, live_count, x8, y8, held):
    y8[...] = jnp.zeros_like(y8)
    for h in range(held.shape[0]):
        a, b = pairs[h, 0], pairs[h, 1]
        delta = x8[a] - x8[b]
        delta = jnp.where(h < live_count, delta, 0.0)
        coarse = delta.astype(jnp.bfloat16).astype(F32)
        both = jnp.concatenate([coarse, delta - coarse], axis=0).astype(jnp.bfloat16)
        product = jnp.dot(both, held[h], preferred_element_type=F32)
        y = product[0:8] + product[8:16]
        y8[a] = y8[a] + y
        y8[b] = y8[b] - y


def wide(row):
    return jnp.broadcast_to(row, (8, row.shape[1]))


def contact_dot(x8, y8):
    value = x8[0] * y8[0]
    for p in range(1, x8.shape[0]):
        value = value + x8[p] * y8[p]
    return total(value[0:1])


def owner_kernel(
    pairs, live, got, hessian, message, held, own, known, x8, y8, z8, f8, tiles, corr
):
    peers, _, _ = got.shape
    width = x8.shape[2]
    block_len = width // 3
    for d in range(peers):
        tiles[d] = got[d].astype(F32)

    def one(d, carry):
        energy, sums = carry
        before, after = around(d, peers)
        diff = tiles[d, 0:8, 0:width] - across(
            tiles[before, 0:8, 0:width], tiles[after, 0:8, 0:width]
        )
        fix = rim_coefs(tiles, d) * diff
        corr[d] = fix
        body, extra = tiles[d, 8:16, 0:width], tiles[d, 8:16, width:]
        line = extra[4:5, :]
        rest = [body[6:7], body[7:8], jnp.concatenate([extra[j : j + 1] for j in range(3)], axis=1)]
        for c in range(CAP):
            p = d * CAP + c
            x8[p] = wide(body[c : c + 1])
            value = body[CAP + c : CAP + c + 1] + rest[c]
            f8[p] = wide(value + chosen(pick(line, CODE_LANE + c), fix))
        return energy + fix * diff, sums + line

    zero = jnp.zeros((8, width), F32)
    energy, sums = lax.fori_loop(0, peers, one, (zero, jnp.zeros((1, block_len), F32)), unroll=4)
    known[...] = line_of(
        [pick_packed(sums, 0), pick_packed(sums, 1) + 0.5 * total(energy)], known.shape[1]
    )
    own[...] = corr[lax.axis_index("gx")]

    contact_products(pairs, live[0], x8, y8, hessian)
    line = line_of([contact_dot(x8, y8)], width)
    for p in range(x8.shape[0]):
        x8[p] = f8[p] + y8[p]
    contact_products(pairs, live[0], x8, z8, hessian)
    sub = iota((8, width), 0)
    for d in range(peers):
        tile = jnp.where(sub == SUMS_TWO, wide(line), 0.0)
        kept = tiles[d, 8:16, 0:width]
        for c in range(CAP):
            tile = jnp.where(sub == c, y8[d * CAP + c], tile)
            tile = jnp.where(sub == CAP + c, z8[d * CAP + c], tile)
            kept = jnp.where(sub == CAP + c, x8[d * CAP + c], kept)
        message[d] = tile
        held[d] = kept


def middle_kernel(
    send, got2, own, known1, b, loc, mass, stiff, message, v1, v2, known, cb, cv1, panels, common, stage
):
    rows, peers = b.shape[1], message.shape[0]
    col_blocks, block_len = panels.shape[1], panels.shape[3]
    scatter_blocks(send, got2, [cb, cv1])
    ky = masked_ky(stiff)
    rr0 = pick(known1[...], 0)
    alpha0 = rr0 / (pick(known1[...], 1) + pick(line_sum(got2, SUMS_TWO), 0))
    known[...] = line_of([rr0, alpha0], known.shape[1])
    sums = None
    for e in range(3):
        v1[e] = loc[e] + from_panels(cb, e)
        for side, row in enumerate((0, rows - 1)):
            v1[e, row : row + 1, :] = v1[e, row : row + 1, :] + rim_row(own[...], side, e)
        image = v1[e]
        inner = inner_apply(image, mass[...], stiff[0], ky)
        to_panels(panels, e, inner)
        second = inner + from_panels(cv1, e)
        v2[e] = second
        right = b[e]
        r1 = right - alpha0 * image
        w = image - alpha0 * second
        terms = [r1 * r1, r1 * w, r1 * image, right * w, right * image, w * w, w * image, image * image]
        sums = terms if sums is None else [s + t for s, t in zip(sums, terms)]
    write_rim(common.at[0], v1)
    write_rim(common.at[1], v2)
    line = packed_line([total(s) for s in sums])
    line = jnp.broadcast_to(line, (16, block_len))
    sub = iota((16, block_len), 0)

    def one(d, carry):
        for c in range(CAP):
            row, col = place_of(send, d * CAP + c, col_blocks)
            for e in range(3):
                stage[d, c * 3 + e : c * 3 + e + 1, :] = panels[e, col, pl.ds(row, 1), :]
        extra = jnp.where(sub < 9, stage[d], jnp.where(sub == 9, line, 0.0))
        rims = jnp.concatenate([common[0], common[1]], axis=0)
        message[d] = jnp.concatenate([rims, extra], axis=1).astype(BF16)
        return carry

    lax.fori_loop(0, peers, one, 0, unroll=4)


def coefficients(known, sums, b_x, v1_x, v2_x, x_x):
    rr0, alpha0 = pick(known, 0), pick(known, 1)
    rr1, r1w, r1v1, bw, bv1, ww, wv1, v1v1 = [pick_packed(sums, k) for k in range(8)]
    r1w = r1w - alpha0 * (b_x - alpha0 * v1_x)
    bw = bw - alpha0 * b_x
    ww = ww - 2.0 * alpha0 * (v1_x - alpha0 * v2_x) + alpha0 * alpha0 * x_x
    wv1 = wv1 - alpha0 * v1_x
    beta0 = rr1 / rr0
    alpha1 = rr1 / (r1w + beta0 * (r1v1 + bw) + beta0 * beta0 * bv1)
    image_sq = ww + 2.0 * beta0 * wv1 + beta0 * beta0 * v1v1
    rr2 = rr1 - 2.0 * alpha1 * (r1w + beta0 * r1v1) + alpha1 * alpha1 * image_sq
    return alpha0, beta0, alpha1, rr2 / rr1


def advance(b, v1, v2, coefs):
    alpha0, beta0, alpha1, beta1 = coefs
    r1 = b - alpha0 * v1
    d1 = r1 + beta0 * b
    r2 = r1 - alpha1 * (v1 - alpha0 * v2 + beta0 * v1)
    return d1, r2, r2 + beta1 * d1


def last_kernel(
    pairs, live, got1, got3, held, sent2, known, b, v1, v2, mass, stiff, hessian,
    message, part, r2_out, d2_out, dd2, x8, y8, tiles1, tiles3, corr, rim,
):
    peers = got1.shape[0]
    width = x8.shape[2]
    rows = b.shape[1]
    for d in range(peers):
        tiles1[d] = got1[d].astype(F32)
        tiles3[d] = got3[d].astype(F32)

    def one(d, carry):
        before, after = around(d, peers)
        first = tiles3[d, 0:8, 0:width]
        fix = rim_coefs(tiles1, d) * (
            first - across(tiles3[before, 0:8, 0:width], tiles3[after, 0:8, 0:width])
        )
        corr[d] = fix
        others = [tiles1[d, 0:8, 0:width], first, tiles3[d, 8:16, 0:width], fix]
        return (
            *[kept + other * fix for kept, other in zip(carry, others)],
            carry[4] + tiles3[d, 9:10, width:],
        )

    zero = jnp.zeros((8, width), F32)
    *crossing, sums = lax.fori_loop(
        0, peers, one, (zero, zero, zero, zero, jnp.zeros((1, 128), F32)), unroll=4
    )
    coefs = coefficients(known[...], sums, *[total(value) for value in crossing])

    def two(d, carry):
        extra, line = tiles3[d, 0:16, width:], tiles1[d, 12:13, width:]
        fix = corr[d]
        kept, sent = held[d], sent2[d]
        for c in range(CAP):
            value = jnp.concatenate([extra[c * 3 + e : c * 3 + e + 1] for e in range(3)], axis=1)
            value = value + chosen(pick(line, CODE_LANE + c), fix) + sent[CAP + c : CAP + c + 1]
            x8[d * CAP + c] = wide(
                advance(kept[c : c + 1], kept[CAP + c : CAP + c + 1], value, coefs)[2]
            )
        return carry

    lax.fori_loop(0, peers, two, 0, unroll=4)

    me = lax.axis_index("gx")
    before, after = around(me, peers)
    ky = masked_ky(stiff)
    mine = corr[me] * (coefs[0] * coefs[2])
    for e in range(3):
        d1, r2, d2 = advance(b[e], v1[e], v2[e], coefs)
        part[e] = coefs[0] * b[e] + coefs[2] * d1
        r2_out[e] = r2
        d2_out[e] = d2
        for side, row in enumerate((0, rows - 1)):
            r2_out[e, row : row + 1, :] = r2_out[e, row : row + 1, :] + rim_row(mine, side, e)
            d2_out[e, row : row + 1, :] = d2_out[e, row : row + 1, :] + rim_row(mine, side, e)
    write_rim(rim, d2_out)

    def rim_direction(d):
        return advance(
            tiles1[d, 0:8, 0:width],
            tiles3[d, 0:8, 0:width],
            tiles3[d, 8:16, 0:width] + corr[d],
            coefs,
        )[2]

    fix = rim_coefs(tiles1, me) * (rim[...] - across(rim_direction(before), rim_direction(after)))
    sq = dot = None
    for e in range(3):
        r2, d2 = r2_out[e], d2_out[e]
        dd2[e] = inner_apply(d2, mass[...], stiff[0], ky)
        for side, row in enumerate((0, rows - 1)):
            dd2[e, row : row + 1, :] = dd2[e, row : row + 1, :] + rim_row(fix, side, e)
        sq = r2 * r2 if sq is None else sq + r2 * r2
        dot = d2 * dd2[e] if dot is None else dot + d2 * dd2[e]
    rr2, dad2 = total(sq), total(dot)

    contact_products(pairs, live[0], x8, y8, hessian)
    line = line_of([rr2, dad2 + contact_dot(x8, y8)], width)
    for d in range(peers):
        for c in range(CAP):
            message[d, c : c + 1, :] = y8[d * CAP + c, 0:1, :]
    put_line(message, SUMS_ONE, line)


def finish_kernel(send, got4, part, r2, d2, dd2, solution, residual, cd2):
    scatter_blocks(send, got4, [cd2])
    sums = line_sum(got4, SUMS_ONE)
    alpha2 = pick(sums, 0) / pick(sums, 1)
    for e in range(3):
        solution[e] = part[e] + alpha2 * d2[e]
        residual[e] = r2[e] - alpha2 * (dd2[e] + from_panels(cd2, e))


def call(kernel, spaces, outs, scratch=(), mebibytes=16, name=None):
    kinds = {"s": pltpu.SMEM, "v": pltpu.VMEM}
    return pl.pallas_call(
        kernel,
        out_shape=tuple(jax.ShapeDtypeStruct(shape, kind) for shape, kind in outs),
        in_specs=[pl.BlockSpec(memory_space=kinds[k]) for k in spaces],
        out_specs=tuple(pl.BlockSpec(memory_space=pltpu.VMEM) for _ in outs),
        scratch_shapes=[pltpu.VMEM(shape, F32) for shape in scratch],
        compiler_params=pltpu.CompilerParams(vmem_limit_bytes=mebibytes * 2**20),
        name=name,
    )


def per_device(right_side, masses, stiffness, hessian, send_list, pair_refs, counts):
    _, row_count, col_count = right_side.shape
    width = hessian.shape[1]
    block_len = width // 3
    peers = lax.axis_size("gx")
    assert send_list.shape[1] == peers * CAP and col_count == 4 * block_len and block_len == 128
    field = (right_side.shape, F32)
    two, one = ((peers, 8, width), F32), ((peers, 4, width), F32)
    full = ((peers, 16, 4 * block_len), BF16)
    panels = (3, 4, row_count, block_len)
    tiles, wide_tiles, rims = (peers * CAP, 8, width), (peers, 16, 4 * block_len), (peers, 8, width)
    line = ((1, 128), F32)

    def swap(message):
        return lax.all_to_all(message, "gx", split_axis=0, concat_axis=0, tiled=True)

    sent1, loc = call(
        start_kernel,
        "svvv",
        [full, field],
        [panels, panels, (8, 4 * block_len), rims],
        name="start",
    )(send_list, right_side, masses, stiffness)
    got1 = swap(sent1)
    sent2, held, own, known1 = call(
        owner_kernel,
        "ssvv",
        [two, two, ((8, width), F32), line],
        [tiles, tiles, tiles, tiles, wide_tiles, rims],
        32,
        name="owner",
    )(pair_refs, counts, got1, hessian)
    got2 = swap(sent2)
    sent3, v1, v2, known = call(
        middle_kernel,
        "svvvvvvv",
        [full, field, field, line],
        [panels, panels, panels, (2, 8, width), (peers, 16, block_len)],
        name="middle",
    )(send_list, got2, own, known1, right_side, loc, masses, stiffness)
    got3 = swap(sent3)
    sent4, part, r2, d2, dd2 = call(
        last_kernel,
        "ssvvvvvvvvvvv",
        [one, field, field, field, field],
        [tiles, tiles, wide_tiles, wide_tiles, rims, (8, width)],
        32,
        name="last",
    )(
        pair_refs, counts, got1, got3, held, sent2, known, right_side, v1, v2, masses, stiffness,
        hessian,
    )
    got4 = swap(sent4)
    return call(finish_kernel, "svvvvv", [field, field], [panels], name="finish")(
        send_list, got4, part, r2, d2, dd2
    )


def solution(mesh):
    placed = (
        P(None, ("groups", "gx"), None),
        P(("groups", "gx"), None),
        P(None, ("groups", "gx"), None),
        P(("groups", "gx"), None, None),
        P(("groups", "gx"), None),
        P(("groups", "gx"), None),
        P(("groups", "gx")),
    )
    return jax.shard_map(
        per_device,
        mesh=mesh,
        in_specs=placed,
        out_specs=(P(None, ("groups", "gx"), None), P(None, ("groups", "gx"), None)),
        check_vma=False,
    )
```

```python
import jax
import jax.numpy as jnp
from jax import lax
from jax.experimental import pallas as pl
from jax.experimental.pallas import tpu as pltpu
from jax.sharding import PartitionSpec as P

F32 = jnp.float32
BF16 = jnp.bfloat16
CAP = 3
SUMS_TWO, SUMS_ONE = 2 * CAP, CAP
CODE_LANE = 64


def iota(shape, dim):
    return lax.broadcasted_iota(jnp.int32, shape, dim)


def total(value):
    return jnp.sum(jnp.sum(value, axis=0, keepdims=True), axis=1, keepdims=True)


def line_of(scalars, width):
    lanes = iota((1, width), 1)
    line = jnp.zeros((1, width), F32)
    for k, value in enumerate(scalars):
        line = jnp.where(lanes == k, value, line)
    return line


def line_sum(message, row):
    peers = message.shape[0]
    parts = [message[d, row : row + 1, 0:128] for d in range(peers)]
    while len(parts) > 1:
        parts = [a + b for a, b in zip(parts[::2], parts[1::2])] + (
            parts[-1:] if len(parts) % 2 else []
        )
    return parts[0]


def pick(line, k):
    return line[:, k : k + 1]


def place_of(send, position, col_blocks):
    block = send[0, position]
    return lax.div(block, jnp.int32(col_blocks)), lax.rem(block, jnp.int32(col_blocks))


def scatter_blocks(send, message, panels):
    peers = message.shape[0]
    _, col_blocks, _, block_len = panels[0].shape
    for field in panels:
        field[...] = jnp.zeros_like(field)

    def one(d, carry):
        for c in range(CAP):
            row, col = place_of(send, d * CAP + c, col_blocks)
            for f, field in enumerate(panels):
                for e in range(3):
                    field[e, col, pl.ds(row, 1), :] = message[
                        d, f * CAP + c : f * CAP + c + 1, e * block_len : (e + 1) * block_len
                    ]
        return carry

    lax.fori_loop(0, peers, one, 0, unroll=4)


def to_panels(panels, e, value):
    _, col_blocks, _, block_len = panels.shape
    for q in range(col_blocks):
        panels[e, q] = value[:, q * block_len : (q + 1) * block_len]


def from_panels(panels, e):
    return jnp.concatenate([panels[e, q] for q in range(panels.shape[1])], axis=1)


def put_line(message, row, line):
    for d in range(message.shape[0]):
        message[d, row : row + 1, :] = line


def inner_apply(v, mass, kx, ky):
    rows, cols = v.shape
    row_ids = iota((rows, cols), 0)
    flux_x = jnp.where(row_ids == rows - 1, 0.0, kx * (v - pltpu.roll(v, rows - 1, 0)))
    flux_y = ky * (v - pltpu.roll(v, cols - 1, 1))
    return mass * v + (flux_x - pltpu.roll(flux_x, 1, 0)) + (flux_y - pltpu.roll(flux_y, 1, 1))


def masked_ky(stiff):
    ky = stiff[1]
    return jnp.where(iota(ky.shape, 1) == ky.shape[1] - 1, 0.0, ky)


def rounded(value):
    return value.astype(BF16).astype(F32)


def packed_line(scalars):
    parts = []
    for value in scalars:
        high = rounded(value)
        middle = rounded(value - high)
        parts += [high, middle, value - high - middle]
    return line_of(parts, 128)


def pick_packed(line, k):
    return pick(line, 3 * k) + pick(line, 3 * k + 1) + pick(line, 3 * k + 2)


def thrice(tile):
    return jnp.concatenate([tile] * 3, axis=1)


def write_rim(target, field):
    rows, block_len = field.shape[1], 128
    col_blocks = field.shape[2] // block_len
    for side, row in enumerate((0, rows - 1)):
        for q in range(col_blocks):
            for e in range(3):
                line = side * col_blocks + q
                target[line : line + 1, e * block_len : (e + 1) * block_len] = field[
                    e, row : row + 1, q * block_len : (q + 1) * block_len
                ]


def rim_row(tile, side, e):
    block_len = tile.shape[1] // 3
    half = tile.shape[0] // 2
    return jnp.concatenate(
        [
            tile[side * half + q : side * half + q + 1, e * block_len : (e + 1) * block_len]
            for q in range(half)
        ],
        axis=1,
    )


def across(before, after):
    half = before.shape[0] // 2
    return pltpu.roll(jnp.where(iota(before.shape, 0) >= half, before, after), half, 0)


def around(d, peers):
    return jnp.maximum(d - 1, 0), jnp.minimum(d + 1, peers - 1)


def rim_coefs(tiles, d):
    before, _ = around(d, tiles.shape[0])
    here, other = tiles[d, 0:8, 384:512], tiles[before, 0:8, 384:512]
    other = jnp.where(d > 0, other, 0.0)
    return thrice(jnp.where(iota(here.shape, 0) < 4, other, here))


def chosen(code, tile):
    return jnp.sum(
        jnp.where(iota(tile.shape, 0).astype(F32) == code, tile, 0.0), axis=0, keepdims=True
    )


def announce_kernel(hessian, token):
    token[...] = jnp.zeros_like(token)


def start_kernel(_, send, b, mass, stiff, message, loc, b_panels, loc_panels, rim, stage):
    rows, peers = b.shape[1], message.shape[0]
    col_blocks, block_len = b_panels.shape[1], b_panels.shape[3]
    ky = masked_ky(stiff)
    sq = dot = None
    for e in range(3):
        v = b[e]
        image = inner_apply(v, mass[...], stiff[0], ky)
        loc[e] = image
        to_panels(b_panels, e, v)
        to_panels(loc_panels, e, image)
        sq = v * v if sq is None else sq + v * v
        dot = v * image if dot is None else dot + v * image
    write_rim(rim, b)
    ends = lax.axis_index("gx") == peers - 1
    for q in range(col_blocks):
        kx = stiff[0, rows - 1 : rows, q * block_len : (q + 1) * block_len]
        kx = jnp.where(ends, 0.0, kx)
        rim[q : q + 1, 3 * block_len :] = kx
        rim[col_blocks + q : col_blocks + q + 1, 3 * block_len :] = kx
    line = packed_line([total(sq), total(dot)])
    lanes, sub = iota((1, 128), 1), iota((8, 3 * block_len), 0)
    sub_one = iota((8, block_len), 0)

    def one(d, carry):
        own_line = line
        for c in range(CAP):
            row, col = place_of(send, d * CAP + c, col_blocks)
            code = jnp.where(row == 0, col, jnp.where(row == rows - 1, col_blocks + col, 99))
            own_line = jnp.where(lanes == CODE_LANE + c, code.astype(F32), own_line)
            for e in range(3):
                span = slice(e * block_len, (e + 1) * block_len)
                stage[d, c : c + 1, span] = b_panels[e, col, pl.ds(row, 1), :]
                stage[d, CAP + c : CAP + c + 1, span] = loc_panels[e, col, pl.ds(row, 1), :]
        body = stage[d]
        rest = pltpu.roll(body - rounded(body), 3, 0)
        body = jnp.where(sub >= 2 * CAP, rest, body)
        extra = jnp.where(sub_one == 4, wide(own_line), 0.0)
        for j in range(3):
            piece = rest[0:1, j * block_len : (j + 1) * block_len]
            extra = jnp.where(sub_one == j, wide(piece), extra)
        lower = jnp.concatenate([body, extra], axis=1)
        message[d] = jnp.concatenate([rim[...], lower], axis=0).astype(BF16)
        return carry

    lax.fori_loop(0, peers, one, 0, unroll=4)


def contact_products(pairs, live_count, x8, y8, held):
    y8[...] = jnp.zeros_like(y8)
    for h in range(held.shape[0]):
        a, b = pairs[0, h], pairs[1, h]
        delta = x8[a] - x8[b]
        delta = jnp.where(h < live_count, delta, 0.0)
        coarse = delta.astype(jnp.bfloat16).astype(F32)
        both = jnp.concatenate([coarse, delta - coarse], axis=0).astype(jnp.bfloat16)
        product = jnp.dot(both, held[h], preferred_element_type=F32)
        y = product[0:8] + product[8:16]
        y8[a] = y8[a] + y
        y8[b] = y8[b] - y


def wide(row):
    return jnp.broadcast_to(row, (8, row.shape[1]))


def contact_dot(x8, y8):
    value = x8[0] * y8[0]
    for p in range(1, x8.shape[0]):
        value = value + x8[p] * y8[p]
    return total(value[0:1])


def owner_kernel(
    pairs, live, got, hessian, message, held, own, known, x8, y8, z8, f8, tiles, corr
):
    peers, _, _ = got.shape
    width = x8.shape[2]
    block_len = width // 3
    for d in range(peers):
        tiles[d] = got[d].astype(F32)

    def one(d, carry):
        energy, sums = carry
        before, after = around(d, peers)
        diff = tiles[d, 0:8, 0:width] - across(
            tiles[before, 0:8, 0:width], tiles[after, 0:8, 0:width]
        )
        fix = rim_coefs(tiles, d) * diff
        corr[d] = fix
        body, extra = tiles[d, 8:16, 0:width], tiles[d, 8:16, width:]
        line = extra[4:5, :]
        rest = [body[6:7], body[7:8], jnp.concatenate([extra[j : j + 1] for j in range(3)], axis=1)]
        for c in range(CAP):
            p = d * CAP + c
            x8[p] = wide(body[c : c + 1])
            value = body[CAP + c : CAP + c + 1] + rest[c]
            f8[p] = wide(value + chosen(pick(line, CODE_LANE + c), fix))
        return energy + fix * diff, sums + line

    zero = jnp.zeros((8, width), F32)
    energy, sums = lax.fori_loop(0, peers, one, (zero, jnp.zeros((1, block_len), F32)), unroll=4)
    known[...] = line_of(
        [pick_packed(sums, 0), pick_packed(sums, 1) + 0.5 * total(energy)], known.shape[1]
    )
    own[...] = corr[lax.axis_index("gx")]

    contact_products(pairs, live[0, live.shape[1] - 1], x8, y8, hessian)
    line = line_of([contact_dot(x8, y8)], width)
    for p in range(x8.shape[0]):
        x8[p] = f8[p] + y8[p]
    contact_products(pairs, live[0, live.shape[1] - 1], x8, z8, hessian)
    sub = iota((8, width), 0)
    for d in range(peers):
        tile = jnp.where(sub == SUMS_TWO, wide(line), 0.0)
        kept = tiles[d, 8:16, 0:width]
        for c in range(CAP):
            tile = jnp.where(sub == c, y8[d * CAP + c], tile)
            tile = jnp.where(sub == CAP + c, z8[d * CAP + c], tile)
            kept = jnp.where(sub == CAP + c, x8[d * CAP + c], kept)
        message[d] = tile
        held[d] = kept


def middle_kernel(
    send, got2, own, known1, b, loc, mass, stiff, message, v1, v2, known, cb, cv1, panels, common, stage
):
    rows, peers = b.shape[1], message.shape[0]
    col_blocks, block_len = panels.shape[1], panels.shape[3]
    scatter_blocks(send, got2, [cb, cv1])
    ky = masked_ky(stiff)
    rr0 = pick(known1[...], 0)
    alpha0 = rr0 / (pick(known1[...], 1) + pick(line_sum(got2, SUMS_TWO), 0))
    known[...] = line_of([rr0, alpha0], known.shape[1])
    sums = None
    for e in range(3):
        v1[e] = loc[e] + from_panels(cb, e)
        for side, row in enumerate((0, rows - 1)):
            v1[e, row : row + 1, :] = v1[e, row : row + 1, :] + rim_row(own[...], side, e)
        image = v1[e]
        inner = inner_apply(image, mass[...], stiff[0], ky)
        to_panels(panels, e, inner)
        second = inner + from_panels(cv1, e)
        v2[e] = second
        right = b[e]
        r1 = right - alpha0 * image
        w = image - alpha0 * second
        terms = [r1 * r1, r1 * w, r1 * image, right * w, right * image, w * w, w * image, image * image]
        sums = terms if sums is None else [s + t for s, t in zip(sums, terms)]
    write_rim(common.at[0], v1)
    write_rim(common.at[1], v2)
    line = packed_line([total(s) for s in sums])
    line = jnp.broadcast_to(line, (16, block_len))
    sub = iota((16, block_len), 0)

    def one(d, carry):
        for c in range(CAP):
            row, col = place_of(send, d * CAP + c, col_blocks)
            for e in range(3):
                stage[d, c * 3 + e : c * 3 + e + 1, :] = panels[e, col, pl.ds(row, 1), :]
        extra = jnp.where(sub < 9, stage[d], jnp.where(sub == 9, line, 0.0))
        rims = jnp.concatenate([common[0], common[1]], axis=0)
        message[d] = jnp.concatenate([rims, extra], axis=1).astype(BF16)
        return carry

    lax.fori_loop(0, peers, one, 0, unroll=4)


def coefficients(known, sums, b_x, v1_x, v2_x, x_x):
    rr0, alpha0 = pick(known, 0), pick(known, 1)
    rr1, r1w, r1v1, bw, bv1, ww, wv1, v1v1 = [pick_packed(sums, k) for k in range(8)]
    r1w = r1w - alpha0 * (b_x - alpha0 * v1_x)
    bw = bw - alpha0 * b_x
    ww = ww - 2.0 * alpha0 * (v1_x - alpha0 * v2_x) + alpha0 * alpha0 * x_x
    wv1 = wv1 - alpha0 * v1_x
    beta0 = rr1 / rr0
    alpha1 = rr1 / (r1w + beta0 * (r1v1 + bw) + beta0 * beta0 * bv1)
    image_sq = ww + 2.0 * beta0 * wv1 + beta0 * beta0 * v1v1
    rr2 = rr1 - 2.0 * alpha1 * (r1w + beta0 * r1v1) + alpha1 * alpha1 * image_sq
    return alpha0, beta0, alpha1, rr2 / rr1


def advance(b, v1, v2, coefs):
    alpha0, beta0, alpha1, beta1 = coefs
    r1 = b - alpha0 * v1
    d1 = r1 + beta0 * b
    r2 = r1 - alpha1 * (v1 - alpha0 * v2 + beta0 * v1)
    return d1, r2, r2 + beta1 * d1


def last_kernel(
    pairs, live, got1, got3, held, sent2, known, b, v1, v2, mass, stiff, hessian,
    message, part, r2_out, d2_out, dd2, x8, y8, tiles1, tiles3, corr, rim,
):
    peers = got1.shape[0]
    width = x8.shape[2]
    rows = b.shape[1]
    for d in range(peers):
        tiles1[d] = got1[d].astype(F32)
        tiles3[d] = got3[d].astype(F32)

    def one(d, carry):
        before, after = around(d, peers)
        first = tiles3[d, 0:8, 0:width]
        fix = rim_coefs(tiles1, d) * (
            first - across(tiles3[before, 0:8, 0:width], tiles3[after, 0:8, 0:width])
        )
        corr[d] = fix
        others = [tiles1[d, 0:8, 0:width], first, tiles3[d, 8:16, 0:width], fix]
        return (
            *[kept + other * fix for kept, other in zip(carry, others)],
            carry[4] + tiles3[d, 9:10, width:],
        )

    zero = jnp.zeros((8, width), F32)
    *crossing, sums = lax.fori_loop(
        0, peers, one, (zero, zero, zero, zero, jnp.zeros((1, 128), F32)), unroll=4
    )
    coefs = coefficients(known[...], sums, *[total(value) for value in crossing])

    def two(d, carry):
        extra, line = tiles3[d, 0:16, width:], tiles1[d, 12:13, width:]
        fix = corr[d]
        kept, sent = held[d], sent2[d]
        for c in range(CAP):
            value = jnp.concatenate([extra[c * 3 + e : c * 3 + e + 1] for e in range(3)], axis=1)
            value = value + chosen(pick(line, CODE_LANE + c), fix) + sent[CAP + c : CAP + c + 1]
            x8[d * CAP + c] = wide(
                advance(kept[c : c + 1], kept[CAP + c : CAP + c + 1], value, coefs)[2]
            )
        return carry

    lax.fori_loop(0, peers, two, 0, unroll=4)

    me = lax.axis_index("gx")
    before, after = around(me, peers)
    ky = masked_ky(stiff)
    mine = corr[me] * (coefs[0] * coefs[2])
    for e in range(3):
        d1, r2, d2 = advance(b[e], v1[e], v2[e], coefs)
        part[e] = coefs[0] * b[e] + coefs[2] * d1
        r2_out[e] = r2
        d2_out[e] = d2
        for side, row in enumerate((0, rows - 1)):
            r2_out[e, row : row + 1, :] = r2_out[e, row : row + 1, :] + rim_row(mine, side, e)
            d2_out[e, row : row + 1, :] = d2_out[e, row : row + 1, :] + rim_row(mine, side, e)
    write_rim(rim, d2_out)

    def rim_direction(d):
        return advance(
            tiles1[d, 0:8, 0:width],
            tiles3[d, 0:8, 0:width],
            tiles3[d, 8:16, 0:width] + corr[d],
            coefs,
        )[2]

    fix = rim_coefs(tiles1, me) * (rim[...] - across(rim_direction(before), rim_direction(after)))
    sq = dot = None
    for e in range(3):
        r2, d2 = r2_out[e], d2_out[e]
        dd2[e] = inner_apply(d2, mass[...], stiff[0], ky)
        for side, row in enumerate((0, rows - 1)):
            dd2[e, row : row + 1, :] = dd2[e, row : row + 1, :] + rim_row(fix, side, e)
        sq = r2 * r2 if sq is None else sq + r2 * r2
        dot = d2 * dd2[e] if dot is None else dot + d2 * dd2[e]
    rr2, dad2 = total(sq), total(dot)

    contact_products(pairs, live[0, live.shape[1] - 1], x8, y8, hessian)
    line = line_of([rr2, dad2 + contact_dot(x8, y8)], width)
    for d in range(peers):
        for c in range(CAP):
            message[d, c : c + 1, :] = y8[d * CAP + c, 0:1, :]
    put_line(message, SUMS_ONE, line)


def finish_kernel(send, got4, part, r2, d2, dd2, solution, residual, cd2):
    scatter_blocks(send, got4, [cd2])
    sums = line_sum(got4, SUMS_ONE)
    alpha2 = pick(sums, 0) / pick(sums, 1)
    for e in range(3):
        solution[e] = part[e] + alpha2 * d2[e]
        residual[e] = r2[e] - alpha2 * (dd2[e] + from_panels(cd2, e))


def call(kernel, spaces, outs, scratch=(), mebibytes=16, name=None):
    kinds = {"s": pltpu.SMEM, "v": pltpu.VMEM, "a": pl.ANY}
    return pl.pallas_call(
        kernel,
        out_shape=tuple(jax.ShapeDtypeStruct(shape, kind) for shape, kind in outs),
        in_specs=[pl.BlockSpec(memory_space=kinds[k]) for k in spaces],
        out_specs=tuple(pl.BlockSpec(memory_space=pltpu.VMEM) for _ in outs),
        scratch_shapes=[pltpu.VMEM(shape, F32) for shape in scratch],
        compiler_params=pltpu.CompilerParams(vmem_limit_bytes=mebibytes * 2**20),
        name=name,
    )


def per_device(right_side, masses, stiffness, hessian, send_list, pair_refs, counts):
    _, row_count, col_count = right_side.shape
    width = hessian.shape[1]
    block_len = width // 3
    peers = lax.axis_size("gx")
    assert send_list.shape[1] == peers * CAP and col_count == 4 * block_len and block_len == 128
    field = (right_side.shape, F32)
    two, one = ((peers, 8, width), F32), ((peers, 4, width), F32)
    full = ((peers, 16, 4 * block_len), BF16)
    panels = (3, 4, row_count, block_len)
    tiles, wide_tiles, rims = (peers * CAP, 8, width), (peers, 16, 4 * block_len), (peers, 8, width)
    line = ((1, 128), F32)

    routes = jnp.concatenate([send_list, counts.reshape(1, 1)], axis=1)
    pair_refs = pair_refs.T

    def swap(message):
        return lax.all_to_all(message, "gx", split_axis=0, concat_axis=0, tiled=True)

    (token,) = call(announce_kernel, "a", [line], [], 56, name="announce")(hessian)
    sent1, loc = call(
        start_kernel,
        "asvvv",
        [full, field],
        [panels, panels, (8, 4 * block_len), rims],
        name="start",
    )(token, routes, right_side, masses, stiffness)
    got1 = swap(sent1)
    sent2, held, own, known1 = call(
        owner_kernel,
        "ssvv",
        [two, two, ((8, width), F32), line],
        [tiles, tiles, tiles, tiles, wide_tiles, rims],
        32,
        name="owner",
    )(pair_refs, routes, got1, hessian)
    got2 = swap(sent2)
    sent3, v1, v2, known = call(
        middle_kernel,
        "svvvvvvv",
        [full, field, field, line],
        [panels, panels, panels, (2, 8, width), (peers, 16, block_len)],
        name="middle",
    )(routes, got2, own, known1, right_side, loc, masses, stiffness)
    got3 = swap(sent3)
    sent4, part, r2, d2, dd2 = call(
        last_kernel,
        "ssvvvvvvvvvvv",
        [one, field, field, field, field],
        [tiles, tiles, wide_tiles, wide_tiles, rims, (8, width)],
        32,
        name="last",
    )(
        pair_refs, routes, got1, got3, held, sent2, known, right_side, v1, v2, masses, stiffness,
        hessian,
    )
    got4 = swap(sent4)
    return call(finish_kernel, "svvvvv", [field, field], [panels], name="finish")(
        routes, got4, part, r2, d2, dd2
    )


def solution(mesh):
    placed = (
        P(None, ("groups", "gx"), None),
        P(("groups", "gx"), None),
        P(None, ("groups", "gx"), None),
        P(("groups", "gx"), None, None),
        P(("groups", "gx"), None),
        P(("groups", "gx"), None),
        P(("groups", "gx")),
    )
    return jax.shard_map(
        per_device,
        mesh=mesh,
        in_specs=placed,
        out_specs=(P(None, ("groups", "gx"), None), P(None, ("groups", "gx"), None)),
        check_vma=False,
    )
```

```python
import jax
import jax.numpy as jnp
from jax import lax
from jax.experimental import pallas as pl
from jax.experimental.pallas import tpu as pltpu
from jax.sharding import PartitionSpec as P

F32 = jnp.float32
BF16 = jnp.bfloat16
CAP = 3
SUMS_TWO, SUMS_ONE = 2 * CAP, CAP
CODE_LANE = 64


def iota(shape, dim):
    return lax.broadcasted_iota(jnp.int32, shape, dim)


def total(value):
    return jnp.sum(jnp.sum(value, axis=0, keepdims=True), axis=1, keepdims=True)


def line_of(scalars, width):
    lanes = iota((1, width), 1)
    line = jnp.zeros((1, width), F32)
    for k, value in enumerate(scalars):
        line = jnp.where(lanes == k, value, line)
    return line


def line_sum(message, row):
    peers = message.shape[0]
    parts = [message[d, row : row + 1, 0:128] for d in range(peers)]
    while len(parts) > 1:
        parts = [a + b for a, b in zip(parts[::2], parts[1::2])] + (
            parts[-1:] if len(parts) % 2 else []
        )
    return parts[0]


def pick(line, k):
    return line[:, k : k + 1]


def place_of(send, position, col_blocks):
    block = send[0, position]
    return lax.div(block, jnp.int32(col_blocks)), lax.rem(block, jnp.int32(col_blocks))


def scatter_blocks(send, message, panels):
    peers = message.shape[0]
    _, col_blocks, _, block_len = panels[0].shape
    for field in panels:
        field[...] = jnp.zeros_like(field)

    def one(d, carry):
        for c in range(CAP):
            row, col = place_of(send, d * CAP + c, col_blocks)
            for f, field in enumerate(panels):
                for e in range(3):
                    field[e, col, pl.ds(row, 1), :] = message[
                        d, f * CAP + c : f * CAP + c + 1, e * block_len : (e + 1) * block_len
                    ]
        return carry

    lax.fori_loop(0, peers, one, 0, unroll=4)


def to_panels(panels, e, value):
    _, col_blocks, _, block_len = panels.shape
    for q in range(col_blocks):
        panels[e, q] = value[:, q * block_len : (q + 1) * block_len]


def from_panels(panels, e):
    return jnp.concatenate([panels[e, q] for q in range(panels.shape[1])], axis=1)


def put_line(message, row, line):
    for d in range(message.shape[0]):
        message[d, row : row + 1, :] = line


def inner_apply(v, mass, kx, ky):
    rows, cols = v.shape
    row_ids = iota((rows, cols), 0)
    flux_x = jnp.where(row_ids == rows - 1, 0.0, kx * (v - pltpu.roll(v, rows - 1, 0)))
    flux_y = ky * (v - pltpu.roll(v, cols - 1, 1))
    return mass * v + (flux_x - pltpu.roll(flux_x, 1, 0)) + (flux_y - pltpu.roll(flux_y, 1, 1))


def masked_ky(stiff):
    ky = stiff[1]
    return jnp.where(iota(ky.shape, 1) == ky.shape[1] - 1, 0.0, ky)


def rounded(value):
    return value.astype(BF16).astype(F32)


def packed_line(scalars):
    parts = []
    for value in scalars:
        high = rounded(value)
        middle = rounded(value - high)
        parts += [high, middle, value - high - middle]
    return line_of(parts, 128)


def pick_packed(line, k):
    return pick(line, 3 * k) + pick(line, 3 * k + 1) + pick(line, 3 * k + 2)


def thrice(tile):
    return jnp.concatenate([tile] * 3, axis=1)


def write_rim(target, field):
    rows, block_len = field.shape[1], 128
    col_blocks = field.shape[2] // block_len
    for side, row in enumerate((0, rows - 1)):
        for q in range(col_blocks):
            for e in range(3):
                line = side * col_blocks + q
                target[line : line + 1, e * block_len : (e + 1) * block_len] = field[
                    e, row : row + 1, q * block_len : (q + 1) * block_len
                ]


def rim_row(tile, side, e):
    block_len = tile.shape[1] // 3
    half = tile.shape[0] // 2
    return jnp.concatenate(
        [
            tile[side * half + q : side * half + q + 1, e * block_len : (e + 1) * block_len]
            for q in range(half)
        ],
        axis=1,
    )


def across(before, after):
    half = before.shape[0] // 2
    return pltpu.roll(jnp.where(iota(before.shape, 0) >= half, before, after), half, 0)


def around(d, peers):
    return jnp.maximum(d - 1, 0), jnp.minimum(d + 1, peers - 1)


def unpack_first(got, tiles, edges):
    sub = iota(edges.shape[1:], 0)
    for d in range(got.shape[0]):
        tile = got[d].astype(F32)
        tiles[d] = tile
        kx = jnp.where(sub % 4 == 3, wide(tile[15:16, 0:128]), 0.0)
        for q in range(3):
            kx = jnp.where(sub % 4 == q, wide(tile[14:15, q * 128 : (q + 1) * 128]), kx)
        edges[d] = kx


def rim_coefs(edges, d):
    before, _ = around(d, edges.shape[0])
    here, other = edges[d], edges[before]
    other = jnp.where(d > 0, other, 0.0)
    return thrice(jnp.where(iota(here.shape, 0) < 4, other, here))


def chosen(code, tile):
    return jnp.sum(
        jnp.where(iota(tile.shape, 0).astype(F32) == code, tile, 0.0), axis=0, keepdims=True
    )


def announce_kernel(hessian, token):
    token[...] = jnp.zeros_like(token)


def start_kernel(_, send, b, mass, stiff, message, loc, b_panels, loc_panels, rim, stage):
    rows, peers = b.shape[1], message.shape[0]
    col_blocks, block_len = b_panels.shape[1], b_panels.shape[3]
    ky = masked_ky(stiff)
    sq = dot = None
    for e in range(3):
        v = b[e]
        image = inner_apply(v, mass[...], stiff[0], ky)
        loc[e] = image
        to_panels(b_panels, e, v)
        to_panels(loc_panels, e, image)
        sq = v * v if sq is None else sq + v * v
        dot = v * image if dot is None else dot + v * image
    write_rim(rim, b)
    ends = lax.axis_index("gx") == peers - 1
    kx = jnp.where(ends, 0.0, stiff[0, rows - 1 : rows, :])
    line = packed_line([total(sq), total(dot)])
    lanes, sub = iota((1, 128), 1), iota((8, 3 * block_len), 0)

    def one(d, carry):
        own_line = line
        for c in range(CAP):
            row, col = place_of(send, d * CAP + c, col_blocks)
            code = jnp.where(row == 0, col, jnp.where(row == rows - 1, col_blocks + col, 99))
            own_line = jnp.where(lanes == CODE_LANE + c, code.astype(F32), own_line)
            for e in range(3):
                span = slice(e * block_len, (e + 1) * block_len)
                stage[d, c : c + 1, span] = b_panels[e, col, pl.ds(row, 1), :]
                stage[d, CAP + c : CAP + c + 1, span] = loc_panels[e, col, pl.ds(row, 1), :]
        tail = jnp.concatenate([kx[:, 3 * block_len :], own_line, jnp.zeros_like(own_line)], axis=1)
        lower = jnp.where(sub == 2 * CAP, wide(kx[:, : 3 * block_len]), stage[d])
        lower = jnp.where(sub == 2 * CAP + 1, wide(tail), lower)
        message[d] = jnp.concatenate([rim[...], lower], axis=0).astype(BF16)
        return carry

    lax.fori_loop(0, peers, one, 0, unroll=4)


def contact_products(pairs, live_count, x8, y8, held):
    y8[...] = jnp.zeros_like(y8)
    for h in range(held.shape[0]):
        a, b = pairs[0, h], pairs[1, h]
        delta = x8[a] - x8[b]
        delta = jnp.where(h < live_count, delta, 0.0)
        coarse = delta.astype(jnp.bfloat16).astype(F32)
        both = jnp.concatenate([coarse, delta - coarse], axis=0).astype(jnp.bfloat16)
        product = jnp.dot(both, held[h], preferred_element_type=F32)
        y = product[0:8] + product[8:16]
        y8[a] = y8[a] + y
        y8[b] = y8[b] - y


def wide(row):
    return jnp.broadcast_to(row, (8, row.shape[1]))


def contact_dot(x8, y8):
    value = x8[0] * y8[0]
    for p in range(1, x8.shape[0]):
        value = value + x8[p] * y8[p]
    return total(value[0:1])


def owner_kernel(
    pairs, live, got, hessian, message, held, own, known, x8, y8, z8, f8, tiles, corr, edges
):
    peers, _, _ = got.shape
    width = x8.shape[2]
    block_len = width // 3
    unpack_first(got, tiles, edges)

    def one(d, carry):
        energy, sums = carry
        before, after = around(d, peers)
        diff = tiles[d, 0:8, 0:width] - across(
            tiles[before, 0:8, 0:width], tiles[after, 0:8, 0:width]
        )
        fix = rim_coefs(edges, d) * diff
        corr[d] = fix
        body, line = tiles[d, 8:16, 0:width], tiles[d, 15:16, block_len : 2 * block_len]
        for c in range(CAP):
            p = d * CAP + c
            x8[p] = wide(body[c : c + 1])
            f8[p] = wide(body[CAP + c : CAP + c + 1] + chosen(pick(line, CODE_LANE + c), fix))
        return energy + fix * diff, sums + line

    zero = jnp.zeros((8, width), F32)
    energy, sums = lax.fori_loop(0, peers, one, (zero, jnp.zeros((1, block_len), F32)), unroll=4)
    known[...] = line_of(
        [pick_packed(sums, 0), pick_packed(sums, 1) + 0.5 * total(energy)], known.shape[1]
    )
    own[...] = corr[lax.axis_index("gx")]

    contact_products(pairs, live[0, live.shape[1] - 1], x8, y8, hessian)
    line = packed_line([contact_dot(x8, y8)])
    line = jnp.concatenate([line, jnp.zeros((1, width - block_len), F32)], axis=1)
    for p in range(x8.shape[0]):
        x8[p] = f8[p] + rounded(y8[p])
    contact_products(pairs, live[0, live.shape[1] - 1], x8, z8, hessian)
    sub = iota((8, width), 0)
    for d in range(peers):
        tile = jnp.where(sub == SUMS_TWO, wide(line), 0.0)
        kept = tiles[d, 8:16, 0:width]
        for c in range(CAP):
            tile = jnp.where(sub == c, y8[d * CAP + c], tile)
            tile = jnp.where(sub == CAP + c, z8[d * CAP + c], tile)
            kept = jnp.where(sub == CAP + c, x8[d * CAP + c], kept)
        message[d] = tile.astype(BF16)
        held[d] = kept


def middle_kernel(
    send, got2, own, known1, b, loc, mass, stiff, message, v1, v2, known, cb, cv1, panels, common, stage, back
):
    rows, peers = b.shape[1], message.shape[0]
    col_blocks, block_len = panels.shape[1], panels.shape[3]
    for d in range(peers):
        back[d] = got2[d].astype(F32)
    scatter_blocks(send, back, [cb, cv1])
    ky = masked_ky(stiff)
    rr0 = pick(known1[...], 0)
    alpha0 = rr0 / (pick(known1[...], 1) + pick_packed(line_sum(back, SUMS_TWO), 0))
    known[...] = line_of([rr0, alpha0], known.shape[1])
    sums = None
    for e in range(3):
        v1[e] = loc[e] + from_panels(cb, e)
        for side, row in enumerate((0, rows - 1)):
            v1[e, row : row + 1, :] = v1[e, row : row + 1, :] + rim_row(own[...], side, e)
        image = v1[e]
        inner = inner_apply(image, mass[...], stiff[0], ky)
        to_panels(panels, e, inner)
        second = inner + from_panels(cv1, e)
        v2[e] = second
        right = b[e]
        r1 = right - alpha0 * image
        w = image - alpha0 * second
        terms = [r1 * r1, r1 * w, r1 * image, right * w, right * image, w * w, w * image, image * image]
        sums = terms if sums is None else [s + t for s, t in zip(sums, terms)]
    write_rim(common.at[0], v1)
    write_rim(common.at[1], v2)
    line = packed_line([total(s) for s in sums])
    line = jnp.broadcast_to(line, (16, block_len))
    sub = iota((16, block_len), 0)

    def one(d, carry):
        for c in range(CAP):
            row, col = place_of(send, d * CAP + c, col_blocks)
            for e in range(3):
                stage[d, c * 3 + e : c * 3 + e + 1, :] = panels[e, col, pl.ds(row, 1), :]
        extra = jnp.where(sub < 9, stage[d], jnp.where(sub == 9, line, 0.0))
        rims = jnp.concatenate([common[0], common[1]], axis=0)
        message[d] = jnp.concatenate([rims, extra], axis=1).astype(BF16)
        return carry

    lax.fori_loop(0, peers, one, 0, unroll=4)


def coefficients(known, sums, b_x, v1_x, v2_x, x_x):
    rr0, alpha0 = pick(known, 0), pick(known, 1)
    rr1, r1w, r1v1, bw, bv1, ww, wv1, v1v1 = [pick_packed(sums, k) for k in range(8)]
    r1w = r1w - alpha0 * (b_x - alpha0 * v1_x)
    bw = bw - alpha0 * b_x
    ww = ww - 2.0 * alpha0 * (v1_x - alpha0 * v2_x) + alpha0 * alpha0 * x_x
    wv1 = wv1 - alpha0 * v1_x
    beta0 = rr1 / rr0
    alpha1 = rr1 / (r1w + beta0 * (r1v1 + bw) + beta0 * beta0 * bv1)
    image_sq = ww + 2.0 * beta0 * wv1 + beta0 * beta0 * v1v1
    rr2 = rr1 - 2.0 * alpha1 * (r1w + beta0 * r1v1) + alpha1 * alpha1 * image_sq
    return alpha0, beta0, alpha1, rr2 / rr1


def advance(b, v1, v2, coefs):
    alpha0, beta0, alpha1, beta1 = coefs
    r1 = b - alpha0 * v1
    d1 = r1 + beta0 * b
    r2 = r1 - alpha1 * (v1 - alpha0 * v2 + beta0 * v1)
    return d1, r2, r2 + beta1 * d1


def last_kernel(
    pairs, live, got1, got3, held, sent2, known, b, v1, v2, mass, stiff, hessian,
    message, part, r2_out, d2_out, dd2, x8, y8, tiles1, tiles3, corr, rim, edges,
):
    peers = got1.shape[0]
    width = x8.shape[2]
    rows = b.shape[1]
    unpack_first(got1, tiles1, edges)
    for d in range(peers):
        tiles3[d] = got3[d].astype(F32)

    def one(d, carry):
        before, after = around(d, peers)
        first = tiles3[d, 0:8, 0:width]
        fix = rim_coefs(edges, d) * (
            first - across(tiles3[before, 0:8, 0:width], tiles3[after, 0:8, 0:width])
        )
        corr[d] = fix
        others = [tiles1[d, 0:8, 0:width], first, tiles3[d, 8:16, 0:width], fix]
        return (
            *[kept + other * fix for kept, other in zip(carry, others)],
            carry[4] + tiles3[d, 9:10, width:],
        )

    zero = jnp.zeros((8, width), F32)
    *crossing, sums = lax.fori_loop(
        0, peers, one, (zero, zero, zero, zero, jnp.zeros((1, 128), F32)), unroll=4
    )
    coefs = coefficients(known[...], sums, *[total(value) for value in crossing])

    def two(d, carry):
        extra, line = tiles3[d, 0:16, width:], tiles1[d, 15:16, 128:256]
        fix = corr[d]
        kept, sent = held[d], sent2[d].astype(F32)
        for c in range(CAP):
            value = jnp.concatenate([extra[c * 3 + e : c * 3 + e + 1] for e in range(3)], axis=1)
            value = value + chosen(pick(line, CODE_LANE + c), fix) + sent[CAP + c : CAP + c + 1]
            x8[d * CAP + c] = wide(
                advance(kept[c : c + 1], kept[CAP + c : CAP + c + 1], value, coefs)[2]
            )
        return carry

    lax.fori_loop(0, peers, two, 0, unroll=4)

    me = lax.axis_index("gx")
    before, after = around(me, peers)
    ky = masked_ky(stiff)
    mine = corr[me] * (coefs[0] * coefs[2])
    for e in range(3):
        d1, r2, d2 = advance(b[e], v1[e], v2[e], coefs)
        part[e] = coefs[0] * b[e] + coefs[2] * d1
        r2_out[e] = r2
        d2_out[e] = d2
        for side, row in enumerate((0, rows - 1)):
            r2_out[e, row : row + 1, :] = r2_out[e, row : row + 1, :] + rim_row(mine, side, e)
            d2_out[e, row : row + 1, :] = d2_out[e, row : row + 1, :] + rim_row(mine, side, e)
    write_rim(rim, d2_out)

    def rim_direction(d):
        return advance(
            tiles1[d, 0:8, 0:width],
            tiles3[d, 0:8, 0:width],
            tiles3[d, 8:16, 0:width] + corr[d],
            coefs,
        )[2]

    fix = rim_coefs(edges, me) * (rim[...] - across(rim_direction(before), rim_direction(after)))
    sq = dot = None
    for e in range(3):
        r2, d2 = r2_out[e], d2_out[e]
        dd2[e] = inner_apply(d2, mass[...], stiff[0], ky)
        for side, row in enumerate((0, rows - 1)):
            dd2[e, row : row + 1, :] = dd2[e, row : row + 1, :] + rim_row(fix, side, e)
        sq = r2 * r2 if sq is None else sq + r2 * r2
        dot = d2 * dd2[e] if dot is None else dot + d2 * dd2[e]
    rr2, dad2 = total(sq), total(dot)

    contact_products(pairs, live[0, live.shape[1] - 1], x8, y8, hessian)
    line = packed_line([rr2, dad2 + contact_dot(x8, y8)])
    line = jnp.concatenate([line, jnp.zeros((1, width - 128), F32)], axis=1)
    for d in range(peers):
        rows = [y8[d * CAP + c, 0:1, :] for c in range(CAP)]
        message[d] = jnp.concatenate([*rows, line], axis=0).astype(BF16)


def finish_kernel(send, got4, part, r2, d2, dd2, solution, residual, cd2, back):
    for d in range(got4.shape[0]):
        back[d] = got4[d].astype(F32)
    scatter_blocks(send, back, [cd2])
    sums = line_sum(back, SUMS_ONE)
    alpha2 = pick_packed(sums, 0) / pick_packed(sums, 1)
    for e in range(3):
        solution[e] = part[e] + alpha2 * d2[e]
        residual[e] = r2[e] - alpha2 * (dd2[e] + from_panels(cd2, e))


def call(kernel, spaces, outs, scratch=(), mebibytes=16, name=None):
    kinds = {"s": pltpu.SMEM, "v": pltpu.VMEM, "a": pl.ANY}
    return pl.pallas_call(
        kernel,
        out_shape=tuple(jax.ShapeDtypeStruct(shape, kind) for shape, kind in outs),
        in_specs=[pl.BlockSpec(memory_space=kinds[k]) for k in spaces],
        out_specs=tuple(pl.BlockSpec(memory_space=pltpu.VMEM) for _ in outs),
        scratch_shapes=[pltpu.VMEM(shape, F32) for shape in scratch],
        compiler_params=pltpu.CompilerParams(vmem_limit_bytes=mebibytes * 2**20),
        name=name,
    )


def per_device(right_side, masses, stiffness, hessian, send_list, pair_refs, counts):
    _, row_count, col_count = right_side.shape
    width = hessian.shape[1]
    block_len = width // 3
    peers = lax.axis_size("gx")
    assert send_list.shape[1] == peers * CAP and col_count == 4 * block_len and block_len == 128
    field = (right_side.shape, F32)
    first, second = ((peers, 16, width), BF16), ((peers, 8, width), BF16)
    third, fourth = ((peers, 16, 4 * block_len), BF16), ((peers, 4, width), BF16)
    held_shape, edges = ((peers, 8, width), F32), (peers, 8, block_len)
    panels = (3, 4, row_count, block_len)
    tiles, wide_tiles, rims = (peers * CAP, 8, width), (peers, 16, 4 * block_len), (peers, 8, width)
    line = ((1, 128), F32)

    routes = jnp.concatenate([send_list, counts.reshape(1, 1)], axis=1)
    pair_refs = pair_refs.T

    def swap(message):
        return lax.all_to_all(message, "gx", split_axis=0, concat_axis=0, tiled=True)

    (token,) = call(announce_kernel, "a", [line], [], 56, name="announce")(hessian)
    sent1, loc = call(
        start_kernel,
        "asvvv",
        [first, field],
        [panels, panels, (8, width), rims],
        name="start",
    )(token, routes, right_side, masses, stiffness)
    got1 = swap(sent1)
    sent2, held, own, known1 = call(
        owner_kernel,
        "ssvv",
        [second, held_shape, ((8, width), F32), line],
        [tiles, tiles, tiles, tiles, (peers, 16, width), rims, edges],
        32,
        name="owner",
    )(pair_refs, routes, got1, hessian)
    got2 = swap(sent2)
    sent3, v1, v2, known = call(
        middle_kernel,
        "svvvvvvv",
        [third, field, field, line],
        [panels, panels, panels, (2, 8, width), (peers, 16, block_len), rims],
        name="middle",
    )(routes, got2, own, known1, right_side, loc, masses, stiffness)
    got3 = swap(sent3)
    sent4, part, r2, d2, dd2 = call(
        last_kernel,
        "ssvvvvvvvvvvv",
        [fourth, field, field, field, field],
        [tiles, tiles, (peers, 16, width), wide_tiles, rims, (8, width), edges],
        32,
        name="last",
    )(
        pair_refs, routes, got1, got3, held, sent2, known, right_side, v1, v2, masses, stiffness,
        hessian,
    )
    got4 = swap(sent4)
    return call(finish_kernel, "svvvvv", [field, field], [panels, (peers, 4, width)], name="finish")(
        routes, got4, part, r2, d2, dd2
    )


def solution(mesh):
    placed = (
        P(None, ("groups", "gx"), None),
        P(("groups", "gx"), None),
        P(None, ("groups", "gx"), None),
        P(("groups", "gx"), None, None),
        P(("groups", "gx"), None),
        P(("groups", "gx"), None),
        P(("groups", "gx")),
    )
    return jax.shard_map(
        per_device,
        mesh=mesh,
        in_specs=placed,
        out_specs=(P(None, ("groups", "gx"), None), P(None, ("groups", "gx"), None)),
        check_vma=False,
    )
```

```python
import jax
import jax.numpy as jnp
from jax import lax
from jax.experimental import pallas as pl
from jax.experimental.pallas import tpu as pltpu
from jax.sharding import PartitionSpec as P

F32 = jnp.float32
BF16 = jnp.bfloat16
CAP = 3
SUMS_TWO, SUMS_ONE = 2 * CAP, CAP
CODE_LANE = 64


def iota(shape, dim):
    return lax.broadcasted_iota(jnp.int32, shape, dim)


def total(value):
    return jnp.sum(jnp.sum(value, axis=0, keepdims=True), axis=1, keepdims=True)


def line_of(scalars, width):
    lanes = iota((1, width), 1)
    line = jnp.zeros((1, width), F32)
    for k, value in enumerate(scalars):
        line = jnp.where(lanes == k, value, line)
    return line


def line_sum(message, row):
    peers = message.shape[0]
    parts = [message[d, row : row + 1, 0:128] for d in range(peers)]
    while len(parts) > 1:
        parts = [a + b for a, b in zip(parts[::2], parts[1::2])] + (
            parts[-1:] if len(parts) % 2 else []
        )
    return parts[0]


def pick(line, k):
    return line[:, k : k + 1]


def place_of(send, position, col_blocks):
    block = send[0, position]
    return lax.div(block, jnp.int32(col_blocks)), lax.rem(block, jnp.int32(col_blocks))


def scatter_blocks(send, message, panels):
    peers = message.shape[0]
    _, col_blocks, _, block_len = panels[0].shape
    for field in panels:
        field[...] = jnp.zeros_like(field)

    def one(d, carry):
        for c in range(CAP):
            row, col = place_of(send, d * CAP + c, col_blocks)
            for f, field in enumerate(panels):
                for e in range(3):
                    field[e, col, pl.ds(row, 1), :] = message[
                        d, f * CAP + c : f * CAP + c + 1, e * block_len : (e + 1) * block_len
                    ]
        return carry

    lax.fori_loop(0, peers, one, 0, unroll=4)


def to_panels(panels, e, value):
    _, col_blocks, _, block_len = panels.shape
    for q in range(col_blocks):
        panels[e, q] = value[:, q * block_len : (q + 1) * block_len]


def from_panels(panels, e):
    return jnp.concatenate([panels[e, q] for q in range(panels.shape[1])], axis=1)


def put_line(message, row, line):
    for d in range(message.shape[0]):
        message[d, row : row + 1, :] = line


def inner_apply(v, mass, kx, ky):
    rows, cols = v.shape
    row_ids = iota((rows, cols), 0)
    flux_x = jnp.where(row_ids == rows - 1, 0.0, kx * (v - pltpu.roll(v, rows - 1, 0)))
    flux_y = ky * (v - pltpu.roll(v, cols - 1, 1))
    return mass * v + (flux_x - pltpu.roll(flux_x, 1, 0)) + (flux_y - pltpu.roll(flux_y, 1, 1))


def masked_ky(stiff):
    ky = stiff[1]
    return jnp.where(iota(ky.shape, 1) == ky.shape[1] - 1, 0.0, ky)


def rounded(value):
    return value.astype(BF16).astype(F32)


def packed_line(scalars):
    parts = []
    for value in scalars:
        high = rounded(value)
        middle = rounded(value - high)
        parts += [high, middle, value - high - middle]
    return line_of(parts, 128)


def pick_packed(line, k):
    return pick(line, 3 * k) + pick(line, 3 * k + 1) + pick(line, 3 * k + 2)


def thrice(tile):
    return jnp.concatenate([tile] * 3, axis=1)


def write_rim(target, field):
    rows, block_len = field.shape[1], 128
    col_blocks = field.shape[2] // block_len
    for side, row in enumerate((0, rows - 1)):
        for q in range(col_blocks):
            for e in range(3):
                line = side * col_blocks + q
                target[line : line + 1, e * block_len : (e + 1) * block_len] = field[
                    e, row : row + 1, q * block_len : (q + 1) * block_len
                ]


def rim_row(tile, side, e):
    block_len = tile.shape[1] // 3
    half = tile.shape[0] // 2
    return jnp.concatenate(
        [
            tile[side * half + q : side * half + q + 1, e * block_len : (e + 1) * block_len]
            for q in range(half)
        ],
        axis=1,
    )


def across(before, after):
    half = before.shape[0] // 2
    return pltpu.roll(jnp.where(iota(before.shape, 0) >= half, before, after), half, 0)


def around(d, peers):
    return jnp.maximum(d - 1, 0), jnp.minimum(d + 1, peers - 1)


def unpack_first(got, tiles, edges):
    sub = iota(edges.shape[1:], 0)
    for d in range(got.shape[0]):
        tile = got[d].astype(F32)
        tiles[d] = tile
        kx = jnp.where(sub % 4 == 3, wide(tile[15:16, 0:128]), 0.0)
        for q in range(3):
            kx = jnp.where(sub % 4 == q, wide(tile[14:15, q * 128 : (q + 1) * 128]), kx)
        edges[d] = kx


def rim_coefs(edges, d):
    before, _ = around(d, edges.shape[0])
    here, other = edges[d], edges[before]
    other = jnp.where(d > 0, other, 0.0)
    return thrice(jnp.where(iota(here.shape, 0) < 4, other, here))


def chosen(code, tile):
    return jnp.sum(
        jnp.where(iota(tile.shape, 0).astype(F32) == code, tile, 0.0), axis=0, keepdims=True
    )


def announce_kernel(hessian, _, token):
    token[...] = jnp.zeros_like(token)


def start_kernel(_, send, b, mass, stiff, message, loc, b_panels, loc_panels, rim, stage):
    rows, peers = b.shape[1], message.shape[0]
    col_blocks, block_len = b_panels.shape[1], b_panels.shape[3]
    ky = masked_ky(stiff)
    sq = dot = None
    for e in range(3):
        v = b[e]
        image = inner_apply(v, mass[...], stiff[0], ky)
        loc[e] = image
        to_panels(b_panels, e, v)
        to_panels(loc_panels, e, image)
        sq = v * v if sq is None else sq + v * v
        dot = v * image if dot is None else dot + v * image
    write_rim(rim, b)
    ends = lax.axis_index("gx") == peers - 1
    kx = jnp.where(ends, 0.0, stiff[0, rows - 1 : rows, :])
    line = packed_line([total(sq), total(dot)])
    lanes, sub = iota((1, 128), 1), iota((8, 3 * block_len), 0)

    def one(d, carry):
        own_line = line
        for c in range(CAP):
            row, col = place_of(send, d * CAP + c, col_blocks)
            code = jnp.where(row == 0, col, jnp.where(row == rows - 1, col_blocks + col, 99))
            own_line = jnp.where(lanes == CODE_LANE + c, code.astype(F32), own_line)
            for e in range(3):
                span = slice(e * block_len, (e + 1) * block_len)
                stage[d, c : c + 1, span] = b_panels[e, col, pl.ds(row, 1), :]
                stage[d, CAP + c : CAP + c + 1, span] = loc_panels[e, col, pl.ds(row, 1), :]
        tail = jnp.concatenate([kx[:, 3 * block_len :], own_line, jnp.zeros_like(own_line)], axis=1)
        lower = jnp.where(sub == 2 * CAP, wide(kx[:, : 3 * block_len]), stage[d])
        lower = jnp.where(sub == 2 * CAP + 1, wide(tail), lower)
        message[d] = jnp.concatenate([rim[...], lower], axis=0).astype(BF16)
        return carry

    lax.fori_loop(0, peers, one, 0, unroll=4)


def contact_products(pairs, live_count, x8, y8, held):
    y8[...] = jnp.zeros_like(y8)
    for h in range(held.shape[0]):
        a, b = pairs[0, h], pairs[1, h]
        delta = x8[a] - x8[b]
        delta = jnp.where(h < live_count, delta, 0.0)
        coarse = delta.astype(jnp.bfloat16).astype(F32)
        both = jnp.concatenate([coarse, delta - coarse], axis=0).astype(jnp.bfloat16)
        product = jnp.dot(both, held[h], preferred_element_type=F32)
        y = product[0:8] + product[8:16]
        y8[a] = y8[a] + y
        y8[b] = y8[b] - y


def wide(row):
    return jnp.broadcast_to(row, (8, row.shape[1]))


def contact_dot(x8, y8):
    value = x8[0] * y8[0]
    for p in range(1, x8.shape[0]):
        value = value + x8[p] * y8[p]
    return total(value[0:1])


def owner_kernel(
    pairs, live, got, hessian, message, held, own, known, x8, y8, z8, f8, tiles, corr, edges
):
    peers, _, _ = got.shape
    width = x8.shape[2]
    block_len = width // 3
    unpack_first(got, tiles, edges)

    def one(d, carry):
        energy, sums = carry
        before, after = around(d, peers)
        diff = tiles[d, 0:8, 0:width] - across(
            tiles[before, 0:8, 0:width], tiles[after, 0:8, 0:width]
        )
        fix = rim_coefs(edges, d) * diff
        corr[d] = fix
        body, line = tiles[d, 8:16, 0:width], tiles[d, 15:16, block_len : 2 * block_len]
        for c in range(CAP):
            p = d * CAP + c
            x8[p] = wide(body[c : c + 1])
            f8[p] = wide(body[CAP + c : CAP + c + 1] + chosen(pick(line, CODE_LANE + c), fix))
        return energy + fix * diff, sums + line

    zero = jnp.zeros((8, width), F32)
    energy, sums = lax.fori_loop(0, peers, one, (zero, jnp.zeros((1, block_len), F32)), unroll=4)
    known[...] = line_of(
        [pick_packed(sums, 0), pick_packed(sums, 1) + 0.5 * total(energy)], known.shape[1]
    )
    own[...] = corr[lax.axis_index("gx")]

    contact_products(pairs, live[0, live.shape[1] - 1], x8, y8, hessian)
    line = packed_line([contact_dot(x8, y8)])
    line = jnp.concatenate([line, jnp.zeros((1, width - block_len), F32)], axis=1)
    for p in range(x8.shape[0]):
        x8[p] = f8[p] + rounded(y8[p])
    contact_products(pairs, live[0, live.shape[1] - 1], x8, z8, hessian)
    sub = iota((8, width), 0)
    for d in range(peers):
        tile = jnp.where(sub == SUMS_TWO, wide(line), 0.0)
        kept = tiles[d, 8:16, 0:width]
        for c in range(CAP):
            tile = jnp.where(sub == c, y8[d * CAP + c], tile)
            tile = jnp.where(sub == CAP + c, z8[d * CAP + c], tile)
            kept = jnp.where(sub == CAP + c, x8[d * CAP + c], kept)
        message[d] = tile.astype(BF16)
        held[d] = kept


def middle_kernel(
    send, got2, own, known1, b, loc, mass, stiff, message, v1, v2, known, cb, cv1, panels, common, stage, back
):
    rows, peers = b.shape[1], message.shape[0]
    col_blocks, block_len = panels.shape[1], panels.shape[3]
    for d in range(peers):
        back[d] = got2[d].astype(F32)
    scatter_blocks(send, back, [cb, cv1])
    ky = masked_ky(stiff)
    rr0 = pick(known1[...], 0)
    alpha0 = rr0 / (pick(known1[...], 1) + pick_packed(line_sum(back, SUMS_TWO), 0))
    known[...] = line_of([rr0, alpha0], known.shape[1])
    sums = None
    for e in range(3):
        v1[e] = loc[e] + from_panels(cb, e)
        for side, row in enumerate((0, rows - 1)):
            v1[e, row : row + 1, :] = v1[e, row : row + 1, :] + rim_row(own[...], side, e)
        image = v1[e]
        inner = inner_apply(image, mass[...], stiff[0], ky)
        to_panels(panels, e, inner)
        second = inner + from_panels(cv1, e)
        v2[e] = second
        right = b[e]
        r1 = right - alpha0 * image
        w = image - alpha0 * second
        terms = [r1 * r1, r1 * w, r1 * image, right * w, right * image, w * w, w * image, image * image]
        sums = terms if sums is None else [s + t for s, t in zip(sums, terms)]
    write_rim(common.at[0], v1)
    write_rim(common.at[1], v2)
    line = packed_line([total(s) for s in sums])
    line = jnp.broadcast_to(line, (16, block_len))
    sub = iota((16, block_len), 0)

    def one(d, carry):
        for c in range(CAP):
            row, col = place_of(send, d * CAP + c, col_blocks)
            for e in range(3):
                stage[d, c * 3 + e : c * 3 + e + 1, :] = panels[e, col, pl.ds(row, 1), :]
        extra = jnp.where(sub < 9, stage[d], jnp.where(sub == 9, line, 0.0))
        rims = jnp.concatenate([common[0], common[1]], axis=0)
        message[d] = jnp.concatenate([rims, extra], axis=1).astype(BF16)
        return carry

    lax.fori_loop(0, peers, one, 0, unroll=4)


def coefficients(known, sums, b_x, v1_x, v2_x, x_x):
    rr0, alpha0 = pick(known, 0), pick(known, 1)
    rr1, r1w, r1v1, bw, bv1, ww, wv1, v1v1 = [pick_packed(sums, k) for k in range(8)]
    r1w = r1w - alpha0 * (b_x - alpha0 * v1_x)
    bw = bw - alpha0 * b_x
    ww = ww - 2.0 * alpha0 * (v1_x - alpha0 * v2_x) + alpha0 * alpha0 * x_x
    wv1 = wv1 - alpha0 * v1_x
    beta0 = rr1 / rr0
    alpha1 = rr1 / (r1w + beta0 * (r1v1 + bw) + beta0 * beta0 * bv1)
    image_sq = ww + 2.0 * beta0 * wv1 + beta0 * beta0 * v1v1
    rr2 = rr1 - 2.0 * alpha1 * (r1w + beta0 * r1v1) + alpha1 * alpha1 * image_sq
    return alpha0, beta0, alpha1, rr2 / rr1


def advance(b, v1, v2, coefs):
    alpha0, beta0, alpha1, beta1 = coefs
    r1 = b - alpha0 * v1
    d1 = r1 + beta0 * b
    r2 = r1 - alpha1 * (v1 - alpha0 * v2 + beta0 * v1)
    return d1, r2, r2 + beta1 * d1


def last_kernel(
    pairs, live, got1, got3, held, sent2, known, b, v1, v2, mass, stiff, hessian,
    message, part, r2_out, d2_out, dd2, x8, y8, tiles1, tiles3, corr, rim, edges,
):
    peers = got1.shape[0]
    width = x8.shape[2]
    rows = b.shape[1]
    unpack_first(got1, tiles1, edges)
    for d in range(peers):
        tiles3[d] = got3[d].astype(F32)

    def one(d, carry):
        before, after = around(d, peers)
        first = tiles3[d, 0:8, 0:width]
        fix = rim_coefs(edges, d) * (
            first - across(tiles3[before, 0:8, 0:width], tiles3[after, 0:8, 0:width])
        )
        corr[d] = fix
        others = [tiles1[d, 0:8, 0:width], first, tiles3[d, 8:16, 0:width], fix]
        return (
            *[kept + other * fix for kept, other in zip(carry, others)],
            carry[4] + tiles3[d, 9:10, width:],
        )

    zero = jnp.zeros((8, width), F32)
    *crossing, sums = lax.fori_loop(
        0, peers, one, (zero, zero, zero, zero, jnp.zeros((1, 128), F32)), unroll=4
    )
    coefs = coefficients(known[...], sums, *[total(value) for value in crossing])

    def two(d, carry):
        extra, line = tiles3[d, 0:16, width:], tiles1[d, 15:16, 128:256]
        fix = corr[d]
        kept, sent = held[d], sent2[d].astype(F32)
        for c in range(CAP):
            value = jnp.concatenate([extra[c * 3 + e : c * 3 + e + 1] for e in range(3)], axis=1)
            value = value + chosen(pick(line, CODE_LANE + c), fix) + sent[CAP + c : CAP + c + 1]
            x8[d * CAP + c] = wide(
                advance(kept[c : c + 1], kept[CAP + c : CAP + c + 1], value, coefs)[2]
            )
        return carry

    lax.fori_loop(0, peers, two, 0, unroll=4)

    me = lax.axis_index("gx")
    before, after = around(me, peers)
    ky = masked_ky(stiff)
    mine = corr[me] * (coefs[0] * coefs[2])
    for e in range(3):
        d1, r2, d2 = advance(b[e], v1[e], v2[e], coefs)
        part[e] = coefs[0] * b[e] + coefs[2] * d1
        r2_out[e] = r2
        d2_out[e] = d2
        for side, row in enumerate((0, rows - 1)):
            r2_out[e, row : row + 1, :] = r2_out[e, row : row + 1, :] + rim_row(mine, side, e)
            d2_out[e, row : row + 1, :] = d2_out[e, row : row + 1, :] + rim_row(mine, side, e)
    write_rim(rim, d2_out)

    def rim_direction(d):
        return advance(
            tiles1[d, 0:8, 0:width],
            tiles3[d, 0:8, 0:width],
            tiles3[d, 8:16, 0:width] + corr[d],
            coefs,
        )[2]

    fix = rim_coefs(edges, me) * (rim[...] - across(rim_direction(before), rim_direction(after)))
    sq = dot = None
    for e in range(3):
        r2, d2 = r2_out[e], d2_out[e]
        dd2[e] = inner_apply(d2, mass[...], stiff[0], ky)
        for side, row in enumerate((0, rows - 1)):
            dd2[e, row : row + 1, :] = dd2[e, row : row + 1, :] + rim_row(fix, side, e)
        sq = r2 * r2 if sq is None else sq + r2 * r2
        dot = d2 * dd2[e] if dot is None else dot + d2 * dd2[e]
    rr2, dad2 = total(sq), total(dot)

    contact_products(pairs, live[0, live.shape[1] - 1], x8, y8, hessian)
    line = packed_line([rr2, dad2 + contact_dot(x8, y8)])
    line = jnp.concatenate([line, jnp.zeros((1, width - 128), F32)], axis=1)
    for d in range(peers):
        rows = [y8[d * CAP + c, 0:1, :] for c in range(CAP)]
        message[d] = jnp.concatenate([*rows, line], axis=0).astype(BF16)


def finish_kernel(send, got4, part, r2, d2, dd2, solution, residual, cd2, back):
    for d in range(got4.shape[0]):
        back[d] = got4[d].astype(F32)
    scatter_blocks(send, back, [cd2])
    sums = line_sum(back, SUMS_ONE)
    alpha2 = pick_packed(sums, 0) / pick_packed(sums, 1)
    for e in range(3):
        solution[e] = part[e] + alpha2 * d2[e]
        residual[e] = r2[e] - alpha2 * (dd2[e] + from_panels(cd2, e))


def call(kernel, spaces, outs, scratch=(), mebibytes=16, name=None):
    kinds = {"s": pltpu.SMEM, "v": pltpu.VMEM, "a": pl.ANY}
    return pl.pallas_call(
        kernel,
        out_shape=tuple(jax.ShapeDtypeStruct(shape, kind) for shape, kind in outs),
        in_specs=[pl.BlockSpec(memory_space=kinds[k]) for k in spaces],
        out_specs=tuple(pl.BlockSpec(memory_space=pltpu.VMEM) for _ in outs),
        scratch_shapes=[pltpu.VMEM(shape, F32) for shape in scratch],
        compiler_params=pltpu.CompilerParams(vmem_limit_bytes=mebibytes * 2**20),
        name=name,
    )


def per_device(right_side, masses, stiffness, hessian, send_list, pair_refs, counts):
    _, row_count, col_count = right_side.shape
    width = hessian.shape[1]
    block_len = width // 3
    peers = lax.axis_size("gx")
    assert send_list.shape[1] == peers * CAP and col_count == 4 * block_len and block_len == 128
    field = (right_side.shape, F32)
    first, second = ((peers, 16, width), BF16), ((peers, 8, width), BF16)
    third, fourth = ((peers, 16, 4 * block_len), BF16), ((peers, 4, width), BF16)
    held_shape, edges = ((peers, 8, width), F32), (peers, 8, block_len)
    panels = (3, 4, row_count, block_len)
    tiles, wide_tiles, rims = (peers * CAP, 8, width), (peers, 16, 4 * block_len), (peers, 8, width)
    line = ((1, 128), F32)

    routes = jnp.concatenate([send_list, counts.reshape(1, 1)], axis=1)
    pair_refs = pair_refs.T

    def swap(message):
        return lax.all_to_all(message, "gx", split_axis=0, concat_axis=0, tiled=True)

    token = jnp.zeros(line[0], F32)
    for _ in range(2):
        (token,) = call(announce_kernel, "aa", [line], [], 51, name="announce")(hessian, token)
    sent1, loc = call(
        start_kernel,
        "asvvv",
        [first, field],
        [panels, panels, (8, width), rims],
        name="start",
    )(token, routes, right_side, masses, stiffness)
    got1 = swap(sent1)
    sent2, held, own, known1 = call(
        owner_kernel,
        "ssvv",
        [second, held_shape, ((8, width), F32), line],
        [tiles, tiles, tiles, tiles, (peers, 16, width), rims, edges],
        32,
        name="owner",
    )(pair_refs, routes, got1, hessian)
    got2 = swap(sent2)
    sent3, v1, v2, known = call(
        middle_kernel,
        "svvvvvvv",
        [third, field, field, line],
        [panels, panels, panels, (2, 8, width), (peers, 16, block_len), rims],
        name="middle",
    )(routes, got2, own, known1, right_side, loc, masses, stiffness)
    got3 = swap(sent3)
    sent4, part, r2, d2, dd2 = call(
        last_kernel,
        "ssvvvvvvvvvvv",
        [fourth, field, field, field, field],
        [tiles, tiles, (peers, 16, width), wide_tiles, rims, (8, width), edges],
        32,
        name="last",
    )(
        pair_refs, routes, got1, got3, held, sent2, known, right_side, v1, v2, masses, stiffness,
        hessian,
    )
    got4 = swap(sent4)
    return call(finish_kernel, "svvvvv", [field, field], [panels, (peers, 4, width)], name="finish")(
        routes, got4, part, r2, d2, dd2
    )


def solution(mesh):
    placed = (
        P(None, ("groups", "gx"), None),
        P(("groups", "gx"), None),
        P(None, ("groups", "gx"), None),
        P(("groups", "gx"), None, None),
        P(("groups", "gx"), None),
        P(("groups", "gx"), None),
        P(("groups", "gx")),
    )
    return jax.shard_map(
        per_device,
        mesh=mesh,
        in_specs=placed,
        out_specs=(P(None, ("groups", "gx"), None), P(None, ("groups", "gx"), None)),
        check_vma=False,
    )
```

```python
import jax
import jax.numpy as jnp
from jax import lax
from jax.experimental import pallas as pl
from jax.experimental.pallas import tpu as pltpu
from jax.sharding import PartitionSpec as P

F32 = jnp.float32
BF16 = jnp.bfloat16
CAP = 3
SUMS_TWO, SUMS_ONE = 2 * CAP, CAP
CODE_LANE = 64


def iota(shape, dim):
    return lax.broadcasted_iota(jnp.int32, shape, dim)


def total(value):
    return jnp.sum(jnp.sum(value, axis=0, keepdims=True), axis=1, keepdims=True)


def line_of(scalars, width):
    lanes = iota((1, width), 1)
    line = jnp.zeros((1, width), F32)
    for k, value in enumerate(scalars):
        line = jnp.where(lanes == k, value, line)
    return line


def line_sum(message, row):
    peers = message.shape[0]
    parts = [message[d, row : row + 1, 0:128] for d in range(peers)]
    while len(parts) > 1:
        parts = [a + b for a, b in zip(parts[::2], parts[1::2])] + (
            parts[-1:] if len(parts) % 2 else []
        )
    return parts[0]


def pick(line, k):
    return line[:, k : k + 1]


def place_of(send, position, col_blocks):
    block = send[0, position]
    return lax.div(block, jnp.int32(col_blocks)), lax.rem(block, jnp.int32(col_blocks))


def scatter_blocks(send, message, panels):
    peers = message.shape[0]
    _, col_blocks, _, block_len = panels[0].shape
    for field in panels:
        field[...] = jnp.zeros_like(field)

    def one(d, carry):
        for c in range(CAP):
            row, col = place_of(send, d * CAP + c, col_blocks)
            for f, field in enumerate(panels):
                for e in range(3):
                    field[e, col, pl.ds(row, 1), :] = message[
                        d, f * CAP + c : f * CAP + c + 1, e * block_len : (e + 1) * block_len
                    ]
        return carry

    lax.fori_loop(0, peers, one, 0, unroll=4)


def to_panels(panels, e, value):
    _, col_blocks, _, block_len = panels.shape
    for q in range(col_blocks):
        panels[e, q] = value[:, q * block_len : (q + 1) * block_len]


def from_panels(panels, e):
    return jnp.concatenate([panels[e, q] for q in range(panels.shape[1])], axis=1)


def put_line(message, row, line):
    for d in range(message.shape[0]):
        message[d, row : row + 1, :] = line


def inner_apply(v, mass, kx, ky):
    rows, cols = v.shape
    row_ids = iota((rows, cols), 0)
    flux_x = jnp.where(row_ids == rows - 1, 0.0, kx * (v - pltpu.roll(v, rows - 1, 0)))
    flux_y = ky * (v - pltpu.roll(v, cols - 1, 1))
    return mass * v + (flux_x - pltpu.roll(flux_x, 1, 0)) + (flux_y - pltpu.roll(flux_y, 1, 1))


def masked_ky(stiff):
    ky = stiff[1]
    return jnp.where(iota(ky.shape, 1) == ky.shape[1] - 1, 0.0, ky)


def rounded(value):
    return value.astype(BF16).astype(F32)


def packed_line(scalars):
    parts = []
    for value in scalars:
        high = rounded(value)
        middle = rounded(value - high)
        parts += [high, middle, value - high - middle]
    return line_of(parts, 128)


def pick_packed(line, k):
    return pick(line, 3 * k) + pick(line, 3 * k + 1) + pick(line, 3 * k + 2)


def thrice(tile):
    return jnp.concatenate([tile] * 3, axis=1)


def write_rim(target, field):
    rows, block_len = field.shape[1], 128
    col_blocks = field.shape[2] // block_len
    for side, row in enumerate((0, rows - 1)):
        for q in range(col_blocks):
            for e in range(3):
                line = side * col_blocks + q
                target[line : line + 1, e * block_len : (e + 1) * block_len] = field[
                    e, row : row + 1, q * block_len : (q + 1) * block_len
                ]


def rim_row(tile, side, e):
    block_len = tile.shape[1] // 3
    half = tile.shape[0] // 2
    return jnp.concatenate(
        [
            tile[side * half + q : side * half + q + 1, e * block_len : (e + 1) * block_len]
            for q in range(half)
        ],
        axis=1,
    )


def across(before, after):
    half = before.shape[0] // 2
    return pltpu.roll(jnp.where(iota(before.shape, 0) >= half, before, after), half, 0)


def around(d, peers):
    return jnp.maximum(d - 1, 0), jnp.minimum(d + 1, peers - 1)


def unpack_first(got, tiles, edges):
    sub = iota(edges.shape[1:], 0)
    for d in range(got.shape[0]):
        tile = got[d].astype(F32)
        tiles[d] = tile
        kx = jnp.where(sub % 4 == 3, wide(tile[15:16, 0:128]), 0.0)
        for q in range(3):
            kx = jnp.where(sub % 4 == q, wide(tile[14:15, q * 128 : (q + 1) * 128]), kx)
        edges[d] = kx


def rim_coefs(edges, d):
    before, _ = around(d, edges.shape[0])
    here, other = edges[d], edges[before]
    other = jnp.where(d > 0, other, 0.0)
    return thrice(jnp.where(iota(here.shape, 0) < 4, other, here))


def chosen(code, tile):
    return jnp.sum(
        jnp.where(iota(tile.shape, 0).astype(F32) == code, tile, 0.0), axis=0, keepdims=True
    )


def announce_kernel(hessian, _, token):
    token[...] = jnp.zeros_like(token)


def start_kernel(_, send, b, mass, stiff, message, loc, b_panels, loc_panels, rim, stage):
    rows, peers = b.shape[1], message.shape[0]
    col_blocks, block_len = b_panels.shape[1], b_panels.shape[3]
    ky = masked_ky(stiff)
    sq = dot = None
    for e in range(3):
        v = b[e]
        image = inner_apply(v, mass[...], stiff[0], ky)
        loc[e] = image
        to_panels(b_panels, e, v)
        to_panels(loc_panels, e, image)
        sq = v * v if sq is None else sq + v * v
        dot = v * image if dot is None else dot + v * image
    write_rim(rim, b)
    ends = lax.axis_index("gx") == peers - 1
    kx = jnp.where(ends, 0.0, stiff[0, rows - 1 : rows, :])
    line = packed_line([total(sq), total(dot)])
    lanes, sub = iota((1, 128), 1), iota((8, 3 * block_len), 0)

    def one(d, carry):
        own_line = line
        for c in range(CAP):
            row, col = place_of(send, d * CAP + c, col_blocks)
            code = jnp.where(row == 0, col, jnp.where(row == rows - 1, col_blocks + col, 99))
            own_line = jnp.where(lanes == CODE_LANE + c, code.astype(F32), own_line)
            for e in range(3):
                span = slice(e * block_len, (e + 1) * block_len)
                stage[d, c : c + 1, span] = b_panels[e, col, pl.ds(row, 1), :]
                stage[d, CAP + c : CAP + c + 1, span] = loc_panels[e, col, pl.ds(row, 1), :]
        tail = jnp.concatenate([kx[:, 3 * block_len :], own_line, jnp.zeros_like(own_line)], axis=1)
        lower = jnp.where(sub == 2 * CAP, wide(kx[:, : 3 * block_len]), stage[d])
        lower = jnp.where(sub == 2 * CAP + 1, wide(tail), lower)
        message[d] = jnp.concatenate([rim[...], lower], axis=0).astype(BF16)
        return carry

    lax.fori_loop(0, peers, one, 0, unroll=4)


def contact_products(pairs, live_count, x8, y8, held):
    y8[...] = jnp.zeros_like(y8)
    for h in range(held.shape[0]):
        a, b = pairs[0, h], pairs[1, h]
        delta = x8[a] - x8[b]
        delta = jnp.where(h < live_count, delta, 0.0)
        coarse = delta.astype(jnp.bfloat16).astype(F32)
        both = jnp.concatenate([coarse, delta - coarse], axis=0).astype(jnp.bfloat16)
        product = jnp.dot(both, held[h], preferred_element_type=F32)
        y = product[0:8] + product[8:16]
        y8[a] = y8[a] + y
        y8[b] = y8[b] - y


def wide(row):
    return jnp.broadcast_to(row, (8, row.shape[1]))


def contact_dot(x8, y8):
    value = x8[0] * y8[0]
    for p in range(1, x8.shape[0]):
        value = value + x8[p] * y8[p]
    return total(value[0:1])


def owner_kernel(
    pairs, live, got, hessian, message, held, own, known, x8, y8, z8, f8, tiles, corr, edges
):
    peers, _, _ = got.shape
    width = x8.shape[2]
    block_len = width // 3
    unpack_first(got, tiles, edges)

    def one(d, carry):
        energy, sums = carry
        before, after = around(d, peers)
        diff = tiles[d, 0:8, 0:width] - across(
            tiles[before, 0:8, 0:width], tiles[after, 0:8, 0:width]
        )
        fix = rim_coefs(edges, d) * diff
        corr[d] = fix
        body, line = tiles[d, 8:16, 0:width], tiles[d, 15:16, block_len : 2 * block_len]
        for c in range(CAP):
            p = d * CAP + c
            x8[p] = wide(body[c : c + 1])
            f8[p] = wide(body[CAP + c : CAP + c + 1] + chosen(pick(line, CODE_LANE + c), fix))
        return energy + fix * diff, sums + line

    zero = jnp.zeros((8, width), F32)
    energy, sums = lax.fori_loop(0, peers, one, (zero, jnp.zeros((1, block_len), F32)), unroll=4)
    known[...] = line_of(
        [pick_packed(sums, 0), pick_packed(sums, 1) + 0.5 * total(energy)], known.shape[1]
    )
    own[...] = corr[lax.axis_index("gx")]

    contact_products(pairs, live[0, live.shape[1] - 1], x8, y8, hessian)
    line = packed_line([contact_dot(x8, y8)])
    line = jnp.concatenate([line, jnp.zeros((1, width - block_len), F32)], axis=1)
    for p in range(x8.shape[0]):
        x8[p] = f8[p] + rounded(y8[p])
    contact_products(pairs, live[0, live.shape[1] - 1], x8, z8, hessian)
    sub = iota((8, width), 0)
    for d in range(peers):
        tile = jnp.where(sub == SUMS_TWO, wide(line), 0.0)
        kept = tiles[d, 8:16, 0:width]
        for c in range(CAP):
            tile = jnp.where(sub == c, y8[d * CAP + c], tile)
            tile = jnp.where(sub == CAP + c, z8[d * CAP + c], tile)
            kept = jnp.where(sub == CAP + c, x8[d * CAP + c], kept)
        message[d] = tile.astype(BF16)
        held[d] = kept


def middle_kernel(
    send, got2, own, known1, b, loc, mass, stiff, message, v1, v2, known, cb, cv1, panels, common, stage, back
):
    rows, peers = b.shape[1], message.shape[0]
    col_blocks, block_len = panels.shape[1], panels.shape[3]
    for d in range(peers):
        back[d] = got2[d].astype(F32)
    scatter_blocks(send, back, [cb, cv1])
    ky = masked_ky(stiff)
    rr0 = pick(known1[...], 0)
    alpha0 = rr0 / (pick(known1[...], 1) + pick_packed(line_sum(back, SUMS_TWO), 0))
    known[...] = line_of([rr0, alpha0], known.shape[1])
    sums = None
    for e in range(3):
        v1[e] = loc[e] + from_panels(cb, e)
        for side, row in enumerate((0, rows - 1)):
            v1[e, row : row + 1, :] = v1[e, row : row + 1, :] + rim_row(own[...], side, e)
        image = v1[e]
        inner = inner_apply(image, mass[...], stiff[0], ky)
        to_panels(panels, e, inner)
        second = inner + from_panels(cv1, e)
        v2[e] = second
        right = b[e]
        r1 = right - alpha0 * image
        w = image - alpha0 * second
        terms = [r1 * r1, r1 * w, r1 * image, right * w, right * image]
        sums = terms if sums is None else [s + t for s, t in zip(sums, terms)]
    write_rim(common.at[0], v1)
    write_rim(common.at[1], v2)
    line = packed_line([total(s) for s in sums])
    width = stage.shape[2]
    line = wide(jnp.concatenate([line, jnp.zeros((1, width - block_len), F32)], axis=1))
    sub = iota((8, width), 0)
    me = lax.axis_index("gx")

    def one(d, carry):
        for c in range(CAP):
            row, col = place_of(send, d * CAP + c, col_blocks)
            for e in range(3):
                stage[d, 4 + c : 5 + c, e * block_len : (e + 1) * block_len] = panels[
                    e, col, pl.ds(row, 1), :
                ]
        facing = jnp.where(d < me, common[1], pltpu.roll(common[1], 4, 0))
        lower = jnp.where(sub < 4, facing, jnp.where(sub == 7, line, stage[d]))
        message[d] = jnp.concatenate([common[0], lower], axis=0).astype(BF16)
        return carry

    lax.fori_loop(0, peers, one, 0, unroll=4)


def coefficients(known, sums, b_x, v1_x):
    rr0, alpha0 = pick(known, 0), pick(known, 1)
    rr1, r1w, r1v1, bw, bv1 = [pick_packed(sums, k) for k in range(5)]
    r1w = r1w - alpha0 * (b_x - alpha0 * v1_x)
    bw = bw - alpha0 * b_x
    beta0 = rr1 / rr0
    dad1 = r1w + beta0 * (r1v1 + bw) + beta0 * beta0 * bv1
    return (alpha0, beta0, rr1 / dad1), line_of([rr1, dad1], known.shape[1])


def advance(b, v1, v2, coefs):
    alpha0, beta0, alpha1 = coefs
    r1 = b - alpha0 * v1
    image = v1 - alpha0 * v2 + beta0 * v1
    return r1 + beta0 * b, image, r1 - alpha1 * image


def last_kernel(
    pairs, live, got1, got3, held, sent2, known, b, v1, v2, mass, stiff, hessian,
    message, part, d1_out, ad1_out, r2_out, ar2, known_out,
    x8, y8, tiles1, tiles3, corr, rim, edges,
):
    peers = got1.shape[0]
    width = x8.shape[2]
    rows = b.shape[1]
    unpack_first(got1, tiles1, edges)
    for d in range(peers):
        tiles3[d] = got3[d].astype(F32)

    def one(d, carry):
        before, after = around(d, peers)
        first = tiles3[d, 0:8, :]
        fix = rim_coefs(edges, d) * (first - across(tiles3[before, 0:8, :], tiles3[after, 0:8, :]))
        corr[d] = fix
        return (
            carry[0] + tiles1[d, 0:8, :] * fix,
            carry[1] + first * fix,
            carry[2] + tiles3[d, 15:16, 0:128],
        )

    zero = jnp.zeros((8, width), F32)
    b_x, v1_x, sums = lax.fori_loop(
        0, peers, one, (zero, zero, jnp.zeros((1, 128), F32)), unroll=4
    )
    coefs, known_line = coefficients(known[...], sums, total(b_x), total(v1_x))
    known_out[...] = known_line

    def two(d, carry):
        line = tiles1[d, 15:16, 128:256]
        fix, values = corr[d], tiles3[d, 8:16, :]
        kept, sent = held[d], sent2[d].astype(F32)
        for c in range(CAP):
            value = values[4 + c : 5 + c] + chosen(pick(line, CODE_LANE + c), fix)
            value = value + sent[CAP + c : CAP + c + 1]
            x8[d * CAP + c] = wide(
                advance(kept[c : c + 1], kept[CAP + c : CAP + c + 1], value, coefs)[2]
            )
        return carry

    lax.fori_loop(0, peers, two, 0, unroll=4)

    me = lax.axis_index("gx")
    before, after = around(me, peers)
    ky = masked_ky(stiff)
    mine = corr[me] * coefs[0]
    for e in range(3):
        d1, image, r2 = advance(b[e], v1[e], v2[e], coefs)
        part[e] = coefs[0] * b[e] + coefs[2] * d1
        d1_out[e] = d1
        ad1_out[e] = image
        r2_out[e] = r2
        for side, row in enumerate((0, rows - 1)):
            change = rim_row(mine, side, e)
            ad1_out[e, row : row + 1, :] = ad1_out[e, row : row + 1, :] - change
            r2_out[e, row : row + 1, :] = r2_out[e, row : row + 1, :] + coefs[2] * change
    write_rim(rim, r2_out)

    facing = jnp.where(
        iota((8, width), 0) < 4, tiles3[before, 8:16, :], pltpu.roll(tiles3[after, 8:16, :], 4, 0)
    )
    others = advance(
        across(tiles1[before, 0:8, :], tiles1[after, 0:8, :]),
        across(tiles3[before, 0:8, :], tiles3[after, 0:8, :]),
        facing + across(corr[before], corr[after]),
        coefs,
    )[2]
    fix = rim_coefs(edges, me) * (rim[...] - others)
    sums = None
    for e in range(3):
        r2 = r2_out[e]
        ar2[e] = inner_apply(r2, mass[...], stiff[0], ky)
        for side, row in enumerate((0, rows - 1)):
            ar2[e, row : row + 1, :] = ar2[e, row : row + 1, :] + rim_row(fix, side, e)
        terms = [r2 * r2, r2 * ar2[e], r2 * ad1_out[e]]
        sums = terms if sums is None else [s + t for s, t in zip(sums, terms)]
    sums = [total(value) for value in sums]

    contact_products(pairs, live[0, live.shape[1] - 1], x8, y8, hessian)
    line = packed_line([sums[0], sums[1] + contact_dot(x8, y8), sums[2]])
    line = jnp.concatenate([line, jnp.zeros((1, width - 128), F32)], axis=1)
    for d in range(peers):
        rows = [y8[d * CAP + c, 0:1, :] for c in range(CAP)]
        message[d] = jnp.concatenate([*rows, line], axis=0).astype(BF16)


def finish_kernel(send, got4, known, part, d1, ad1, r2, ar2, solution, residual, cr2, back):
    for d in range(got4.shape[0]):
        back[d] = got4[d].astype(F32)
    scatter_blocks(send, back, [cr2])
    sums = line_sum(back, SUMS_ONE)
    rr2, rar2, rad1 = [pick_packed(sums, k) for k in range(3)]
    beta1 = rr2 / pick(known[...], 0)
    alpha2 = rr2 / (rar2 + 2.0 * beta1 * rad1 + beta1 * beta1 * pick(known[...], 1))
    for e in range(3):
        solution[e] = part[e] + alpha2 * (r2[e] + beta1 * d1[e])
        residual[e] = r2[e] - alpha2 * (ar2[e] + from_panels(cr2, e) + beta1 * ad1[e])


def call(kernel, spaces, outs, scratch=(), mebibytes=16, name=None):
    kinds = {"s": pltpu.SMEM, "v": pltpu.VMEM, "a": pl.ANY}
    return pl.pallas_call(
        kernel,
        out_shape=tuple(jax.ShapeDtypeStruct(shape, kind) for shape, kind in outs),
        in_specs=[pl.BlockSpec(memory_space=kinds[k]) for k in spaces],
        out_specs=tuple(pl.BlockSpec(memory_space=pltpu.VMEM) for _ in outs),
        scratch_shapes=[pltpu.VMEM(shape, F32) for shape in scratch],
        compiler_params=pltpu.CompilerParams(vmem_limit_bytes=mebibytes * 2**20),
        name=name,
    )


def per_device(right_side, masses, stiffness, hessian, send_list, pair_refs, counts):
    _, row_count, col_count = right_side.shape
    width = hessian.shape[1]
    block_len = width // 3
    peers = lax.axis_size("gx")
    assert send_list.shape[1] == peers * CAP and col_count == 4 * block_len and block_len == 128
    field = (right_side.shape, F32)
    first, second = ((peers, 16, width), BF16), ((peers, 8, width), BF16)
    third, fourth = ((peers, 16, width), BF16), ((peers, 4, width), BF16)
    held_shape, edges = ((peers, 8, width), F32), (peers, 8, block_len)
    panels = (3, 4, row_count, block_len)
    tiles, wide_tiles, rims = (peers * CAP, 8, width), (peers, 16, width), (peers, 8, width)
    line = ((1, 128), F32)

    routes = jnp.concatenate([send_list, counts.reshape(1, 1)], axis=1)
    pair_refs = pair_refs.T

    def swap(message):
        return lax.all_to_all(message, "gx", split_axis=0, concat_axis=0, tiled=True)

    token = jnp.zeros(line[0], F32)
    for _ in range(2):
        (token,) = call(announce_kernel, "aa", [line], [], 51, name="announce")(hessian, token)
    sent1, loc = call(
        start_kernel,
        "asvvv",
        [first, field],
        [panels, panels, (8, width), rims],
        name="start",
    )(token, routes, right_side, masses, stiffness)
    got1 = swap(sent1)
    sent2, held, own, known1 = call(
        owner_kernel,
        "ssvv",
        [second, held_shape, ((8, width), F32), line],
        [tiles, tiles, tiles, tiles, wide_tiles, rims, edges],
        32,
        name="owner",
    )(pair_refs, routes, got1, hessian)
    got2 = swap(sent2)
    sent3, v1, v2, known = call(
        middle_kernel,
        "svvvvvvv",
        [third, field, field, line],
        [panels, panels, panels, (2, 8, width), rims, rims],
        name="middle",
    )(routes, got2, own, known1, right_side, loc, masses, stiffness)
    got3 = swap(sent3)
    sent4, part, d1, ad1, r2, ar2, known2 = call(
        last_kernel,
        "ssvvvvvvvvvvv",
        [fourth, field, field, field, field, field, line],
        [tiles, tiles, wide_tiles, wide_tiles, rims, (8, width), edges],
        32,
        name="last",
    )(
        pair_refs, routes, got1, got3, held, sent2, known, right_side, v1, v2, masses, stiffness,
        hessian,
    )
    got4 = swap(sent4)
    return call(finish_kernel, "svvvvvvv", [field, field], [panels, (peers, 4, width)], name="finish")(
        routes, got4, known2, part, d1, ad1, r2, ar2
    )


def solution(mesh):
    placed = (
        P(None, ("groups", "gx"), None),
        P(("groups", "gx"), None),
        P(None, ("groups", "gx"), None),
        P(("groups", "gx"), None, None),
        P(("groups", "gx"), None),
        P(("groups", "gx"), None),
        P(("groups", "gx")),
    )
    return jax.shard_map(
        per_device,
        mesh=mesh,
        in_specs=placed,
        out_specs=(P(None, ("groups", "gx"), None), P(None, ("groups", "gx"), None)),
        check_vma=False,
    )
```

```python
import jax
import jax.numpy as jnp
from jax import lax
from jax.experimental import pallas as pl
from jax.experimental.pallas import tpu as pltpu
from jax.sharding import PartitionSpec as P

F32 = jnp.float32
BF16 = jnp.bfloat16
CAP = 3
SUMS_TWO, SUMS_ONE = 2 * CAP, CAP
CODE_LANE = 64


def iota(shape, dim):
    return lax.broadcasted_iota(jnp.int32, shape, dim)


def total(value):
    return jnp.sum(jnp.sum(value, axis=0, keepdims=True), axis=1, keepdims=True)


def line_of(scalars, width):
    lanes = iota((1, width), 1)
    line = jnp.zeros((1, width), F32)
    for k, value in enumerate(scalars):
        line = jnp.where(lanes == k, value, line)
    return line


def line_sum(message, row):
    peers = message.shape[0]
    parts = [message[d, row : row + 1, 0:128] for d in range(peers)]
    while len(parts) > 1:
        parts = [a + b for a, b in zip(parts[::2], parts[1::2])] + (
            parts[-1:] if len(parts) % 2 else []
        )
    return parts[0]


def pick(line, k):
    return line[:, k : k + 1]


def place_of(send, position, col_blocks):
    block = send[0, position]
    shift = col_blocks.bit_length() - 1
    return lax.shift_right_logical(block, jnp.int32(shift)), block & (col_blocks - 1)


def scatter_blocks(send, message, panels):
    peers = message.shape[0]
    _, col_blocks, _, block_len = panels[0].shape
    for field in panels:
        field[...] = jnp.zeros_like(field)

    def one(d, carry):
        for c in range(CAP):
            row, col = place_of(send, d * CAP + c, col_blocks)
            for f, field in enumerate(panels):
                for e in range(3):
                    field[e, col, pl.ds(row, 1), :] = message[
                        d, f * CAP + c : f * CAP + c + 1, e * block_len : (e + 1) * block_len
                    ]
        return carry

    lax.fori_loop(0, peers, one, 0, unroll=16)


def to_panels(panels, e, value):
    _, col_blocks, _, block_len = panels.shape
    for q in range(col_blocks):
        panels[e, q] = value[:, q * block_len : (q + 1) * block_len]


def from_panels(panels, e):
    return jnp.concatenate([panels[e, q] for q in range(panels.shape[1])], axis=1)


def put_line(message, row, line):
    for d in range(message.shape[0]):
        message[d, row : row + 1, :] = line


def inner_apply(v, mass, kx, ky):
    rows, cols = v.shape
    row_ids = iota((rows, cols), 0)
    flux_x = jnp.where(row_ids == rows - 1, 0.0, kx * (v - pltpu.roll(v, rows - 1, 0)))
    flux_y = ky * (v - pltpu.roll(v, cols - 1, 1))
    return mass * v + (flux_x - pltpu.roll(flux_x, 1, 0)) + (flux_y - pltpu.roll(flux_y, 1, 1))


def masked_ky(stiff):
    ky = stiff[1]
    return jnp.where(iota(ky.shape, 1) == ky.shape[1] - 1, 0.0, ky)


def rounded(value):
    return value.astype(BF16).astype(F32)


def packed_line(scalars):
    parts = []
    for value in scalars:
        high = rounded(value)
        middle = rounded(value - high)
        parts += [high, middle, value - high - middle]
    return line_of(parts, 128)


def pick_packed(line, k):
    return pick(line, 3 * k) + pick(line, 3 * k + 1) + pick(line, 3 * k + 2)


def thrice(tile):
    return jnp.concatenate([tile] * 3, axis=1)


def write_rim(target, field):
    rows, block_len = field.shape[1], 128
    col_blocks = field.shape[2] // block_len
    for side, row in enumerate((0, rows - 1)):
        for q in range(col_blocks):
            for e in range(3):
                line = side * col_blocks + q
                target[line : line + 1, e * block_len : (e + 1) * block_len] = field[
                    e, row : row + 1, q * block_len : (q + 1) * block_len
                ]


def rim_row(tile, side, e):
    block_len = tile.shape[1] // 3
    half = tile.shape[0] // 2
    return jnp.concatenate(
        [
            tile[side * half + q : side * half + q + 1, e * block_len : (e + 1) * block_len]
            for q in range(half)
        ],
        axis=1,
    )


def across(before, after):
    half = before.shape[0] // 2
    return pltpu.roll(jnp.where(iota(before.shape, 0) >= half, before, after), half, 0)


def around(d, peers):
    return jnp.maximum(d - 1, 0), jnp.minimum(d + 1, peers - 1)


def unpack_first(got, tiles, edges):
    sub = iota(edges.shape[1:], 0)
    for d in range(got.shape[0]):
        tile = got[d].astype(F32)
        tiles[d] = tile
        kx = jnp.where(sub % 4 == 3, wide(tile[15:16, 0:128]), 0.0)
        for q in range(3):
            kx = jnp.where(sub % 4 == q, wide(tile[14:15, q * 128 : (q + 1) * 128]), kx)
        edges[d] = kx


def rim_coefs(edges, d):
    before, _ = around(d, edges.shape[0])
    here, other = edges[d], edges[before]
    other = jnp.where(d > 0, other, 0.0)
    return thrice(jnp.where(iota(here.shape, 0) < 4, other, here))


def chosen(code, tile):
    return jnp.sum(
        jnp.where(iota(tile.shape, 0).astype(F32) == code, tile, 0.0), axis=0, keepdims=True
    )


def announce_kernel(hessian, _, token):
    token[...] = jnp.zeros_like(token)


def start_kernel(_, send, b, mass, stiff, message, loc, b_panels, loc_panels, rim, stage):
    rows, peers = b.shape[1], message.shape[0]
    col_blocks, block_len = b_panels.shape[1], b_panels.shape[3]
    ky = masked_ky(stiff)
    sq = dot = None
    for e in range(3):
        v = b[e]
        image = inner_apply(v, mass[...], stiff[0], ky)
        loc[e] = image
        to_panels(b_panels, e, v)
        to_panels(loc_panels, e, image)
        sq = v * v if sq is None else sq + v * v
        dot = v * image if dot is None else dot + v * image
    write_rim(rim, b)
    ends = lax.axis_index("gx") == peers - 1
    kx = jnp.where(ends, 0.0, stiff[0, rows - 1 : rows, :])
    line = packed_line([total(sq), total(dot)])
    lanes, sub = iota((1, 128), 1), iota((8, 3 * block_len), 0)

    def one(d, carry):
        own_line = line
        for c in range(CAP):
            row, col = place_of(send, d * CAP + c, col_blocks)
            code = jnp.where(row == 0, col, jnp.where(row == rows - 1, col_blocks + col, 99))
            own_line = jnp.where(lanes == CODE_LANE + c, code.astype(F32), own_line)
            for e in range(3):
                span = slice(e * block_len, (e + 1) * block_len)
                stage[d, c : c + 1, span] = b_panels[e, col, pl.ds(row, 1), :]
                stage[d, CAP + c : CAP + c + 1, span] = loc_panels[e, col, pl.ds(row, 1), :]
        tail = jnp.concatenate([kx[:, 3 * block_len :], own_line, jnp.zeros_like(own_line)], axis=1)
        lower = jnp.where(sub == 2 * CAP, wide(kx[:, : 3 * block_len]), stage[d])
        lower = jnp.where(sub == 2 * CAP + 1, wide(tail), lower)
        message[d] = jnp.concatenate([rim[...], lower], axis=0).astype(BF16)
        return carry

    lax.fori_loop(0, peers, one, 0, unroll=16)


def contact_products(pairs, live_count, x8, y8, held):
    y8[...] = jnp.zeros_like(y8)
    for h in range(held.shape[0]):
        a, b = pairs[0, h], pairs[1, h]
        delta = x8[a] - x8[b]
        delta = jnp.where(h < live_count, delta, 0.0)
        coarse = delta.astype(jnp.bfloat16).astype(F32)
        both = jnp.concatenate([coarse, delta - coarse], axis=0).astype(jnp.bfloat16)
        product = jnp.dot(both, held[h], preferred_element_type=F32)
        y = product[0:8] + product[8:16]
        y8[a] = y8[a] + y
        y8[b] = y8[b] - y


def wide(row):
    return jnp.broadcast_to(row, (8, row.shape[1]))


def contact_dot(x8, y8):
    value = x8[0] * y8[0]
    for p in range(1, x8.shape[0]):
        value = value + x8[p] * y8[p]
    return total(value[0:1])


def owner_kernel(
    pairs, live, got, hessian, message, held, own, known, x8, y8, z8, f8, tiles, corr, edges
):
    peers, _, _ = got.shape
    width = x8.shape[2]
    block_len = width // 3
    unpack_first(got, tiles, edges)

    def one(d, carry):
        energy, sums = carry
        before, after = around(d, peers)
        diff = tiles[d, 0:8, 0:width] - across(
            tiles[before, 0:8, 0:width], tiles[after, 0:8, 0:width]
        )
        fix = rim_coefs(edges, d) * diff
        corr[d] = fix
        body, line = tiles[d, 8:16, 0:width], tiles[d, 15:16, block_len : 2 * block_len]
        for c in range(CAP):
            p = d * CAP + c
            x8[p] = wide(body[c : c + 1])
            f8[p] = wide(body[CAP + c : CAP + c + 1] + chosen(pick(line, CODE_LANE + c), fix))
        return energy + fix * diff, sums + line

    zero = jnp.zeros((8, width), F32)
    energy, sums = lax.fori_loop(0, peers, one, (zero, jnp.zeros((1, block_len), F32)), unroll=16)
    known[...] = line_of(
        [pick_packed(sums, 0), pick_packed(sums, 1) + 0.5 * total(energy)], known.shape[1]
    )
    own[...] = corr[lax.axis_index("gx")]

    contact_products(pairs, live[0, live.shape[1] - 1], x8, y8, hessian)
    line = packed_line([contact_dot(x8, y8)])
    line = jnp.concatenate([line, jnp.zeros((1, width - block_len), F32)], axis=1)
    for p in range(x8.shape[0]):
        x8[p] = f8[p] + rounded(y8[p])
    contact_products(pairs, live[0, live.shape[1] - 1], x8, z8, hessian)
    sub = iota((8, width), 0)
    for d in range(peers):
        tile = jnp.where(sub == SUMS_TWO, wide(line), 0.0)
        kept = tiles[d, 8:16, 0:width]
        for c in range(CAP):
            tile = jnp.where(sub == c, y8[d * CAP + c], tile)
            tile = jnp.where(sub == CAP + c, z8[d * CAP + c], tile)
            kept = jnp.where(sub == CAP + c, x8[d * CAP + c], kept)
        message[d] = tile.astype(BF16)
        held[d] = kept


def middle_kernel(
    send, got2, own, known1, b, loc, mass, stiff, message, v1, v2, known, cb, cv1, panels, common, stage, back
):
    rows, peers = b.shape[1], message.shape[0]
    col_blocks, block_len = panels.shape[1], panels.shape[3]
    for d in range(peers):
        back[d] = got2[d].astype(F32)
    scatter_blocks(send, back, [cb, cv1])
    ky = masked_ky(stiff)
    rr0 = pick(known1[...], 0)
    alpha0 = rr0 / (pick(known1[...], 1) + pick_packed(line_sum(back, SUMS_TWO), 0))
    known[...] = line_of([rr0, alpha0], known.shape[1])
    sums = None
    for e in range(3):
        v1[e] = loc[e] + from_panels(cb, e)
        for side, row in enumerate((0, rows - 1)):
            v1[e, row : row + 1, :] = v1[e, row : row + 1, :] + rim_row(own[...], side, e)
        image = v1[e]
        inner = inner_apply(image, mass[...], stiff[0], ky)
        to_panels(panels, e, inner)
        second = inner + from_panels(cv1, e)
        v2[e] = second
        right = b[e]
        r1 = right - alpha0 * image
        w = image - alpha0 * second
        terms = [r1 * r1, r1 * w, r1 * image, right * w, right * image]
        sums = terms if sums is None else [s + t for s, t in zip(sums, terms)]
    write_rim(common.at[0], v1)
    write_rim(common.at[1], v2)
    line = packed_line([total(s) for s in sums])
    width = stage.shape[2]
    line = wide(jnp.concatenate([line, jnp.zeros((1, width - block_len), F32)], axis=1))
    sub = iota((8, width), 0)
    me = lax.axis_index("gx")

    def one(d, carry):
        for c in range(CAP):
            row, col = place_of(send, d * CAP + c, col_blocks)
            for e in range(3):
                stage[d, 4 + c : 5 + c, e * block_len : (e + 1) * block_len] = panels[
                    e, col, pl.ds(row, 1), :
                ]
        facing = jnp.where(d < me, common[1], pltpu.roll(common[1], 4, 0))
        lower = jnp.where(sub < 4, facing, jnp.where(sub == 7, line, stage[d]))
        message[d] = jnp.concatenate([common[0], lower], axis=0).astype(BF16)
        return carry

    lax.fori_loop(0, peers, one, 0, unroll=16)


def coefficients(known, sums, b_x, v1_x):
    rr0, alpha0 = pick(known, 0), pick(known, 1)
    rr1, r1w, r1v1, bw, bv1 = [pick_packed(sums, k) for k in range(5)]
    r1w = r1w - alpha0 * (b_x - alpha0 * v1_x)
    bw = bw - alpha0 * b_x
    beta0 = rr1 / rr0
    dad1 = r1w + beta0 * (r1v1 + bw) + beta0 * beta0 * bv1
    return (alpha0, beta0, rr1 / dad1), line_of([rr1, dad1], known.shape[1])


def advance(b, v1, v2, coefs):
    alpha0, beta0, alpha1 = coefs
    r1 = b - alpha0 * v1
    image = v1 - alpha0 * v2 + beta0 * v1
    return r1 + beta0 * b, image, r1 - alpha1 * image


def last_kernel(
    pairs, live, got1, got3, held, sent2, known, b, v1, v2, mass, stiff, hessian,
    message, part, d1_out, ad1_out, r2_out, ar2, known_out,
    x8, y8, tiles1, tiles3, corr, rim, edges,
):
    peers = got1.shape[0]
    width = x8.shape[2]
    rows = b.shape[1]
    unpack_first(got1, tiles1, edges)
    for d in range(peers):
        tiles3[d] = got3[d].astype(F32)

    def one(d, carry):
        before, after = around(d, peers)
        first = tiles3[d, 0:8, :]
        fix = rim_coefs(edges, d) * (first - across(tiles3[before, 0:8, :], tiles3[after, 0:8, :]))
        corr[d] = fix
        return (
            carry[0] + tiles1[d, 0:8, :] * fix,
            carry[1] + first * fix,
            carry[2] + tiles3[d, 15:16, 0:128],
        )

    zero = jnp.zeros((8, width), F32)
    b_x, v1_x, sums = lax.fori_loop(
        0, peers, one, (zero, zero, jnp.zeros((1, 128), F32)), unroll=4
    )
    coefs, known_line = coefficients(known[...], sums, total(b_x), total(v1_x))
    known_out[...] = known_line

    def two(d, carry):
        line = tiles1[d, 15:16, 128:256]
        fix, values = corr[d], tiles3[d, 8:16, :]
        kept, sent = held[d], sent2[d].astype(F32)
        for c in range(CAP):
            value = values[4 + c : 5 + c] + chosen(pick(line, CODE_LANE + c), fix)
            value = value + sent[CAP + c : CAP + c + 1]
            x8[d * CAP + c] = wide(
                advance(kept[c : c + 1], kept[CAP + c : CAP + c + 1], value, coefs)[2]
            )
        return carry

    lax.fori_loop(0, peers, two, 0, unroll=16)

    me = lax.axis_index("gx")
    before, after = around(me, peers)
    ky = masked_ky(stiff)
    mine = corr[me] * coefs[0]
    for e in range(3):
        d1, image, r2 = advance(b[e], v1[e], v2[e], coefs)
        part[e] = coefs[0] * b[e] + coefs[2] * d1
        d1_out[e] = d1
        ad1_out[e] = image
        r2_out[e] = r2
        for side, row in enumerate((0, rows - 1)):
            change = rim_row(mine, side, e)
            ad1_out[e, row : row + 1, :] = ad1_out[e, row : row + 1, :] - change
            r2_out[e, row : row + 1, :] = r2_out[e, row : row + 1, :] + coefs[2] * change
    write_rim(rim, r2_out)

    facing = jnp.where(
        iota((8, width), 0) < 4, tiles3[before, 8:16, :], pltpu.roll(tiles3[after, 8:16, :], 4, 0)
    )
    others = advance(
        across(tiles1[before, 0:8, :], tiles1[after, 0:8, :]),
        across(tiles3[before, 0:8, :], tiles3[after, 0:8, :]),
        facing + across(corr[before], corr[after]),
        coefs,
    )[2]
    fix = rim_coefs(edges, me) * (rim[...] - others)
    sums = None
    for e in range(3):
        r2 = r2_out[e]
        ar2[e] = inner_apply(r2, mass[...], stiff[0], ky)
        for side, row in enumerate((0, rows - 1)):
            ar2[e, row : row + 1, :] = ar2[e, row : row + 1, :] + rim_row(fix, side, e)
        terms = [r2 * r2, r2 * ar2[e], r2 * ad1_out[e]]
        sums = terms if sums is None else [s + t for s, t in zip(sums, terms)]
    sums = [total(value) for value in sums]

    contact_products(pairs, live[0, live.shape[1] - 1], x8, y8, hessian)
    line = packed_line([sums[0], sums[1] + contact_dot(x8, y8), sums[2]])
    line = jnp.concatenate([line, jnp.zeros((1, width - 128), F32)], axis=1)
    for d in range(peers):
        rows = [y8[d * CAP + c, 0:1, :] for c in range(CAP)]
        message[d] = jnp.concatenate([*rows, line], axis=0).astype(BF16)


def finish_kernel(
    send, got4, known, part, d1, ad1, r2, ar2, solution, residual, cr2, back, x, r3, sems
):
    for d in range(got4.shape[0]):
        back[d] = got4[d].astype(F32)
    sums = line_sum(back, SUMS_ONE)
    rr2, rar2, rad1 = [pick_packed(sums, k) for k in range(3)]
    beta1 = rr2 / pick(known[...], 0)
    alpha2 = rr2 / (rar2 + 2.0 * beta1 * rad1 + beta1 * beta1 * pick(known[...], 1))
    copies = []

    def send_out(source, target):
        copies.append(pltpu.make_async_copy(source, target, sems.at[len(copies)]))
        copies[-1].start()

    for e in range(3):
        x[e] = part[e] + alpha2 * (r2[e] + beta1 * d1[e])
        send_out(x.at[e], solution.at[e])
    scatter_blocks(send, back, [cr2])
    for e in range(3):
        r3[e] = r2[e] - alpha2 * (ar2[e] + from_panels(cr2, e) + beta1 * ad1[e])
        send_out(r3.at[e], residual.at[e])
    for copy in copies:
        copy.wait()


def call(kernel, spaces, outs, scratch=(), mebibytes=16, semaphores=0, name=None):
    kinds = {"s": pltpu.SMEM, "v": pltpu.VMEM, "a": pl.ANY}
    return pl.pallas_call(
        kernel,
        out_shape=tuple(jax.ShapeDtypeStruct(shape, kind) for shape, kind in outs),
        in_specs=[pl.BlockSpec(memory_space=kinds[k]) for k in spaces],
        out_specs=tuple(
            pl.BlockSpec(memory_space=pl.ANY if semaphores else pltpu.VMEM) for _ in outs
        ),
        scratch_shapes=[pltpu.VMEM(shape, F32) for shape in scratch]
        + [pltpu.SemaphoreType.DMA((semaphores,))] * bool(semaphores),
        compiler_params=pltpu.CompilerParams(vmem_limit_bytes=mebibytes * 2**20),
        name=name,
    )


def per_device(right_side, masses, stiffness, hessian, send_list, pair_refs, counts):
    _, row_count, col_count = right_side.shape
    width = hessian.shape[1]
    block_len = width // 3
    peers = lax.axis_size("gx")
    assert send_list.shape[1] == peers * CAP and col_count == 4 * block_len and block_len == 128
    field = (right_side.shape, F32)
    first, second = ((peers, 16, width), BF16), ((peers, 8, width), BF16)
    third, fourth = ((peers, 16, width), BF16), ((peers, 4, width), BF16)
    held_shape, edges = ((peers, 8, width), F32), (peers, 8, block_len)
    panels = (3, 4, row_count, block_len)
    tiles, wide_tiles, rims = (peers * CAP, 8, width), (peers, 16, width), (peers, 8, width)
    line = ((1, 128), F32)

    routes = jnp.concatenate([send_list, counts.reshape(1, 1)], axis=1)
    pair_refs = pair_refs.T

    def swap(message):
        return lax.all_to_all(message, "gx", split_axis=0, concat_axis=0, tiled=True)

    token = jnp.zeros(line[0], F32)
    for _ in range(2):
        (token,) = call(announce_kernel, "aa", [line], [], 51, name="announce")(hessian, token)
    sent1, loc = call(
        start_kernel,
        "asvvv",
        [first, field],
        [panels, panels, (8, width), rims],
        name="start",
    )(token, routes, right_side, masses, stiffness)
    got1 = swap(sent1)
    sent2, held, own, known1 = call(
        owner_kernel,
        "ssvv",
        [second, held_shape, ((8, width), F32), line],
        [tiles, tiles, tiles, tiles, wide_tiles, rims, edges],
        32,
        name="owner",
    )(pair_refs, routes, got1, hessian)
    got2 = swap(sent2)
    sent3, v1, v2, known = call(
        middle_kernel,
        "svvvvvvv",
        [third, field, field, line],
        [panels, panels, panels, (2, 8, width), rims, rims],
        name="middle",
    )(routes, got2, own, known1, right_side, loc, masses, stiffness)
    got3 = swap(sent3)
    sent4, part, d1, ad1, r2, ar2, known2 = call(
        last_kernel,
        "ssvvvvvvvvvvv",
        [fourth, field, field, field, field, field, line],
        [tiles, tiles, wide_tiles, wide_tiles, rims, (8, width), edges],
        32,
        name="last",
    )(
        pair_refs, routes, got1, got3, held, sent2, known, right_side, v1, v2, masses, stiffness,
        hessian,
    )
    got4 = swap(sent4)
    return call(finish_kernel, "svvvvvvv", [field, field], [panels, (peers, 4, width), field[0], field[0]], semaphores=6, name="finish")(
        routes, got4, known2, part, d1, ad1, r2, ar2
    )


def solution(mesh):
    placed = (
        P(None, ("groups", "gx"), None),
        P(("groups", "gx"), None),
        P(None, ("groups", "gx"), None),
        P(("groups", "gx"), None, None),
        P(("groups", "gx"), None),
        P(("groups", "gx"), None),
        P(("groups", "gx")),
    )
    return jax.shard_map(
        per_device,
        mesh=mesh,
        in_specs=placed,
        out_specs=(P(None, ("groups", "gx"), None), P(None, ("groups", "gx"), None)),
        check_vma=False,
    )
```

```python
import jax
import jax.numpy as jnp
from jax import lax
from jax.experimental import pallas as pl
from jax.experimental.pallas import tpu as pltpu
from jax.sharding import PartitionSpec as P

F32 = jnp.float32
BF16 = jnp.bfloat16
CAP = 3
SUMS_TWO, SUMS_ONE = 2 * CAP, CAP
CODE_LANE = 64


def iota(shape, dim):
    return lax.broadcasted_iota(jnp.int32, shape, dim)


def total(value):
    return jnp.sum(jnp.sum(value, axis=0, keepdims=True), axis=1, keepdims=True)


def line_of(scalars, width):
    lanes = iota((1, width), 1)
    line = jnp.zeros((1, width), F32)
    for k, value in enumerate(scalars):
        line = jnp.where(lanes == k, value, line)
    return line


def line_sum(message, row):
    peers = message.shape[0]
    parts = [message[d, row : row + 1, 0:128] for d in range(peers)]
    while len(parts) > 1:
        parts = [a + b for a, b in zip(parts[::2], parts[1::2])] + (
            parts[-1:] if len(parts) % 2 else []
        )
    return parts[0]


def pick(line, k):
    return line[:, k : k + 1]


def place_of(send, position, col_blocks):
    block = send[0, position]
    shift = col_blocks.bit_length() - 1
    return lax.shift_right_logical(block, jnp.int32(shift)), block & (col_blocks - 1)


def scatter_blocks(send, message, panels):
    peers = message.shape[0]
    _, col_blocks, _, block_len = panels[0].shape
    for field in panels:
        field[...] = jnp.zeros_like(field)

    def one(d, carry):
        for c in range(CAP):
            row, col = place_of(send, d * CAP + c, col_blocks)
            for f, field in enumerate(panels):
                for e in range(3):
                    field[e, col, pl.ds(row, 1), :] = message[
                        d, f * CAP + c : f * CAP + c + 1, e * block_len : (e + 1) * block_len
                    ]
        return carry

    lax.fori_loop(0, peers, one, 0, unroll=16)


def to_panels(panels, e, value):
    _, col_blocks, _, block_len = panels.shape
    for q in range(col_blocks):
        panels[e, q] = value[:, q * block_len : (q + 1) * block_len]


def from_panels(panels, e):
    return jnp.concatenate([panels[e, q] for q in range(panels.shape[1])], axis=1)


def put_line(message, row, line):
    for d in range(message.shape[0]):
        message[d, row : row + 1, :] = line


def inner_apply(v, mass, kx, ky):
    rows, cols = v.shape
    row_ids = iota((rows, cols), 0)
    flux_x = jnp.where(row_ids == rows - 1, 0.0, kx * (v - pltpu.roll(v, rows - 1, 0)))
    flux_y = ky * (v - pltpu.roll(v, cols - 1, 1))
    return mass * v + (flux_x - pltpu.roll(flux_x, 1, 0)) + (flux_y - pltpu.roll(flux_y, 1, 1))


def masked_ky(stiff):
    ky = stiff[1]
    return jnp.where(iota(ky.shape, 1) == ky.shape[1] - 1, 0.0, ky)


def rounded(value):
    return value.astype(BF16).astype(F32)


def packed_line(scalars):
    parts = []
    for value in scalars:
        high = rounded(value)
        middle = rounded(value - high)
        parts += [high, middle, value - high - middle]
    return line_of(parts, 128)


def pick_packed(line, k):
    return pick(line, 3 * k) + pick(line, 3 * k + 1) + pick(line, 3 * k + 2)


def thrice(tile):
    return jnp.concatenate([tile] * 3, axis=1)


def write_rim(target, field):
    rows, block_len = field.shape[1], 128
    col_blocks = field.shape[2] // block_len
    for side, row in enumerate((0, rows - 1)):
        for q in range(col_blocks):
            for e in range(3):
                line = side * col_blocks + q
                target[line : line + 1, e * block_len : (e + 1) * block_len] = field[
                    e, row : row + 1, q * block_len : (q + 1) * block_len
                ]


def rim_row(tile, side, e):
    block_len = tile.shape[1] // 3
    half = tile.shape[0] // 2
    return jnp.concatenate(
        [
            tile[side * half + q : side * half + q + 1, e * block_len : (e + 1) * block_len]
            for q in range(half)
        ],
        axis=1,
    )


def across(before, after):
    half = before.shape[0] // 2
    return pltpu.roll(jnp.where(iota(before.shape, 0) >= half, before, after), half, 0)


def around(d, peers):
    return jnp.maximum(d - 1, 0), jnp.minimum(d + 1, peers - 1)


def unpack_first(got, tiles, edges):
    sub = iota(edges.shape[1:], 0)
    for d in range(got.shape[0]):
        tile = got[d].astype(F32)
        tiles[d] = tile
        kx = jnp.where(sub % 4 == 3, wide(tile[15:16, 0:128]), 0.0)
        for q in range(3):
            kx = jnp.where(sub % 4 == q, wide(tile[14:15, q * 128 : (q + 1) * 128]), kx)
        edges[d] = kx


def rim_coefs(edges, d):
    before, _ = around(d, edges.shape[0])
    here, other = edges[d], edges[before]
    other = jnp.where(d > 0, other, 0.0)
    return thrice(jnp.where(iota(here.shape, 0) < 4, other, here))


def chosen(code, tile):
    return jnp.sum(
        jnp.where(iota(tile.shape, 0).astype(F32) == code, tile, 0.0), axis=0, keepdims=True
    )


def announce_kernel(hessian, _, token):
    token[...] = jnp.zeros_like(token)


def start_kernel(_, send, b, mass, stiff, message, loc, b_panels, loc_panels, rim, stage):
    rows, peers = b.shape[1], message.shape[0]
    col_blocks, block_len = b_panels.shape[1], b_panels.shape[3]
    ky = masked_ky(stiff)
    sq = dot = None
    for e in range(3):
        v = b[e]
        image = inner_apply(v, mass[...], stiff[0], ky)
        loc[e] = image
        to_panels(b_panels, e, v)
        to_panels(loc_panels, e, image)
        sq = v * v if sq is None else sq + v * v
        dot = v * image if dot is None else dot + v * image
    write_rim(rim, b)
    ends = lax.axis_index("gx") == peers - 1
    kx = jnp.where(ends, 0.0, stiff[0, rows - 1 : rows, :])
    line = packed_line([total(sq), total(dot)])
    lanes, sub = iota((1, 128), 1), iota((8, 3 * block_len), 0)

    def one(d, carry):
        own_line = line
        for c in range(CAP):
            row, col = place_of(send, d * CAP + c, col_blocks)
            code = jnp.where(row == 0, col, jnp.where(row == rows - 1, col_blocks + col, 99))
            own_line = jnp.where(lanes == CODE_LANE + c, code.astype(F32), own_line)
            for e in range(3):
                span = slice(e * block_len, (e + 1) * block_len)
                stage[d, c : c + 1, span] = b_panels[e, col, pl.ds(row, 1), :]
                stage[d, CAP + c : CAP + c + 1, span] = loc_panels[e, col, pl.ds(row, 1), :]
        tail = jnp.concatenate([kx[:, 3 * block_len :], own_line, jnp.zeros_like(own_line)], axis=1)
        lower = jnp.where(sub == 2 * CAP, wide(kx[:, : 3 * block_len]), stage[d])
        lower = jnp.where(sub == 2 * CAP + 1, wide(tail), lower)
        message[d] = jnp.concatenate([rim[...], lower], axis=0).astype(BF16)
        return carry

    lax.fori_loop(0, peers, one, 0, unroll=16)


def contact_products(pairs, live_count, x8, y8, held):
    y8[...] = jnp.zeros_like(y8)
    groups, depth, width = held.shape
    slots = depth // width
    sub = iota((8, width), 0)
    zero = jnp.zeros((8, width), F32)
    for g in range(groups):
        ends, rows = [], []
        for k in range(slots):
            h = g * slots + k
            a, b = pairs[0, h], pairs[1, h]
            delta = jnp.where(h < live_count, x8[a] - x8[b], 0.0)
            coarse = rounded(delta)
            value = jnp.where(sub < 4, coarse, delta - coarse)
            rows.append(jnp.concatenate([value if j == k else zero for j in range(slots)], axis=1))
            ends.append((a, b))
        left = jnp.concatenate(rows, axis=0).astype(BF16)
        product = jnp.dot(left, held[g], preferred_element_type=F32)
        for k, (a, b) in enumerate(ends):
            y = product[8 * k : 8 * k + 8]
            y = y + pltpu.roll(y, 4, 0)
            y8[a] = y8[a] + y
            y8[b] = y8[b] - y


def wide(row):
    return jnp.broadcast_to(row, (8, row.shape[1]))


def contact_dot(x8, y8):
    value = x8[0] * y8[0]
    for p in range(1, x8.shape[0]):
        value = value + x8[p] * y8[p]
    return total(value[0:1])


def owner_kernel(
    pairs, live, got, hessian, message, held, own, known, x8, y8, z8, f8, tiles, corr, edges
):
    peers, _, _ = got.shape
    width = x8.shape[2]
    block_len = width // 3
    unpack_first(got, tiles, edges)

    def one(d, carry):
        energy, sums = carry
        before, after = around(d, peers)
        diff = tiles[d, 0:8, 0:width] - across(
            tiles[before, 0:8, 0:width], tiles[after, 0:8, 0:width]
        )
        fix = rim_coefs(edges, d) * diff
        corr[d] = fix
        body, line = tiles[d, 8:16, 0:width], tiles[d, 15:16, block_len : 2 * block_len]
        for c in range(CAP):
            p = d * CAP + c
            x8[p] = wide(body[c : c + 1])
            f8[p] = wide(body[CAP + c : CAP + c + 1] + chosen(pick(line, CODE_LANE + c), fix))
        return energy + fix * diff, sums + line

    zero = jnp.zeros((8, width), F32)
    energy, sums = lax.fori_loop(0, peers, one, (zero, jnp.zeros((1, block_len), F32)), unroll=16)
    known[...] = line_of(
        [pick_packed(sums, 0), pick_packed(sums, 1) + 0.5 * total(energy)], known.shape[1]
    )
    own[...] = corr[lax.axis_index("gx")]

    contact_products(pairs, live[0, live.shape[1] - 1], x8, y8, hessian)
    line = packed_line([contact_dot(x8, y8)])
    line = jnp.concatenate([line, jnp.zeros((1, width - block_len), F32)], axis=1)
    for p in range(x8.shape[0]):
        x8[p] = f8[p] + rounded(y8[p])
    contact_products(pairs, live[0, live.shape[1] - 1], x8, z8, hessian)
    sub = iota((8, width), 0)
    for d in range(peers):
        tile = jnp.where(sub == SUMS_TWO, wide(line), 0.0)
        kept = tiles[d, 8:16, 0:width]
        for c in range(CAP):
            tile = jnp.where(sub == c, y8[d * CAP + c], tile)
            tile = jnp.where(sub == CAP + c, z8[d * CAP + c], tile)
            kept = jnp.where(sub == CAP + c, x8[d * CAP + c], kept)
        message[d] = tile.astype(BF16)
        held[d] = kept


def middle_kernel(
    send, got2, own, known1, b, loc, mass, stiff, message, v1, v2, known, cb, cv1, panels, common, stage, back
):
    rows, peers = b.shape[1], message.shape[0]
    col_blocks, block_len = panels.shape[1], panels.shape[3]
    for d in range(peers):
        back[d] = got2[d].astype(F32)
    scatter_blocks(send, back, [cb, cv1])
    ky = masked_ky(stiff)
    rr0 = pick(known1[...], 0)
    alpha0 = rr0 / (pick(known1[...], 1) + pick_packed(line_sum(back, SUMS_TWO), 0))
    known[...] = line_of([rr0, alpha0], known.shape[1])
    sums = None
    for e in range(3):
        v1[e] = loc[e] + from_panels(cb, e)
        for side, row in enumerate((0, rows - 1)):
            v1[e, row : row + 1, :] = v1[e, row : row + 1, :] + rim_row(own[...], side, e)
        image = v1[e]
        inner = inner_apply(image, mass[...], stiff[0], ky)
        to_panels(panels, e, inner)
        second = inner + from_panels(cv1, e)
        v2[e] = second
        right = b[e]
        r1 = right - alpha0 * image
        w = image - alpha0 * second
        terms = [r1 * r1, r1 * w, r1 * image, right * w, right * image]
        sums = terms if sums is None else [s + t for s, t in zip(sums, terms)]
    write_rim(common.at[0], v1)
    write_rim(common.at[1], v2)
    line = packed_line([total(s) for s in sums])
    width = stage.shape[2]
    line = wide(jnp.concatenate([line, jnp.zeros((1, width - block_len), F32)], axis=1))
    sub = iota((8, width), 0)
    me = lax.axis_index("gx")

    def one(d, carry):
        for c in range(CAP):
            row, col = place_of(send, d * CAP + c, col_blocks)
            for e in range(3):
                stage[d, 4 + c : 5 + c, e * block_len : (e + 1) * block_len] = panels[
                    e, col, pl.ds(row, 1), :
                ]
        facing = jnp.where(d < me, common[1], pltpu.roll(common[1], 4, 0))
        lower = jnp.where(sub < 4, facing, jnp.where(sub == 7, line, stage[d]))
        message[d] = jnp.concatenate([common[0], lower], axis=0).astype(BF16)
        return carry

    lax.fori_loop(0, peers, one, 0, unroll=16)


def coefficients(known, sums, b_x, v1_x):
    rr0, alpha0 = pick(known, 0), pick(known, 1)
    rr1, r1w, r1v1, bw, bv1 = [pick_packed(sums, k) for k in range(5)]
    r1w = r1w - alpha0 * (b_x - alpha0 * v1_x)
    bw = bw - alpha0 * b_x
    beta0 = rr1 / rr0
    dad1 = r1w + beta0 * (r1v1 + bw) + beta0 * beta0 * bv1
    return (alpha0, beta0, rr1 / dad1), line_of([rr1, dad1], known.shape[1])


def advance(b, v1, v2, coefs):
    alpha0, beta0, alpha1 = coefs
    r1 = b - alpha0 * v1
    image = v1 - alpha0 * v2 + beta0 * v1
    return r1 + beta0 * b, image, r1 - alpha1 * image


def last_kernel(
    pairs, live, got1, got3, held, sent2, known, b, v1, v2, mass, stiff, hessian,
    message, part, d1_out, ad1_out, r2_out, ar2, known_out,
    x8, y8, tiles1, tiles3, corr, rim, edges,
):
    peers = got1.shape[0]
    width = x8.shape[2]
    rows = b.shape[1]
    unpack_first(got1, tiles1, edges)
    for d in range(peers):
        tiles3[d] = got3[d].astype(F32)

    def one(d, carry):
        before, after = around(d, peers)
        first = tiles3[d, 0:8, :]
        fix = rim_coefs(edges, d) * (first - across(tiles3[before, 0:8, :], tiles3[after, 0:8, :]))
        corr[d] = fix
        return (
            carry[0] + tiles1[d, 0:8, :] * fix,
            carry[1] + first * fix,
            carry[2] + tiles3[d, 15:16, 0:128],
        )

    zero = jnp.zeros((8, width), F32)
    b_x, v1_x, sums = lax.fori_loop(
        0, peers, one, (zero, zero, jnp.zeros((1, 128), F32)), unroll=4
    )
    coefs, known_line = coefficients(known[...], sums, total(b_x), total(v1_x))
    known_out[...] = known_line

    def two(d, carry):
        line = tiles1[d, 15:16, 128:256]
        fix, values = corr[d], tiles3[d, 8:16, :]
        kept, sent = held[d], sent2[d].astype(F32)
        for c in range(CAP):
            value = values[4 + c : 5 + c] + chosen(pick(line, CODE_LANE + c), fix)
            value = value + sent[CAP + c : CAP + c + 1]
            x8[d * CAP + c] = wide(
                advance(kept[c : c + 1], kept[CAP + c : CAP + c + 1], value, coefs)[2]
            )
        return carry

    lax.fori_loop(0, peers, two, 0, unroll=16)

    me = lax.axis_index("gx")
    before, after = around(me, peers)
    ky = masked_ky(stiff)
    mine = corr[me] * coefs[0]
    for e in range(3):
        d1, image, r2 = advance(b[e], v1[e], v2[e], coefs)
        part[e] = coefs[0] * b[e] + coefs[2] * d1
        d1_out[e] = d1
        ad1_out[e] = image
        r2_out[e] = r2
        for side, row in enumerate((0, rows - 1)):
            change = rim_row(mine, side, e)
            ad1_out[e, row : row + 1, :] = ad1_out[e, row : row + 1, :] - change
            r2_out[e, row : row + 1, :] = r2_out[e, row : row + 1, :] + coefs[2] * change
    write_rim(rim, r2_out)

    facing = jnp.where(
        iota((8, width), 0) < 4, tiles3[before, 8:16, :], pltpu.roll(tiles3[after, 8:16, :], 4, 0)
    )
    others = advance(
        across(tiles1[before, 0:8, :], tiles1[after, 0:8, :]),
        across(tiles3[before, 0:8, :], tiles3[after, 0:8, :]),
        facing + across(corr[before], corr[after]),
        coefs,
    )[2]
    fix = rim_coefs(edges, me) * (rim[...] - others)
    sums = None
    for e in range(3):
        r2 = r2_out[e]
        ar2[e] = inner_apply(r2, mass[...], stiff[0], ky)
        for side, row in enumerate((0, rows - 1)):
            ar2[e, row : row + 1, :] = ar2[e, row : row + 1, :] + rim_row(fix, side, e)
        terms = [r2 * r2, r2 * ar2[e], r2 * ad1_out[e]]
        sums = terms if sums is None else [s + t for s, t in zip(sums, terms)]
    sums = [total(value) for value in sums]

    contact_products(pairs, live[0, live.shape[1] - 1], x8, y8, hessian)
    line = packed_line([sums[0], sums[1] + contact_dot(x8, y8), sums[2]])
    line = jnp.concatenate([line, jnp.zeros((1, width - 128), F32)], axis=1)
    for d in range(peers):
        rows = [y8[d * CAP + c, 0:1, :] for c in range(CAP)]
        message[d] = jnp.concatenate([*rows, line], axis=0).astype(BF16)


def finish_kernel(
    send, got4, known, part, d1, ad1, r2, ar2, solution, residual, cr2, back, x, r3, sems
):
    for d in range(got4.shape[0]):
        back[d] = got4[d].astype(F32)
    sums = line_sum(back, SUMS_ONE)
    rr2, rar2, rad1 = [pick_packed(sums, k) for k in range(3)]
    beta1 = rr2 / pick(known[...], 0)
    alpha2 = rr2 / (rar2 + 2.0 * beta1 * rad1 + beta1 * beta1 * pick(known[...], 1))
    copies = []

    def send_out(source, target):
        copies.append(pltpu.make_async_copy(source, target, sems.at[len(copies)]))
        copies[-1].start()

    for e in range(3):
        x[e] = part[e] + alpha2 * (r2[e] + beta1 * d1[e])
        send_out(x.at[e], solution.at[e])
    scatter_blocks(send, back, [cr2])
    for e in range(3):
        r3[e] = r2[e] - alpha2 * (ar2[e] + from_panels(cr2, e) + beta1 * ad1[e])
        send_out(r3.at[e], residual.at[e])
    for copy in copies:
        copy.wait()


def call(kernel, spaces, outs, scratch=(), mebibytes=16, semaphores=0, name=None):
    kinds = {"s": pltpu.SMEM, "v": pltpu.VMEM, "a": pl.ANY}
    return pl.pallas_call(
        kernel,
        out_shape=tuple(jax.ShapeDtypeStruct(shape, kind) for shape, kind in outs),
        in_specs=[pl.BlockSpec(memory_space=kinds[k]) for k in spaces],
        out_specs=tuple(
            pl.BlockSpec(memory_space=pl.ANY if semaphores else pltpu.VMEM) for _ in outs
        ),
        scratch_shapes=[pltpu.VMEM(shape, F32) for shape in scratch]
        + [pltpu.SemaphoreType.DMA((semaphores,))] * bool(semaphores),
        compiler_params=pltpu.CompilerParams(vmem_limit_bytes=mebibytes * 2**20),
        name=name,
    )


def per_device(right_side, masses, stiffness, hessian, send_list, pair_refs, counts):
    _, row_count, col_count = right_side.shape
    width = hessian.shape[1]
    block_len = width // 3
    peers = lax.axis_size("gx")
    assert send_list.shape[1] == peers * CAP and col_count == 4 * block_len and block_len == 128
    field = (right_side.shape, F32)
    first, second = ((peers, 16, width), BF16), ((peers, 8, width), BF16)
    third, fourth = ((peers, 16, width), BF16), ((peers, 4, width), BF16)
    held_shape, edges = ((peers, 8, width), F32), (peers, 8, block_len)
    panels = (3, 4, row_count, block_len)
    tiles, wide_tiles, rims = (peers * CAP, 8, width), (peers, 16, width), (peers, 8, width)
    line = ((1, 128), F32)

    routes = jnp.concatenate([send_list, counts.reshape(1, 1)], axis=1)
    pair_refs = pair_refs.T
    slots = hessian.shape[0]
    grouped = 2 if slots % 2 == 0 else 1
    hessian = hessian.reshape(slots // grouped, grouped * width, width)

    def swap(message):
        return lax.all_to_all(message, "gx", split_axis=0, concat_axis=0, tiled=True)

    token = jnp.zeros(line[0], F32)
    for _ in range(2):
        (token,) = call(announce_kernel, "aa", [line], [], 51, name="announce")(hessian, token)
    sent1, loc = call(
        start_kernel,
        "asvvv",
        [first, field],
        [panels, panels, (8, width), rims],
        name="start",
    )(token, routes, right_side, masses, stiffness)
    got1 = swap(sent1)
    sent2, held, own, known1 = call(
        owner_kernel,
        "ssvv",
        [second, held_shape, ((8, width), F32), line],
        [tiles, tiles, tiles, tiles, wide_tiles, rims, edges],
        32,
        name="owner",
    )(pair_refs, routes, got1, hessian)
    got2 = swap(sent2)
    sent3, v1, v2, known = call(
        middle_kernel,
        "svvvvvvv",
        [third, field, field, line],
        [panels, panels, panels, (2, 8, width), rims, rims],
        name="middle",
    )(routes, got2, own, known1, right_side, loc, masses, stiffness)
    got3 = swap(sent3)
    sent4, part, d1, ad1, r2, ar2, known2 = call(
        last_kernel,
        "ssvvvvvvvvvvv",
        [fourth, field, field, field, field, field, line],
        [tiles, tiles, wide_tiles, wide_tiles, rims, (8, width), edges],
        32,
        name="last",
    )(
        pair_refs, routes, got1, got3, held, sent2, known, right_side, v1, v2, masses, stiffness,
        hessian,
    )
    got4 = swap(sent4)
    return call(finish_kernel, "svvvvvvv", [field, field], [panels, (peers, 4, width), field[0], field[0]], semaphores=6, name="finish")(
        routes, got4, known2, part, d1, ad1, r2, ar2
    )


def solution(mesh):
    placed = (
        P(None, ("groups", "gx"), None),
        P(("groups", "gx"), None),
        P(None, ("groups", "gx"), None),
        P(("groups", "gx"), None, None),
        P(("groups", "gx"), None),
        P(("groups", "gx"), None),
        P(("groups", "gx")),
    )
    return jax.shard_map(
        per_device,
        mesh=mesh,
        in_specs=placed,
        out_specs=(P(None, ("groups", "gx"), None), P(None, ("groups", "gx"), None)),
        check_vma=False,
    )
```

```python
import jax
import jax.numpy as jnp
from jax import lax
from jax.experimental import pallas as pl
from jax.experimental.pallas import tpu as pltpu
from jax.sharding import PartitionSpec as P

F32 = jnp.float32
BF16 = jnp.bfloat16
CAP = 3
SUMS_TWO, SUMS_ONE = 2 * CAP, CAP
CODE_LANE = 64


def iota(shape, dim):
    return lax.broadcasted_iota(jnp.int32, shape, dim)


def total(value):
    return jnp.sum(jnp.sum(value, axis=0, keepdims=True), axis=1, keepdims=True)


def line_of(scalars, width):
    lanes = iota((1, width), 1)
    line = jnp.zeros((1, width), F32)
    for k, value in enumerate(scalars):
        line = jnp.where(lanes == k, value, line)
    return line


def line_sum(message, row):
    peers = message.shape[0]
    parts = [message[d, row : row + 1, 0:128] for d in range(peers)]
    while len(parts) > 1:
        parts = [a + b for a, b in zip(parts[::2], parts[1::2])] + (
            parts[-1:] if len(parts) % 2 else []
        )
    return parts[0]


def pick(line, k):
    return line[:, k : k + 1]


def place_of(send, position, col_blocks):
    block = send[0, position]
    shift = col_blocks.bit_length() - 1
    return lax.shift_right_logical(block, jnp.int32(shift)), block & (col_blocks - 1)


def scatter_blocks(send, message, panels):
    peers = message.shape[0]
    _, col_blocks, _, block_len = panels[0].shape
    for field in panels:
        field[...] = jnp.zeros_like(field)

    def one(d, carry):
        for c in range(CAP):
            row, col = place_of(send, d * CAP + c, col_blocks)
            for f, field in enumerate(panels):
                for e in range(3):
                    field[e, col, pl.ds(row, 1), :] = message[
                        d, f * CAP + c : f * CAP + c + 1, e * block_len : (e + 1) * block_len
                    ]
        return carry

    lax.fori_loop(0, peers, one, 0, unroll=16)


def to_panels(panels, e, value):
    _, col_blocks, _, block_len = panels.shape
    for q in range(col_blocks):
        panels[e, q] = value[:, q * block_len : (q + 1) * block_len]


def from_panels(panels, e):
    return jnp.concatenate([panels[e, q] for q in range(panels.shape[1])], axis=1)


def put_line(message, row, line):
    for d in range(message.shape[0]):
        message[d, row : row + 1, :] = line


def inner_apply(v, mass, kx, ky):
    rows, cols = v.shape
    row_ids = iota((rows, cols), 0)
    flux_x = jnp.where(row_ids == rows - 1, 0.0, kx * (v - pltpu.roll(v, rows - 1, 0)))
    flux_y = ky * (v - pltpu.roll(v, cols - 1, 1))
    return mass * v + (flux_x - pltpu.roll(flux_x, 1, 0)) + (flux_y - pltpu.roll(flux_y, 1, 1))


def masked_ky(stiff):
    ky = stiff[1]
    return jnp.where(iota(ky.shape, 1) == ky.shape[1] - 1, 0.0, ky)


def rounded(value):
    return value.astype(BF16).astype(F32)


def packed_line(scalars):
    parts = []
    for value in scalars:
        high = rounded(value)
        middle = rounded(value - high)
        parts += [high, middle, value - high - middle]
    return line_of(parts, 128)


def pick_packed(line, k):
    return pick(line, 3 * k) + pick(line, 3 * k + 1) + pick(line, 3 * k + 2)


def thrice(tile):
    return jnp.concatenate([tile] * 3, axis=1)


def write_rim(target, field):
    rows, block_len = field.shape[1], 128
    col_blocks = field.shape[2] // block_len
    for side, row in enumerate((0, rows - 1)):
        for q in range(col_blocks):
            for e in range(3):
                line = side * col_blocks + q
                target[line : line + 1, e * block_len : (e + 1) * block_len] = field[
                    e, row : row + 1, q * block_len : (q + 1) * block_len
                ]


def rim_row(tile, side, e):
    block_len = tile.shape[1] // 3
    half = tile.shape[0] // 2
    return jnp.concatenate(
        [
            tile[side * half + q : side * half + q + 1, e * block_len : (e + 1) * block_len]
            for q in range(half)
        ],
        axis=1,
    )


def across(before, after):
    half = before.shape[0] // 2
    return pltpu.roll(jnp.where(iota(before.shape, 0) >= half, before, after), half, 0)


def around(d, peers):
    return jnp.maximum(d - 1, 0), jnp.minimum(d + 1, peers - 1)


def unpack_first(got, tiles, edges):
    sub = iota(edges.shape[1:], 0)
    for d in range(got.shape[0]):
        tile = got[d].astype(F32)
        tiles[d] = tile
        kx = jnp.where(sub % 4 == 3, wide(tile[15:16, 0:128]), 0.0)
        for q in range(3):
            kx = jnp.where(sub % 4 == q, wide(tile[14:15, q * 128 : (q + 1) * 128]), kx)
        edges[d] = kx


def rim_coefs(edges, d):
    before, _ = around(d, edges.shape[0])
    here, other = edges[d], edges[before]
    other = jnp.where(d > 0, other, 0.0)
    return thrice(jnp.where(iota(here.shape, 0) < 4, other, here))


def spread_sum(tile):
    for step in (4, 2, 1):
        tile = tile + pltpu.roll(tile, step, 0)
    return tile


def announce_kernel(hessian, _, token):
    token[...] = jnp.zeros_like(token)


def start_kernel(_, send, b, mass, stiff, message, loc, b_panels, loc_panels, rim, stage):
    rows, peers = b.shape[1], message.shape[0]
    col_blocks, block_len = b_panels.shape[1], b_panels.shape[3]
    ky = masked_ky(stiff)
    sq = dot = None
    for e in range(3):
        v = b[e]
        image = inner_apply(v, mass[...], stiff[0], ky)
        loc[e] = image
        to_panels(b_panels, e, v)
        to_panels(loc_panels, e, image)
        sq = v * v if sq is None else sq + v * v
        dot = v * image if dot is None else dot + v * image
    write_rim(rim, b)
    ends = lax.axis_index("gx") == peers - 1
    kx = jnp.where(ends, 0.0, stiff[0, rows - 1 : rows, :])
    line = packed_line([total(sq), total(dot)])
    lanes, sub = iota((1, 128), 1), iota((8, 3 * block_len), 0)

    def one(d, carry):
        own_line = line
        for c in range(CAP):
            row, col = place_of(send, d * CAP + c, col_blocks)
            code = jnp.where(row == 0, col, jnp.where(row == rows - 1, col_blocks + col, 99))
            own_line = jnp.where(lanes == CODE_LANE + c, code.astype(F32), own_line)
            for e in range(3):
                span = slice(e * block_len, (e + 1) * block_len)
                stage[d, c : c + 1, span] = b_panels[e, col, pl.ds(row, 1), :]
                stage[d, CAP + c : CAP + c + 1, span] = loc_panels[e, col, pl.ds(row, 1), :]
        tail = jnp.concatenate([kx[:, 3 * block_len :], own_line, jnp.zeros_like(own_line)], axis=1)
        lower = jnp.where(sub == 2 * CAP, wide(kx[:, : 3 * block_len]), stage[d])
        lower = jnp.where(sub == 2 * CAP + 1, wide(tail), lower)
        message[d] = jnp.concatenate([rim[...], lower], axis=0).astype(BF16)
        return carry

    lax.fori_loop(0, peers, one, 0, unroll=16)


def contact_products(pairs, live_count, x8, y8, held):
    y8[...] = jnp.zeros_like(y8)
    groups, depth, width = held.shape
    slots = depth // width
    sub = iota((8, width), 0)
    zero = jnp.zeros((8, width), F32)
    for g in range(groups):
        ends, rows = [], []
        for k in range(slots):
            h = g * slots + k
            a, b = pairs[0, h], pairs[1, h]
            delta = jnp.where(h < live_count, x8[a] - x8[b], 0.0)
            coarse = rounded(delta)
            value = jnp.where(sub < 4, coarse, delta - coarse)
            rows.append(jnp.concatenate([value if j == k else zero for j in range(slots)], axis=1))
            ends.append((a, b))
        left = jnp.concatenate(rows, axis=0).astype(BF16)
        product = jnp.dot(left, held[g], preferred_element_type=F32)
        for k, (a, b) in enumerate(ends):
            y = product[8 * k : 8 * k + 8]
            y = y + pltpu.roll(y, 4, 0)
            y8[a] = y8[a] + y
            y8[b] = y8[b] - y


def wide(row):
    return jnp.broadcast_to(row, (8, row.shape[1]))


def contact_dot(x8, y8):
    value = x8[0] * y8[0]
    for p in range(1, x8.shape[0]):
        value = value + x8[p] * y8[p]
    return total(value[0:1])


def owner_kernel(
    pairs, live, got, hessian, message, held, own, known, marks, exact, x8, y8, z8, f8, tiles, corr, edges
):
    peers, _, _ = got.shape
    width = x8.shape[2]
    block_len = width // 3
    unpack_first(got, tiles, edges)
    sub, sub_one = iota((8, width), 0), iota((8, block_len), 0).astype(F32)

    def one(d, carry):
        energy, sums = carry
        before, after = around(d, peers)
        diff = tiles[d, 0:8, 0:width] - across(
            tiles[before, 0:8, 0:width], tiles[after, 0:8, 0:width]
        )
        fix = rim_coefs(edges, d) * diff
        corr[d] = fix
        body, line = tiles[d, 8:16, 0:width], tiles[d, 15:16, block_len : 2 * block_len]
        for c in range(CAP):
            p = d * CAP + c
            x8[p] = wide(body[c : c + 1])
            mark = jnp.where(sub_one == pick(line, CODE_LANE + c), 1.0, 0.0)
            marks[p] = mark
            f8[p] = spread_sum(jnp.where(sub == CAP + c, body, 0.0) + thrice(mark) * fix)
        return energy + fix * diff, sums + line

    zero = jnp.zeros((8, width), F32)
    energy, sums = lax.fori_loop(0, peers, one, (zero, jnp.zeros((1, block_len), F32)), unroll=16)
    known[...] = line_of(
        [pick_packed(sums, 0), pick_packed(sums, 1) + 0.5 * total(energy)], known.shape[1]
    )
    own[...] = corr[lax.axis_index("gx")]

    contact_products(pairs, live[0, live.shape[1] - 1], x8, y8, hessian)
    line = packed_line([contact_dot(x8, y8)])
    line = jnp.concatenate([line, jnp.zeros((1, width - block_len), F32)], axis=1)
    for p in range(x8.shape[0]):
        x8[p] = f8[p] + rounded(y8[p])
    contact_products(pairs, live[0, live.shape[1] - 1], x8, z8, hessian)
    sub = iota((8, width), 0)
    for d in range(peers):
        tile = jnp.where(sub == SUMS_TWO, wide(line), 0.0)
        kept = tiles[d, 8:16, 0:width]
        for c in range(CAP):
            tile = jnp.where(sub == c, y8[d * CAP + c], tile)
            tile = jnp.where(sub == CAP + c, z8[d * CAP + c], tile)
            kept = jnp.where(sub == CAP + c, x8[d * CAP + c], kept)
        message[d] = tile.astype(BF16)
        exact[d] = tile
        held[d] = kept


def middle_kernel(
    send, got2, own, known1, b, loc, mass, stiff, message, v1, v2, known, cb, cv1, panels, common, stage, back
):
    rows, peers = b.shape[1], message.shape[0]
    col_blocks, block_len = panels.shape[1], panels.shape[3]
    for d in range(peers):
        back[d] = got2[d].astype(F32)
    scatter_blocks(send, back, [cb, cv1])
    ky = masked_ky(stiff)
    rr0 = pick(known1[...], 0)
    alpha0 = rr0 / (pick(known1[...], 1) + pick_packed(line_sum(back, SUMS_TWO), 0))
    known[...] = line_of([rr0, alpha0], known.shape[1])
    sums = None
    for e in range(3):
        v1[e] = loc[e] + from_panels(cb, e)
        for side, row in enumerate((0, rows - 1)):
            v1[e, row : row + 1, :] = v1[e, row : row + 1, :] + rim_row(own[...], side, e)
        image = v1[e]
        inner = inner_apply(image, mass[...], stiff[0], ky)
        to_panels(panels, e, inner)
        second = inner + from_panels(cv1, e)
        v2[e] = second
        right = b[e]
        r1 = right - alpha0 * image
        w = image - alpha0 * second
        terms = [r1 * r1, r1 * w, r1 * image, right * w, right * image]
        sums = terms if sums is None else [s + t for s, t in zip(sums, terms)]
    write_rim(common.at[0], v1)
    write_rim(common.at[1], v2)
    line = packed_line([total(s) for s in sums])
    width = stage.shape[2]
    line = wide(jnp.concatenate([line, jnp.zeros((1, width - block_len), F32)], axis=1))
    sub = iota((8, width), 0)
    me = lax.axis_index("gx")

    def one(d, carry):
        for c in range(CAP):
            row, col = place_of(send, d * CAP + c, col_blocks)
            for e in range(3):
                stage[d, 4 + c : 5 + c, e * block_len : (e + 1) * block_len] = panels[
                    e, col, pl.ds(row, 1), :
                ]
        facing = jnp.where(d < me, common[1], pltpu.roll(common[1], 4, 0))
        lower = jnp.where(sub < 4, facing, jnp.where(sub == 7, line, stage[d]))
        message[d] = jnp.concatenate([common[0], lower], axis=0).astype(BF16)
        return carry

    lax.fori_loop(0, peers, one, 0, unroll=16)


def coefficients(known, sums, b_x, v1_x):
    rr0, alpha0 = pick(known, 0), pick(known, 1)
    rr1, r1w, r1v1, bw, bv1 = [pick_packed(sums, k) for k in range(5)]
    r1w = r1w - alpha0 * (b_x - alpha0 * v1_x)
    bw = bw - alpha0 * b_x
    beta0 = rr1 / rr0
    dad1 = r1w + beta0 * (r1v1 + bw) + beta0 * beta0 * bv1
    return (alpha0, beta0, rr1 / dad1), line_of([rr1, dad1], known.shape[1])


def advance(b, v1, v2, coefs):
    alpha0, beta0, alpha1 = coefs
    r1 = b - alpha0 * v1
    image = v1 - alpha0 * v2 + beta0 * v1
    return r1 + beta0 * b, image, r1 - alpha1 * image


def last_kernel(
    pairs, live, got1, got3, held, marks, exact, sent2, known, b, v1, v2, mass, stiff, hessian,
    message, part, d1_out, ad1_out, r2_out, ar2, known_out,
    x8, y8, tiles1, tiles3, corr, rim, edges,
):
    peers = got1.shape[0]
    width = x8.shape[2]
    rows = b.shape[1]
    unpack_first(got1, tiles1, edges)
    for d in range(peers):
        tiles3[d] = got3[d].astype(F32)

    def one(d, carry):
        before, after = around(d, peers)
        first = tiles3[d, 0:8, :]
        fix = rim_coefs(edges, d) * (first - across(tiles3[before, 0:8, :], tiles3[after, 0:8, :]))
        corr[d] = fix
        return (
            carry[0] + tiles1[d, 0:8, :] * fix,
            carry[1] + first * fix,
            carry[2] + tiles3[d, 15:16, 0:128],
        )

    zero = jnp.zeros((8, width), F32)
    b_x, v1_x, sums = lax.fori_loop(
        0, peers, one, (zero, zero, jnp.zeros((1, 128), F32)), unroll=4
    )
    coefs, known_line = coefficients(known[...], sums, total(b_x), total(v1_x))
    known_out[...] = known_line

    sub = iota((8, width), 0)

    def two(d, carry):
        sent = sent2[d].astype(F32)
        second = pltpu.roll(tiles3[d, 8:16, :], 4, 0) + pltpu.roll(sent, 8 - CAP, 0)
        for c in range(CAP):
            p = d * CAP + c
            x8[p] = spread_sum(jnp.where(sub == c, second, 0.0) + thrice(marks[p]) * corr[d])
        return carry

    lax.fori_loop(0, peers, two, 0, unroll=16)
    contact_products(pairs, live[0, live.shape[1] - 1], x8, y8, hessian)

    me = lax.axis_index("gx")
    before, after = around(me, peers)
    ky = masked_ky(stiff)
    mine = corr[me] * coefs[0]
    for e in range(3):
        d1, image, r2 = advance(b[e], v1[e], v2[e], coefs)
        part[e] = coefs[0] * b[e] + coefs[2] * d1
        d1_out[e] = d1
        ad1_out[e] = image
        r2_out[e] = r2
        for side, row in enumerate((0, rows - 1)):
            change = rim_row(mine, side, e)
            ad1_out[e, row : row + 1, :] = ad1_out[e, row : row + 1, :] - change
            r2_out[e, row : row + 1, :] = r2_out[e, row : row + 1, :] + coefs[2] * change
    write_rim(rim, r2_out)

    facing = jnp.where(
        iota((8, width), 0) < 4, tiles3[before, 8:16, :], pltpu.roll(tiles3[after, 8:16, :], 4, 0)
    )
    others = advance(
        across(tiles1[before, 0:8, :], tiles1[after, 0:8, :]),
        across(tiles3[before, 0:8, :], tiles3[after, 0:8, :]),
        facing + across(corr[before], corr[after]),
        coefs,
    )[2]
    fix = rim_coefs(edges, me) * (rim[...] - others)
    sums = None
    for e in range(3):
        r2 = r2_out[e]
        ar2[e] = inner_apply(r2, mass[...], stiff[0], ky)
        for side, row in enumerate((0, rows - 1)):
            ar2[e, row : row + 1, :] = ar2[e, row : row + 1, :] + rim_row(fix, side, e)
        terms = [r2 * r2, r2 * ar2[e], r2 * ad1_out[e]]
        sums = terms if sums is None else [s + t for s, t in zip(sums, terms)]
    sums = [total(value) for value in sums]

    p_coef, q_coef = coefs[0] + coefs[2] * (1.0 + coefs[1]), coefs[0] * coefs[2]
    dot = jnp.zeros((8, width), F32)
    for d in range(peers):
        kept, known_c = held[d], exact[d]
        v2_o = jnp.zeros((8, width), F32)
        cv2_o = v2_o
        for c in range(CAP):
            v2_o = jnp.where(sub == c, x8[d * CAP + c], v2_o)
            cv2_o = jnp.where(sub == c, y8[d * CAP + c], cv2_o)
        r2_o = kept - p_coef * pltpu.roll(kept, 8 - CAP, 0) + q_coef * v2_o
        cr2_o = known_c - p_coef * pltpu.roll(known_c, 8 - CAP, 0) + q_coef * cv2_o
        dot = dot + jnp.where(sub < CAP, r2_o * cr2_o, 0.0)
        corr[d] = cr2_o
    line = packed_line([sums[0], sums[1] + total(dot), sums[2]])
    line = jnp.concatenate([line, jnp.zeros((1, width - 128), F32)], axis=1)
    for d in range(peers):
        message[d] = jnp.concatenate([corr[d, 0:CAP, :], line], axis=0).astype(BF16)


def finish_kernel(
    send, got4, known, part, d1, ad1, r2, ar2, solution, residual, cr2, back, x, r3, sems
):
    for d in range(got4.shape[0]):
        back[d] = got4[d].astype(F32)
    sums = line_sum(back, SUMS_ONE)
    rr2, rar2, rad1 = [pick_packed(sums, k) for k in range(3)]
    beta1 = rr2 / pick(known[...], 0)
    alpha2 = rr2 / (rar2 + 2.0 * beta1 * rad1 + beta1 * beta1 * pick(known[...], 1))
    copies = []

    def send_out(source, target):
        copies.append(pltpu.make_async_copy(source, target, sems.at[len(copies)]))
        copies[-1].start()

    for e in range(3):
        x[e] = part[e] + alpha2 * (r2[e] + beta1 * d1[e])
        send_out(x.at[e], solution.at[e])
    scatter_blocks(send, back, [cr2])
    for e in range(3):
        r3[e] = r2[e] - alpha2 * (ar2[e] + from_panels(cr2, e) + beta1 * ad1[e])
        send_out(r3.at[e], residual.at[e])
    for copy in copies:
        copy.wait()


def call(kernel, spaces, outs, scratch=(), mebibytes=16, semaphores=0, name=None):
    kinds = {"s": pltpu.SMEM, "v": pltpu.VMEM, "a": pl.ANY}
    return pl.pallas_call(
        kernel,
        out_shape=tuple(jax.ShapeDtypeStruct(shape, kind) for shape, kind in outs),
        in_specs=[pl.BlockSpec(memory_space=kinds[k]) for k in spaces],
        out_specs=tuple(
            pl.BlockSpec(memory_space=pl.ANY if semaphores else pltpu.VMEM) for _ in outs
        ),
        scratch_shapes=[pltpu.VMEM(shape, F32) for shape in scratch]
        + [pltpu.SemaphoreType.DMA((semaphores,))] * bool(semaphores),
        compiler_params=pltpu.CompilerParams(vmem_limit_bytes=mebibytes * 2**20),
        name=name,
    )


def per_device(right_side, masses, stiffness, hessian, send_list, pair_refs, counts):
    _, row_count, col_count = right_side.shape
    width = hessian.shape[1]
    block_len = width // 3
    peers = lax.axis_size("gx")
    assert send_list.shape[1] == peers * CAP and col_count == 4 * block_len and block_len == 128
    field = (right_side.shape, F32)
    first, second = ((peers, 16, width), BF16), ((peers, 8, width), BF16)
    third, fourth = ((peers, 16, width), BF16), ((peers, 4, width), BF16)
    held_shape, edges = ((peers, 8, width), F32), (peers, 8, block_len)
    panels = (3, 4, row_count, block_len)
    tiles, wide_tiles, rims = (peers * CAP, 8, width), (peers, 16, width), (peers, 8, width)
    line = ((1, 128), F32)

    routes = jnp.concatenate([send_list, counts.reshape(1, 1)], axis=1)
    pair_refs = pair_refs.T
    slots = hessian.shape[0]
    grouped = 2 if slots % 2 == 0 else 1
    hessian = hessian.reshape(slots // grouped, grouped * width, width)

    def swap(message):
        return lax.all_to_all(message, "gx", split_axis=0, concat_axis=0, tiled=True)

    token = jnp.zeros(line[0], F32)
    for _ in range(2):
        (token,) = call(announce_kernel, "aa", [line], [], 51, name="announce")(hessian, token)
    sent1, loc = call(
        start_kernel,
        "asvvv",
        [first, field],
        [panels, panels, (8, width), rims],
        name="start",
    )(token, routes, right_side, masses, stiffness)
    got1 = swap(sent1)
    sent2, held, own, known1, marks, exact = call(
        owner_kernel,
        "ssvv",
        [second, held_shape, ((8, width), F32), line, ((peers * CAP, 8, block_len), F32), held_shape],
        [tiles, tiles, tiles, tiles, wide_tiles, rims, edges],
        32,
        name="owner",
    )(pair_refs, routes, got1, hessian)
    got2 = swap(sent2)
    sent3, v1, v2, known = call(
        middle_kernel,
        "svvvvvvv",
        [third, field, field, line],
        [panels, panels, panels, (2, 8, width), rims, rims],
        name="middle",
    )(routes, got2, own, known1, right_side, loc, masses, stiffness)
    got3 = swap(sent3)
    sent4, part, d1, ad1, r2, ar2, known2 = call(
        last_kernel,
        "ssvvvvvvvvvvvvv",
        [fourth, field, field, field, field, field, line],
        [tiles, tiles, wide_tiles, wide_tiles, rims, (8, width), edges],
        32,
        name="last",
    )(
        pair_refs, routes, got1, got3, held, marks, exact, sent2, known, right_side, v1, v2, masses, stiffness,
        hessian,
    )
    got4 = swap(sent4)
    return call(finish_kernel, "svvvvvvv", [field, field], [panels, (peers, 4, width), field[0], field[0]], semaphores=6, name="finish")(
        routes, got4, known2, part, d1, ad1, r2, ar2
    )


def solution(mesh):
    placed = (
        P(None, ("groups", "gx"), None),
        P(("groups", "gx"), None),
        P(None, ("groups", "gx"), None),
        P(("groups", "gx"), None, None),
        P(("groups", "gx"), None),
        P(("groups", "gx"), None),
        P(("groups", "gx")),
    )
    return jax.shard_map(
        per_device,
        mesh=mesh,
        in_specs=placed,
        out_specs=(P(None, ("groups", "gx"), None), P(None, ("groups", "gx"), None)),
        check_vma=False,
    )
```
